32 devices in a mesh: lat: 8 (over z, x), lon: 4 (over y, core).
Axes of the slice: x: 2, y: 2, z: 4, core: 2. Of those that a mesh axis runs over, the one named last changes fastest.
Arguments:
- inputs: bfloat16 [16, 64, 360, 256], P(None, 'lat', 'lon'), may hold values from -6 to 6
- legendre_forward: bfloat16 [96, 96, 64], P('lat'), may hold values from -0.75 to 0.75
- legendre_inverse: bfloat16 [96, 64, 96], P('lat'), may hold values from -0.625 to 0.625
- spectral_weight: float32 [2, 96, 256], P(None, None, 'lon'), may hold values from -5 to 5
- skip_weight: bfloat16 [256, 256], replicated, may hold values from -0.375 to 0.375
- gain_first: float32 [256], replicated, may hold values from 0.5 to 1.5
- bias_first: float32 [256], replicated, may hold values from -2 to 2
- gain_second: float32 [256], replicated, may hold values from 0.5 to 1.5
- bias_second: float32 [256], replicated, may hold values from -2 to 2
- mlp_in: bfloat16 [256, 512], replicated, may hold values from -0.375 to 0.375
- mlp_in_bias: float32 [512], replicated, may hold values from -2 to 2
- mlp_out: bfloat16 [512, 256], replicated, may hold values from -0.25 to 0.25
- mlp_out_bias: float32 [256], replicated, may hold values from -2 to 2
- cotangent: bfloat16 [16, 64, 360, 256], P(None, 'lat', 'lon'), may hold values from -6 to 6
Outputs:
- output: bfloat16 [16, 64, 360, 256], P(None, 'lat', 'lon')
- grad_inputs: float32 [16, 64, 360, 256], P(None, 'lat', 'lon')
- grad_spectral: float32 [2, 96, 256], P(None, None, 'lon')
- grad_skip: float32 [256, 256], replicated
- grad_gain_first: float32 [256], replicated
- grad_bias_first: float32 [256], replicated
- grad_gain_second: float32 [256], replicated
- grad_bias_second: float32 [256], replicated
- grad_mlp_in: float32 [256, 512], replicated
- grad_mlp_in_bias: float32 [512], replicated
- grad_mlp_out: float32 [512, 256], replicated
- grad_mlp_out_bias: float32 [256], replicated
The draws below stay inside these ranges and needn't reach their ends.
All inputs are finite; a program needn't handle non-finite values.
Results may differ from the reference program's by a relative error of at most 0.012.
Values may be sent and summed in bfloat16 or wider, within the bound.
A program may use at most 256 MiB of HBM per device.

```python
import math
import jax
import jax.numpy as jnp
from jax import lax

C = 256
H = 512
NLON = 360
M = 96
L = 96
B = 16
NLAT = 64


def shard_levels(key, shape, shards, least, high):
    level = 1.0
    for position, parts in shards:
        steps = jax.random.uniform(jax.random.fold_in(jax.random.fold_in(key, 6), position), (parts,), jnp.float32, least / len(shards), high / len(shards))
        level = level * jnp.repeat(jnp.exp(steps), shape[position] // parts).reshape((-1,) + (1,) * (len(shape) - 1 - position))
    return level


def centred(own_key, extent, scale, reach, pieces=(), held_as=jnp.bfloat16):
    drawn = scale * jax.random.normal(own_key, extent, jnp.float32)
    if pieces:
        drawn = drawn * shard_levels(own_key, extent, pieces, -0.22, 0.18)
    return jnp.clip(drawn, -reach, reach).astype(held_as)


def setup_inputs(seed: int = 0) -> dict:
    splits = jax.random.split(jax.random.key(seed), 15)
    return {
        "inputs": centred(splits[0], (B, NLAT, NLON, C), 1.0, 6.0, ((1, 8), (2, 4))),
        "legendre_forward": centred(splits[1], (M, L, NLAT), NLAT ** -0.5, 0.75, ((0, 8),)),
        "legendre_inverse": centred(splits[2], (M, NLAT, L), L ** -0.5, 0.625, ((0, 8),)),
        "spectral_weight": centred(splits[3], (2, L, C), 1.0, 5.0, ((2, 4),), jnp.float32),
        "skip_weight": centred(splits[4], (C, C), C ** -0.5, 0.375),
        "gain_first": jnp.clip(1.0 + 0.1 * jax.random.normal(splits[5], (C,), jnp.float32), 0.5, 1.5),
        "bias_first": centred(splits[6], (C,), 0.3, 2.0, (), jnp.float32),
        "gain_second": jnp.clip(1.0 + 0.1 * jax.random.normal(splits[7], (C,), jnp.float32), 0.5, 1.5),
        "bias_second": centred(splits[8], (C,), 0.3, 2.0, (), jnp.float32),
        "mlp_in": centred(splits[9], (C, H), C ** -0.5, 0.375),
        "mlp_in_bias": centred(splits[10], (H,), 0.3, 2.0, (), jnp.float32),
        "mlp_out": centred(splits[11], (H, C), H ** -0.5, 0.25),
        "mlp_out_bias": centred(splits[12], (C,), 0.3, 2.0, (), jnp.float32),
        "cotangent": centred(splits[13], (B, NLAT, NLON, C), 1.0, 6.0, ((1, 8), (2, 4))),
    }


@jax.custom_vjp
def low(v):
    return lax.optimization_barrier(v.astype(jnp.bfloat16)).astype(jnp.float32)

@jax.custom_vjp
def low_back(v):
    return v

def low_keep(v):
    return (low(v), None)

def low_pass(kept, grad):
    return (grad,)

def back_keep(v):
    return (v, None)

def back_low(kept, grad):
    return (low(grad),)
low.defvjp(low_keep, low_pass)
low_back.defvjp(back_keep, back_low)
epsilon = 1e-05
highest = lax.Precision.HIGHEST

def fourier_tables(points, orders):
    longit = jnp.arange(points, dtype=jnp.int32)
    waves = jnp.arange(orders, dtype=jnp.int32)
    phase = (waves[:, None] * longit[None, :] % points).astype(jnp.float32) * (2.0 * math.pi / points)
    cosine = jnp.cos(phase)
    sine = jnp.sin(phase)
    factor = jnp.where(waves == 0, 1.0, 2.0).astype(jnp.float32)[:, None]
    forward = jnp.concatenate([cosine, -sine], axis=0).T
    inverse = jnp.stack([factor * cosine, -factor * sine], axis=0)
    return (forward.astype(jnp.bfloat16), inverse.astype(jnp.bfloat16))

def layer_norm(values, gain, bias):
    center = values - lax.optimization_barrier(jnp.mean(values, axis=-1, keepdims=True))
    spread = lax.optimization_barrier(jnp.mean(center * center, axis=-1, keepdims=True))
    return center * lax.rsqrt(spread + epsilon) * gain + bias

def reference(inputs, legendre_forward, legendre_inverse, spectral_weight, skip_weight, gain_first, bias_first, gain_second, bias_second, mlp_in, mlp_in_bias, mlp_out, mlp_out_bias, cotangent):
    fourier_forward, fourier_inverse = fourier_tables(NLON, M)
    fourier_forward = lax.optimization_barrier(fourier_forward).astype(jnp.float32)
    fourier_inverse = lax.optimization_barrier(fourier_inverse).astype(jnp.float32)
    degree = jnp.arange(L, dtype=jnp.int32)
    order = jnp.arange(M, dtype=jnp.int32)
    analysis = jnp.where(degree[None, :, None] >= order[:, None, None], legendre_forward.astype(jnp.float32), jnp.float32(0.0))
    synthesis = jnp.where(degree[None, None, :] >= order[:, None, None], legendre_inverse.astype(jnp.float32), jnp.float32(0.0))

    def layer_block(values, spectral, skip, gain_one, bias_one, gain_two, bias_two, weight_in, bias_in, weight_out, bias_out):
        normed = low(layer_norm(values, gain_one, bias_one))
        sent = low_back(normed)
        spectrum = jnp.einsum('bjnc,nk->bjck', sent, fourier_forward, precision=highest) / NLON
        spectrum = low_back(low(spectrum)).reshape(B, NLAT, C, 2, M)
        coeffs = low_back(jnp.einsum('bjcrm,mlj->bcrml', spectrum, analysis, precision=highest))
        weight_real = spectral[0].T[None, :, None, :]
        weight_imag = spectral[1].T[None, :, None, :]
        filt_real = weight_real * coeffs[:, :, 0] - weight_imag * coeffs[:, :, 1]
        filt_imag = weight_real * coeffs[:, :, 1] + weight_imag * coeffs[:, :, 0]
        filtered = low(jnp.stack([filt_real, filt_imag], axis=2))
        synth = low_back(low(jnp.einsum('bcrml,mjl->bjcrm', filtered, synthesis, precision=highest)))
        spatial = low(jnp.einsum('bjcrm,rmn->bjnc', synth, fourier_inverse, precision=highest))
        mixed = low_back(spatial + jnp.einsum('bjnc,cd->bjnd', normed, skip, precision=highest))
        resid = values + mixed
        second = low(layer_norm(resid, gain_two, bias_two))
        pre = low_back(jnp.einsum('bjnc,ch->bjnh', second, weight_in, precision=highest) + bias_in)
        act = low(jax.nn.gelu(pre))
        return resid + jnp.einsum('bjnh,hc->bjnc', act, weight_out, precision=highest) + bias_out
    primal = (inputs.astype(jnp.float32), spectral_weight, skip_weight.astype(jnp.float32), gain_first, bias_first, gain_second, bias_second, mlp_in.astype(jnp.float32), mlp_in_bias, mlp_out.astype(jnp.float32), mlp_out_bias)
    result, pullback = jax.vjp(layer_block, *primal)
    grads = pullback(cotangent.astype(jnp.float32))
    return (result.astype(jnp.bfloat16), grads[0], grads[1], grads[2], grads[3], grads[4], grads[5], grads[6], grads[7], grads[8], grads[9], grads[10])
```

```python
import functools
import math

import jax
import jax.numpy as jnp
import ml_dtypes
import numpy as np
from jax import lax
from jax.experimental import pallas as pl
from jax.experimental.pallas import tpu as pltpu
from jax.sharding import PartitionSpec as P

epsilon = 1e-05
LANES = 128
MESH = pl.DeviceIdType.MESH
root = math.sqrt(2.0 / math.pi)
cubic = 0.044715

OFFSET = {1: 0, 2: 1, 3: 2, 4: 3, 5: 4, 6: 4, 7: 5, 8: 6, 9: 6}
ORDER = (8, 5, 7, 1, 4, 2, 9, 6, 3)


def fourier_tables(points, lat):
    def build(orders):
        waves = np.arange(orders)
        phase = (waves[:, None] * np.arange(points)[None, :] % points).astype(np.float32)
        phase = phase * np.float32(2.0 * math.pi / points)
        cosine, sine = np.cos(phase), np.sin(phase)
        factor = np.where(waves == 0, 1.0, 2.0).astype(np.float32)[:, None]
        slab = orders // lat

        def arrange(parts):
            stacked = np.stack(parts).reshape(2, lat, slab, points).transpose(1, 0, 2, 3)
            return stacked.reshape(2 * orders, points).astype(ml_dtypes.bfloat16)

        forward = arrange([cosine, -sine])
        inverse = arrange([factor * cosine, -factor * sine])
        return forward, inverse

    return build


def row_tile(rows, most):
    fits = [t for t in range(16, most + 1, 16) if rows % t == 0]
    return fits[-1] if fits else rows


def norm_parts(values):
    center = values - jnp.mean(values, axis=-1, keepdims=True)
    spread = jnp.mean(center * center, axis=-1, keepdims=True)
    scaled = lax.rsqrt(spread + epsilon)
    return center * scaled, scaled


def norm_back(grad_out, normal, scaled, gain):
    grad_norm = grad_out * gain
    inner = jnp.mean(grad_norm, axis=-1, keepdims=True)
    cross = jnp.mean(grad_norm * normal, axis=-1, keepdims=True)
    return scaled * (grad_norm - inner - normal * cross)


def fold(values):
    rows, width = values.shape
    return jnp.sum(values.reshape(rows // 8, 8, width), axis=0)


def dot(a, b):
    return jnp.dot(a, b, preferred_element_type=jnp.float32)


def dot_t(a, b):
    return lax.dot_general(a, b, (((1,), (1,)), ((), ())), preferred_element_type=jnp.float32)


def t_dot(a, b):
    return lax.dot_general(a, b, (((0,), (0,)), ((), ())), preferred_element_type=jnp.float32)


def block_kernel(
    lat,
    lon,
    x_hbm,
    g_hbm,
    fwd_t,
    inv_t,
    inv,
    fwd,
    ana,
    ana_t,
    syn,
    syn_t,
    w_real,
    w_imag,
    skip,
    mlp_in,
    mlp_out,
    gain_one,
    bias_one,
    gain_two,
    bias_two,
    bias_in,
    bias_out,
    out_hbm,
    gin_hbm,
    grad_skip,
    grad_in,
    grad_out_t,
    sums_in,
    sums,
    grad_spec,
    x_all,
    normed,
    mixed,
    lon_a,
    lon_b,
    lat_a,
    lat_b,
    coeffs,
    send_2,
    send_3,
    send_4,
    send_6,
    send_7,
    send_8,
    wide,
    slim,
    g_buf,
    o_buf,
    i_buf,
    recv_sem,
    send_sem,
    x_sem,
    g_sem,
    o_sem,
    i_sem,
):
    batch, rows, width = x_hbm.shape
    halves = width // LANES
    group = lon // halves
    chunks = batch // group
    points = fwd_t.shape[1]
    slab, degrees, lats = ana.shape
    band = lats // lat
    block = 2 * slab * band
    waves = 2 * slab * lat
    my_lat, my_lon = lax.axis_index("lat"), lax.axis_index("lon")
    half_tile = row_tile(rows, 144)
    full_tile = row_tile(rows, 240)

    def lon_copy(stage, chunk, src, dst, peer):
        return pltpu.make_async_remote_copy(
            src_ref=src,
            dst_ref=dst,
            send_sem=send_sem.at[stage - 1],
            recv_sem=recv_sem.at[stage - 1, chunk],
            device_id={"lon": peer},
            device_id_type=MESH,
        )

    def lat_copy(stage, chunk, src, dst, peer):
        return pltpu.make_async_remote_copy(
            src_ref=src,
            dst_ref=dst,
            send_sem=send_sem.at[stage - 1],
            recv_sem=recv_sem.at[stage - 1, chunk],
            device_id={"lat": peer},
            device_id_type=MESH,
        )

    def own_copy(stage, chunk, src, dst):
        return pltpu.make_async_copy(src, dst, recv_sem.at[stage - 1, chunk])

    def landed(stage, chunk, whole):
        pltpu.make_async_copy(whole, whole, recv_sem.at[stage - 1, chunk]).wait()

    def sent(stage, part):
        lon_copy(stage, 0, part, part, my_lon).wait_send()

    def x_load(sample):
        return pltpu.make_async_copy(x_hbm.at[sample], x_all.at[sample], x_sem.at[sample])

    def g_load(sample, slot):
        return pltpu.make_async_copy(g_hbm.at[sample], g_buf.at[slot], g_sem.at[slot])

    def o_store(sample, slot):
        return pltpu.make_async_copy(o_buf.at[slot], out_hbm.at[sample], o_sem.at[slot])

    def i_store(sample, slot):
        return pltpu.make_async_copy(i_buf.at[slot], gin_hbm.at[sample], i_sem.at[slot])

    def spread_rows(stage, chunk, held):
        for step in range(1, lon):
            peer = lax.rem(my_lon + step, lon)
            src = held.at[chunk * group + peer // halves, lax.rem(peer, halves)]
            lon_copy(stage, chunk, src, lon_a.at[chunk, my_lon], peer).start()
        src = held.at[chunk * group + my_lon // halves, lax.rem(my_lon, halves)]
        own_copy(stage, chunk, src, lon_a.at[chunk, my_lon]).start()

    def spread_bands(stage, chunk, buffer, target):
        for step in range(1, lat):
            peer = lax.rem(my_lat + step, lat)
            lat_copy(stage, chunk, buffer.at[peer], target.at[chunk, my_lat], peer).start()

    def pair(values, factor):
        return jnp.concatenate([values(0), values(1)], axis=1).astype(jnp.bfloat16)

    def to_waves(stage, chunk, table, scale, buffer):
        landed(stage - 1, chunk, lon_a.at[chunk])
        for source in range(lon):
            wide[pl.ds(source * rows, rows), :] = lon_a[chunk, source, pl.ds(0, rows), :].astype(jnp.float32)
        for first in range(0, band, 2):
            rhs = jnp.concatenate(
                [wide[pl.ds(first + k, points, stride=band), :] for k in range(2)], axis=1
            ).astype(jnp.bfloat16)
            got = dot(table[...], rhs)
            if scale is not None:
                got = got * scale
            for k in range(2):
                slim[pl.ds(first + k, waves, stride=band), :] = got[:, k * LANES : (k + 1) * LANES]

        @pl.when(chunk > 0)
        def _():
            sent(stage, buffer.at[pl.ds(0, lat - 1)])

        for target in range(lat):
            buffer[target] = slim[pl.ds(target * block, block), :].astype(jnp.bfloat16)
        spread_bands(stage, chunk, buffer, lat_a)
        own = pl.ds(pl.multiple_of(my_lat * block, 8), block)
        lat_a[chunk, my_lat] = slim[own, :].astype(jnp.bfloat16)

    def to_points(stage, chunk, table, scale, buffer):
        landed(stage - 1, chunk, lat_b.at[chunk, pl.ds(0, lat - 1)])
        for source in range(lat):
            slim[pl.ds(source * block, block), :] = lat_b[chunk, source].astype(jnp.float32)
        for first in range(0, band, 2):
            rhs = jnp.concatenate(
                [slim[pl.ds(first + k, waves, stride=band), :] for k in range(2)], axis=1
            ).astype(jnp.bfloat16)
            got = dot(table[...], rhs)
            if scale is not None:
                got = got * scale
            for k in range(2):
                wide[pl.ds(first + k, points, stride=band), :] = got[:, k * LANES : (k + 1) * LANES]

        @pl.when(chunk > 0)
        def _():
            sent(stage, buffer.at[pl.ds(0, lon - 1)])

        for target in range(lon):
            buffer[target, pl.ds(0, rows), :] = wide[pl.ds(target * rows, rows), :].astype(jnp.bfloat16)
        sample, half = chunk * group + my_lon // halves, lax.rem(my_lon, halves)
        for step in range(1, lon):
            peer = lax.rem(my_lon + step, lon)
            lon_copy(stage, chunk, buffer.at[peer], lon_b.at[sample, half], peer).start()
        own = pl.ds(pl.multiple_of(my_lon * rows, 8), rows)
        lon_b[sample, half, pl.ds(0, rows), :] = wide[own, :].astype(jnp.bfloat16)

    def slab_step(stage, chunk, first_table, second_table, between, buffer):
        landed(stage - 1, chunk, lat_a.at[chunk, pl.ds(0, lat - 1)])
        for source in range(lat):
            slim[pl.ds(source * block, block), :] = lat_a[chunk, source].astype(jnp.float32)
        for m in range(slab):
            parts = []
            for r in range(2):
                at = (r * slab + m) * band
                parts.append(
                    jnp.concatenate([slim[pl.ds(s * block + at, band), :] for s in range(lat)], axis=0)
                )
            rhs = jnp.concatenate(parts, axis=1).astype(jnp.bfloat16)
            real, imag = between(m, dot(first_table[m], rhs))
            low = jnp.concatenate([real, imag], axis=1).astype(jnp.bfloat16)
            got = dot(second_table[m], low)
            for r in range(2):
                at = (r * slab + m) * band
                for t in range(lat):
                    wide[pl.ds(t * block + at, band), :] = got[
                        t * band : (t + 1) * band, r * LANES : (r + 1) * LANES
                    ]

        @pl.when(chunk > 0)
        def _():
            sent(stage, buffer.at[pl.ds(0, lat - 1)])

        for target in range(lat):
            buffer[target] = wide[pl.ds(target * block, block), :].astype(jnp.bfloat16)
        spread_bands(stage, chunk, buffer, lat_b)
        own = pl.ds(pl.multiple_of(my_lat * block, 8), block)
        lat_b[chunk, my_lat] = wide[own, :].astype(jnp.bfloat16)

    def both(held, sample, where):
        return jnp.concatenate([held[sample, h, where, :] for h in range(halves)], axis=1)

    def stage_1(chunk):
        @pl.when(chunk > 0)
        def _():
            sent(1, lon_a.at[chunk, pl.ds(0, lon - 1)])

        for k in range(group):
            sample = chunk * group + k
            x_load(sample).wait()

            @pl.loop(0, rows // half_tile)
            def _(i):
                where = pl.ds(pl.multiple_of(i * half_tile, 8), half_tile)
                normal, _ = norm_parts(x_all[sample, where, :].astype(jnp.float32))
                low = (normal * gain_one[...] + bias_one[...]).astype(jnp.bfloat16)
                for h in range(halves):
                    normed[sample, h, where, :] = low[:, h * LANES : (h + 1) * LANES]

        spread_rows(1, chunk, normed)

    def stage_2(chunk):
        to_waves(2, chunk, fwd_t, 1.0 / points, send_2)

    def stage_3(chunk):
        def between(m, got):
            coeffs[chunk, m] = got
            real, imag = got[:, :LANES], got[:, LANES:]
            return (
                w_real[...] * real - w_imag[...] * imag,
                w_real[...] * imag + w_imag[...] * real,
            )

        slab_step(3, chunk, ana, syn, between, send_3)

    def stage_4(chunk):
        to_points(4, chunk, inv, None, send_4)

    def stage_5(chunk):
        landed(4, chunk, lon_a.at[chunk, pl.ds(0, lon - 1)])

        @pl.when(chunk > 0)
        def _():
            sent(5, lon_a.at[chunk, pl.ds(0, lon - 1)])

        for k in range(group):
            sample = chunk * group + k
            g_load(sample, k).wait()

            @pl.when(chunk > 0)
            def _():
                o_store(sample, k).wait()

            @pl.loop(0, rows // full_tile)
            def _(i):
                where = pl.ds(pl.multiple_of(i * full_tile, 8), full_tile)
                low_one = both(normed, sample, where)
                spatial = both(lon_b, sample, where).astype(jnp.float32)
                resid = x_all[sample, where, :].astype(jnp.float32) + (spatial + dot(low_one, skip[...]))
                normal, scaled = norm_parts(resid)
                low_two = (normal * gain_two[...] + bias_two[...]).astype(jnp.bfloat16)
                pre = dot(low_two, mlp_in[...]) + bias_in[...]
                square = pre * pre
                curve = jnp.tanh(root * pre * (1.0 + cubic * square))
                lifted = 0.5 + 0.5 * curve
                act = (pre * lifted).astype(jnp.bfloat16)
                slope = lifted + (0.5 * root) * pre * (1.0 - curve * curve) * (1.0 + (3.0 * cubic) * square)
                o_buf[k, where, :] = (resid + dot(act, mlp_out[...]) + bias_out[...]).astype(jnp.bfloat16)
                g_low = g_buf[k, where, :]
                grad_out_t[...] += t_dot(g_low, act)
                grad_pre = (dot_t(g_low, mlp_out[...]) * slope).astype(jnp.bfloat16)
                grad_in[...] += t_dot(low_two, grad_pre)
                sums_in[...] += fold(grad_pre.astype(jnp.float32))
                grad_second = dot_t(grad_pre, mlp_in[...])
                g_full = g_low.astype(jnp.float32)
                sums[0] += fold(g_full)
                sums[3] += fold(grad_second * normal)
                sums[4] += fold(grad_second)
                grad_mixed = (g_full + norm_back(grad_second, normal, scaled, gain_two[...])).astype(jnp.bfloat16)
                grad_skip[...] += t_dot(low_one, grad_mixed)
                for h in range(halves):
                    mixed[sample, h, where, :] = grad_mixed[:, h * LANES : (h + 1) * LANES]

            o_store(sample, k).start()

            @pl.when(chunk < chunks - 1)
            def _():
                g_load(sample + group, k).start()

        spread_rows(5, chunk, mixed)

    def stage_6(chunk):
        to_waves(6, chunk, inv_t, None, send_6)

    def stage_7(chunk):
        def between(m, got):
            dr, di = got[:, :LANES], got[:, LANES:]
            held = coeffs[chunk, m]
            ar, ai = held[:, :LANES], held[:, LANES:]
            grad_spec[0] += dr * ar + di * ai
            grad_spec[1] += di * ar - dr * ai
            return (
                w_real[...] * dr + w_imag[...] * di,
                w_real[...] * di - w_imag[...] * dr,
            )

        slab_step(7, chunk, syn_t, ana_t, between, send_7)

    def stage_8(chunk):
        to_points(8, chunk, fwd, 1.0 / points, send_8)

    def stage_9(chunk):
        landed(8, chunk, lon_a.at[chunk, pl.ds(0, lon - 1)])
        for k in range(group):
            sample = chunk * group + k

            @pl.when(chunk > 0)
            def _():
                i_store(sample, k).wait()

            @pl.loop(0, rows // half_tile)
            def _(i):
                where = pl.ds(pl.multiple_of(i * half_tile, 8), half_tile)
                normal, scaled = norm_parts(x_all[sample, where, :].astype(jnp.float32))
                low = both(mixed, sample, where)
                grad_normed = dot_t(low, skip[...]) + both(lon_b, sample, where).astype(jnp.float32)
                sums[1] += fold(grad_normed * normal)
                sums[2] += fold(grad_normed)
                i_buf[k, where, :] = low.astype(jnp.float32) + norm_back(
                    grad_normed, normal, scaled, gain_one[...]
                )

            i_store(sample, k).start()

    stages = (stage_1, stage_2, stage_3, stage_4, stage_5, stage_6, stage_7, stage_8, stage_9)

    for sample in range(batch):
        x_load(sample).start()
    for k in range(group):
        g_load(k, k).start()

    barrier = pltpu.get_barrier_semaphore()
    for step in range(1, lon):
        pl.semaphore_signal(
            barrier, inc=1, device_id={"lon": lax.rem(my_lon + step, lon)}, device_id_type=MESH
        )
    for step in range(1, lat):
        pl.semaphore_signal(
            barrier, inc=1, device_id={"lat": lax.rem(my_lat + step, lat)}, device_id_type=MESH
        )
    pl.semaphore_wait(barrier, lon - 1 + lat - 1)

    grad_skip[...] = jnp.zeros_like(grad_skip)
    grad_in[...] = jnp.zeros_like(grad_in)
    grad_out_t[...] = jnp.zeros_like(grad_out_t)
    sums_in[...] = jnp.zeros_like(sums_in)
    sums[...] = jnp.zeros_like(sums)
    grad_spec[...] = jnp.zeros_like(grad_spec)
    padded = lon_a.shape[2]
    if padded > rows:
        for held in (normed, mixed):
            held[:, :, rows:, :] = jnp.zeros_like(held[:, :, rows:, :])
        for held in (send_4, send_8):
            held[:, rows:, :] = jnp.zeros_like(held[:, rows:, :])

    def tick(now, carry):
        for stage in ORDER:
            chunk = now - OFFSET[stage]

            @pl.when(jnp.logical_and(chunk >= 0, chunk < chunks))
            def _(stage=stage, chunk=chunk):
                stages[stage - 1](chunk)

        return carry

    lax.fori_loop(0, chunks + max(OFFSET.values()), tick, 0)

    last = chunks - 1
    for stage in (1, 5):
        sent(stage, lon_a.at[last, pl.ds(0, lon - 1)])
    for stage, buffer, count in (
        (2, send_2, lat - 1),
        (3, send_3, lat - 1),
        (4, send_4, lon - 1),
        (6, send_6, lat - 1),
        (7, send_7, lat - 1),
        (8, send_8, lon - 1),
    ):
        sent(stage, buffer.at[pl.ds(0, count)])
    for k in range(group):
        o_store(last * group + k, k).wait()
        i_store(last * group + k, k).wait()


def per_device(
    tables,
    lat,
    lon,
    inputs,
    legendre_forward,
    legendre_inverse,
    spectral_weight,
    skip_weight,
    gain_first,
    bias_first,
    gain_second,
    bias_second,
    mlp_in,
    mlp_in_bias,
    mlp_out,
    mlp_out_bias,
    cotangent,
):
    batch, band, columns, width = inputs.shape
    points = columns * lon
    slab, degrees, lats = legendre_forward.shape
    orders = slab * lat
    hidden = mlp_in.shape[1]
    rows = columns * band
    padded = -(-rows // 16) * 16
    halves = width // LANES
    group = lon // halves
    chunks = batch // group
    block = 2 * slab * band
    waves = 2 * orders

    forward, inverse = tables(points, lat)(orders)
    order_index = lax.axis_index("lat") * slab + jnp.arange(slab, dtype=jnp.int32)
    degree_index = jnp.arange(degrees, dtype=jnp.int32)
    zero_low = jnp.zeros((), jnp.bfloat16)
    analysis = jnp.where(
        degree_index[None, :, None] >= order_index[:, None, None], legendre_forward, zero_low
    )
    synthesis = jnp.where(
        degree_index[None, None, :] >= order_index[:, None, None], legendre_inverse, zero_low
    )
    my_lon = lax.axis_index("lon")
    my_half = lax.rem(my_lon, halves)
    weight = lax.all_gather(spectral_weight, "lon", axis=2, tiled=True)
    weight = lax.dynamic_slice_in_dim(weight, my_half * LANES, LANES, axis=2)

    def flat(values):
        return values.transpose(0, 2, 1, 3).reshape(batch, rows, width)

    def row(values):
        return values.reshape(1, -1)

    vmem = pl.BlockSpec(memory_space=pltpu.VMEM)
    hbm = pl.BlockSpec(memory_space=pl.ANY)
    low, full = jnp.bfloat16, jnp.float32
    results = pl.pallas_call(
        functools.partial(block_kernel, lat, lon),
        out_shape=(
            jax.ShapeDtypeStruct((batch, rows, width), low),
            jax.ShapeDtypeStruct((batch, rows, width), full),
            jax.ShapeDtypeStruct((width, width), full),
            jax.ShapeDtypeStruct((width, hidden), full),
            jax.ShapeDtypeStruct((width, hidden), full),
            jax.ShapeDtypeStruct((8, hidden), full),
            jax.ShapeDtypeStruct((5, 8, width), full),
            jax.ShapeDtypeStruct((2, degrees, LANES), full),
        ),
        in_specs=[hbm, hbm] + [vmem] * 19,
        out_specs=(hbm, hbm) + (vmem,) * 6,
        scratch_shapes=[
            pltpu.VMEM((batch, rows, width), low),
            pltpu.VMEM((batch, halves, padded, LANES), low),
            pltpu.VMEM((batch, halves, padded, LANES), low),
            pltpu.VMEM((chunks, lon, padded, LANES), low),
            pltpu.VMEM((batch, halves, padded, LANES), low),
            pltpu.VMEM((chunks, lat, block, LANES), low),
            pltpu.VMEM((chunks, lat, block, LANES), low),
            pltpu.VMEM((chunks, slab, degrees, 2 * LANES), full),
            pltpu.VMEM((lat, block, LANES), low),
            pltpu.VMEM((lat, block, LANES), low),
            pltpu.VMEM((lon, padded, LANES), low),
            pltpu.VMEM((lat, block, LANES), low),
            pltpu.VMEM((lat, block, LANES), low),
            pltpu.VMEM((lon, padded, LANES), low),
            pltpu.VMEM((max(points, waves) * band, LANES), full),
            pltpu.VMEM((waves * band, LANES), full),
            pltpu.VMEM((group, rows, width), low),
            pltpu.VMEM((group, rows, width), low),
            pltpu.VMEM((group, rows, width), full),
            pltpu.SemaphoreType.DMA((8, chunks)),
            pltpu.SemaphoreType.DMA((8,)),
            pltpu.SemaphoreType.DMA((batch,)),
            pltpu.SemaphoreType.DMA((group,)),
            pltpu.SemaphoreType.DMA((group,)),
            pltpu.SemaphoreType.DMA((group,)),
        ],
        compiler_params=pltpu.CompilerParams(
            collective_id=0, has_side_effects=True, vmem_limit_bytes=63 * 2**20
        ),
    )(
        flat(inputs),
        flat(cotangent),
        jnp.asarray(forward),
        jnp.asarray(inverse),
        jnp.asarray(inverse.T),
        jnp.asarray(forward.T),
        analysis,
        analysis.transpose(0, 2, 1),
        synthesis,
        synthesis.transpose(0, 2, 1),
        weight[0],
        weight[1],
        skip_weight,
        mlp_in,
        mlp_out,
        row(gain_first),
        row(bias_first),
        row(gain_second),
        row(bias_second),
        row(mlp_in_bias),
        row(mlp_out_bias),
    )
    output, grad_inputs, grad_skip, grad_in, grad_out_t, sums_in, sums, grad_spec = results

    def unflat(values):
        return values.reshape(batch, columns, band, width).transpose(0, 2, 1, 3)

    spread = jnp.zeros((2, degrees, width), full)
    spread = lax.dynamic_update_slice_in_dim(spread, grad_spec, my_half * LANES, axis=2)
    sums = jnp.sum(sums, axis=1)
    grad_skip, grad_in, grad_out, in_bias, sums, spread = lax.psum(
        (grad_skip, grad_in, grad_out_t.T, jnp.sum(sums_in, axis=0), sums, spread), ("lat", "lon")
    )
    narrow = width // lon
    grad_spec = lax.dynamic_slice_in_dim(spread, my_lon * narrow, narrow, axis=2)
    return (
        unflat(output),
        unflat(grad_inputs),
        grad_spec,
        grad_skip,
        sums[1],
        sums[2],
        sums[3],
        sums[4],
        grad_in,
        in_bias,
        grad_out,
        sums[0],
    )


def solution(mesh):
    lat, lon = mesh.shape["lat"], mesh.shape["lon"]
    grid = P(None, "lat", "lon", None)
    table = P("lat", None, None)
    channel = P(None, None, "lon")
    return jax.shard_map(
        functools.partial(per_device, fourier_tables, lat, lon),
        mesh=mesh,
        in_specs=(grid, table, table, channel) + (P(),) * 9 + (grid,),
        out_specs=(grid, grid, channel) + (P(),) * 9,
        check_vma=False,
    )
```

```python
import functools
import math

import jax
import jax.numpy as jnp
import ml_dtypes
import numpy as np
from jax import lax
from jax.experimental import pallas as pl
from jax.experimental.pallas import tpu as pltpu
from jax.sharding import PartitionSpec as P

epsilon = 1e-05
LANES = 128
MESH = pl.DeviceIdType.MESH
root = math.sqrt(2.0 / math.pi)
cubic = 0.044715

OFFSET = {1: 0, 2: 1, 3: 2, 4: 3, 5: 4, 6: 4, 7: 5, 8: 6, 9: 6}
ORDER = (8, 5, 7, 1, 4, 2, 9, 6, 3)


def fourier_tables(points, lat):
    def build(orders):
        waves = np.arange(orders)
        phase = (waves[:, None] * np.arange(points)[None, :] % points).astype(np.float32)
        phase = phase * np.float32(2.0 * math.pi / points)
        cosine, sine = np.cos(phase), np.sin(phase)
        factor = np.where(waves == 0, 1.0, 2.0).astype(np.float32)[:, None]
        slab = orders // lat

        def arrange(parts):
            stacked = np.stack(parts).reshape(2, lat, slab, points).transpose(1, 0, 2, 3)
            return stacked.reshape(2 * orders, points).astype(ml_dtypes.bfloat16)

        forward = arrange([cosine, -sine])
        inverse = arrange([factor * cosine, -factor * sine])
        return forward, inverse

    return build


def row_tile(rows, most):
    fits = [t for t in range(16, most + 1, 16) if rows % t == 0]
    return fits[-1] if fits else rows


def norm_parts(values):
    center = values - jnp.mean(values, axis=-1, keepdims=True)
    spread = jnp.mean(center * center, axis=-1, keepdims=True)
    scaled = lax.rsqrt(spread + epsilon)
    return center * scaled, scaled


def norm_back(grad_out, normal, scaled, gain):
    grad_norm = grad_out * gain
    inner = jnp.mean(grad_norm, axis=-1, keepdims=True)
    cross = jnp.mean(grad_norm * normal, axis=-1, keepdims=True)
    return scaled * (grad_norm - inner - normal * cross)


def fold(values):
    rows, width = values.shape
    return jnp.sum(values.reshape(rows // 8, 8, width), axis=0)


def dot(a, b):
    return jnp.dot(a, b, preferred_element_type=jnp.float32)


def dot_t(a, b):
    return lax.dot_general(a, b, (((1,), (1,)), ((), ())), preferred_element_type=jnp.float32)


def t_dot(a, b):
    return lax.dot_general(a, b, (((0,), (0,)), ((), ())), preferred_element_type=jnp.float32)


def block_kernel(
    lat,
    lon,
    x_hbm,
    g_hbm,
    fwd_t,
    inv_t,
    inv,
    fwd,
    raw_ana,
    raw_syn,
    weight,
    skip,
    mlp_in,
    mlp_out,
    gain_one,
    bias_one,
    gain_two,
    bias_two,
    bias_in,
    bias_out,
    out_hbm,
    gin_hbm,
    total_hbm,
    total_spec,
    total_norm,
    x_all,
    normed,
    mixed,
    lon_a,
    lon_b,
    lat_a,
    lat_b,
    coeffs,
    send_2,
    send_3,
    send_4,
    send_6,
    send_7,
    send_8,
    wide,
    slim,
    g_buf,
    o_buf,
    i_buf,
    recv_sem,
    send_sem,
    x_sem,
    g_sem,
    o_sem,
    i_sem,
    ana,
    ana_t,
    syn,
    syn_t,
    w_parts,
    w_real,
    w_imag,
    acc,
    part_core,
    part_chip,
    part_lat,
    spec,
    spec_lat,
    spec_lon,
    spec_sum,
    norm_sums,
    norm_own,
    norm_lon,
    norm_lat,
    w_sem,
    fold_recv,
    fold_send,
    spec_recv,
    spec_send,
    spec_pair,
    norm_recv,
    norm_send,
    own_sem,
):
    batch, rows, width = x_hbm.shape
    halves = width // LANES
    group = lon // halves
    chunks = batch // group
    points = fwd_t.shape[1]
    slab, lats, degrees = raw_ana.shape
    narrow = width // lon
    hidden = mlp_in.shape[1]
    band = lats // lat
    block = 2 * slab * band
    waves = 2 * slab * lat
    my_lat, my_lon = lax.axis_index("lat"), lax.axis_index("lon")
    half_tile = row_tile(rows, 144)
    full_tile = row_tile(rows, 240)

    def lon_copy(stage, chunk, src, dst, peer):
        return pltpu.make_async_remote_copy(
            src_ref=src,
            dst_ref=dst,
            send_sem=send_sem.at[stage - 1],
            recv_sem=recv_sem.at[stage - 1, chunk],
            device_id={"lon": peer},
            device_id_type=MESH,
        )

    def lat_copy(stage, chunk, src, dst, peer):
        return pltpu.make_async_remote_copy(
            src_ref=src,
            dst_ref=dst,
            send_sem=send_sem.at[stage - 1],
            recv_sem=recv_sem.at[stage - 1, chunk],
            device_id={"lat": peer},
            device_id_type=MESH,
        )

    def own_copy(stage, chunk, src, dst):
        return pltpu.make_async_copy(src, dst, recv_sem.at[stage - 1, chunk])

    def landed(stage, chunk, whole):
        pltpu.make_async_copy(whole, whole, recv_sem.at[stage - 1, chunk]).wait()

    def sent(stage, part):
        lon_copy(stage, 0, part, part, my_lon).wait_send()

    def x_load(sample):
        return pltpu.make_async_copy(x_hbm.at[sample], x_all.at[sample], x_sem.at[sample])

    def g_load(sample, slot):
        return pltpu.make_async_copy(g_hbm.at[sample], g_buf.at[slot], g_sem.at[slot])

    def o_store(sample, slot):
        return pltpu.make_async_copy(o_buf.at[slot], out_hbm.at[sample], o_sem.at[slot])

    def i_store(sample, slot):
        return pltpu.make_async_copy(i_buf.at[slot], gin_hbm.at[sample], i_sem.at[slot])

    def spread_rows(stage, chunk, held):
        for step in range(1, lon):
            peer = lax.rem(my_lon + step, lon)
            src = held.at[chunk * group + peer // halves, lax.rem(peer, halves)]
            lon_copy(stage, chunk, src, lon_a.at[chunk, my_lon], peer).start()
        src = held.at[chunk * group + my_lon // halves, lax.rem(my_lon, halves)]
        own_copy(stage, chunk, src, lon_a.at[chunk, my_lon]).start()

    def spread_bands(stage, chunk, buffer, target):
        for step in range(1, lat):
            peer = lax.rem(my_lat + step, lat)
            lat_copy(stage, chunk, buffer.at[peer], target.at[chunk, my_lat], peer).start()

    def pair(values, factor):
        return jnp.concatenate([values(0), values(1)], axis=1).astype(jnp.bfloat16)

    def to_waves(stage, chunk, table, scale, buffer):
        landed(stage - 1, chunk, lon_a.at[chunk])
        for source in range(lon):
            wide[pl.ds(source * rows, rows), :] = lon_a[chunk, source, pl.ds(0, rows), :].astype(jnp.float32)
        for first in range(0, band, 2):
            rhs = jnp.concatenate(
                [wide[pl.ds(first + k, points, stride=band), :] for k in range(2)], axis=1
            ).astype(jnp.bfloat16)
            got = dot(table[...], rhs)
            if scale is not None:
                got = got * scale
            for k in range(2):
                slim[pl.ds(first + k, waves, stride=band), :] = got[:, k * LANES : (k + 1) * LANES]

        @pl.when(chunk > 0)
        def _():
            sent(stage, buffer.at[pl.ds(0, lat - 1)])

        for target in range(lat):
            buffer[target] = slim[pl.ds(target * block, block), :].astype(jnp.bfloat16)
        spread_bands(stage, chunk, buffer, lat_a)
        own = pl.ds(pl.multiple_of(my_lat * block, 8), block)
        lat_a[chunk, my_lat] = slim[own, :].astype(jnp.bfloat16)

    def to_points(stage, chunk, table, scale, buffer):
        landed(stage - 1, chunk, lat_b.at[chunk, pl.ds(0, lat - 1)])
        for source in range(lat):
            slim[pl.ds(source * block, block), :] = lat_b[chunk, source].astype(jnp.float32)
        for first in range(0, band, 2):
            rhs = jnp.concatenate(
                [slim[pl.ds(first + k, waves, stride=band), :] for k in range(2)], axis=1
            ).astype(jnp.bfloat16)
            got = dot(table[...], rhs)
            if scale is not None:
                got = got * scale
            for k in range(2):
                wide[pl.ds(first + k, points, stride=band), :] = got[:, k * LANES : (k + 1) * LANES]

        @pl.when(chunk > 0)
        def _():
            sent(stage, buffer.at[pl.ds(0, lon - 1)])

        for target in range(lon):
            buffer[target, pl.ds(0, rows), :] = wide[pl.ds(target * rows, rows), :].astype(jnp.bfloat16)
        sample, half = chunk * group + my_lon // halves, lax.rem(my_lon, halves)
        for step in range(1, lon):
            peer = lax.rem(my_lon + step, lon)
            lon_copy(stage, chunk, buffer.at[peer], lon_b.at[sample, half], peer).start()
        own = pl.ds(pl.multiple_of(my_lon * rows, 8), rows)
        lon_b[sample, half, pl.ds(0, rows), :] = wide[own, :].astype(jnp.bfloat16)

    def slab_step(stage, chunk, first_table, second_table, between, buffer):
        landed(stage - 1, chunk, lat_a.at[chunk, pl.ds(0, lat - 1)])
        for source in range(lat):
            slim[pl.ds(source * block, block), :] = lat_a[chunk, source].astype(jnp.float32)
        for m in range(slab):
            parts = []
            for r in range(2):
                at = (r * slab + m) * band
                parts.append(
                    jnp.concatenate([slim[pl.ds(s * block + at, band), :] for s in range(lat)], axis=0)
                )
            rhs = jnp.concatenate(parts, axis=1).astype(jnp.bfloat16)
            real, imag = between(m, dot(first_table[m], rhs))
            low = jnp.concatenate([real, imag], axis=1).astype(jnp.bfloat16)
            got = dot(second_table[m], low)
            for r in range(2):
                at = (r * slab + m) * band
                for t in range(lat):
                    wide[pl.ds(t * block + at, band), :] = got[
                        t * band : (t + 1) * band, r * LANES : (r + 1) * LANES
                    ]

        @pl.when(chunk > 0)
        def _():
            sent(stage, buffer.at[pl.ds(0, lat - 1)])

        for target in range(lat):
            buffer[target] = wide[pl.ds(target * block, block), :].astype(jnp.bfloat16)
        spread_bands(stage, chunk, buffer, lat_b)
        own = pl.ds(pl.multiple_of(my_lat * block, 8), block)
        lat_b[chunk, my_lat] = wide[own, :].astype(jnp.bfloat16)

    hidden_rows = width * hidden // LANES
    vector_rows = 2 * hidden_rows + width * width // LANES

    def gather_rows(base, values):
        count = values.shape[0]
        for q in range(values.shape[1] // LANES):
            acc[pl.ds(base + q * count, count), :] += values[:, q * LANES : (q + 1) * LANES]

    def both(held, sample, where):
        return jnp.concatenate([held[sample, h, where, :] for h in range(halves)], axis=1)

    def stage_1(chunk):
        @pl.when(chunk > 0)
        def _():
            sent(1, lon_a.at[chunk, pl.ds(0, lon - 1)])

        for k in range(group):
            sample = chunk * group + k
            x_load(sample).wait()

            @pl.loop(0, rows // half_tile)
            def _(i):
                where = pl.ds(pl.multiple_of(i * half_tile, 8), half_tile)
                normal, _ = norm_parts(x_all[sample, where, :].astype(jnp.float32))
                low = (normal * gain_one[...] + bias_one[...]).astype(jnp.bfloat16)
                for h in range(halves):
                    normed[sample, h, where, :] = low[:, h * LANES : (h + 1) * LANES]

        spread_rows(1, chunk, normed)

    def stage_2(chunk):
        to_waves(2, chunk, fwd_t, 1.0 / points, send_2)

    def stage_3(chunk):
        def between(m, got):
            coeffs[chunk, m] = got.astype(jnp.bfloat16)
            real, imag = got[:, :LANES], got[:, LANES:]
            return (
                w_real[...] * real - w_imag[...] * imag,
                w_real[...] * imag + w_imag[...] * real,
            )

        slab_step(3, chunk, ana, syn, between, send_3)

    def stage_4(chunk):
        to_points(4, chunk, inv, None, send_4)

    def stage_5(chunk):
        landed(4, chunk, lon_a.at[chunk, pl.ds(0, lon - 1)])

        @pl.when(chunk > 0)
        def _():
            sent(5, lon_a.at[chunk, pl.ds(0, lon - 1)])

        for k in range(group):
            sample = chunk * group + k
            g_load(sample, k).wait()

            @pl.when(chunk > 0)
            def _():
                o_store(sample, k).wait()

            @pl.loop(0, rows // full_tile)
            def _(i):
                where = pl.ds(pl.multiple_of(i * full_tile, 8), full_tile)
                low_one = both(normed, sample, where)
                spatial = both(lon_b, sample, where).astype(jnp.float32)
                resid = x_all[sample, where, :].astype(jnp.float32) + (spatial + dot(low_one, skip[...]))
                normal, scaled = norm_parts(resid)
                low_two = (normal * gain_two[...] + bias_two[...]).astype(jnp.bfloat16)
                pre = dot(low_two, mlp_in[...]) + bias_in[...]
                square = pre * pre
                curve = jnp.tanh(root * pre * (1.0 + cubic * square))
                lifted = 0.5 + 0.5 * curve
                act = (pre * lifted).astype(jnp.bfloat16)
                slope = lifted + (0.5 * root) * pre * (1.0 - curve * curve) * (1.0 + (3.0 * cubic) * square)
                o_buf[k, where, :] = (resid + dot(act, mlp_out[...]) + bias_out[...]).astype(jnp.bfloat16)
                g_low = g_buf[k, where, :]
                gather_rows(hidden_rows, t_dot(g_low, act))
                grad_pre = (dot_t(g_low, mlp_out[...]) * slope).astype(jnp.bfloat16)
                gather_rows(0, t_dot(low_two, grad_pre))
                gather_rows(vector_rows, fold(grad_pre.astype(jnp.float32)))
                grad_second = dot_t(grad_pre, mlp_in[...])
                g_full = g_low.astype(jnp.float32)
                for at, values in enumerate((g_full, grad_second * normal, grad_second)):
                    gather_rows(vector_rows + 8 * (hidden + at * width) // LANES, fold(values))
                grad_mixed = (g_full + norm_back(grad_second, normal, scaled, gain_two[...])).astype(jnp.bfloat16)
                gather_rows(2 * hidden_rows, t_dot(low_one, grad_mixed))
                for h in range(halves):
                    mixed[sample, h, where, :] = grad_mixed[:, h * LANES : (h + 1) * LANES]

            o_store(sample, k).start()

            @pl.when(chunk < chunks - 1)
            def _():
                g_load(sample + group, k).start()

        spread_rows(5, chunk, mixed)

    def stage_6(chunk):
        to_waves(6, chunk, inv_t, None, send_6)

    def stage_7(chunk):
        def between(m, got):
            dr, di = got[:, :LANES], got[:, LANES:]
            held = coeffs[chunk, m].astype(jnp.float32)
            ar, ai = held[:, :LANES], held[:, LANES:]
            spec[pl.ds(0, degrees), :] += dr * ar + di * ai
            spec[pl.ds(degrees, degrees), :] += di * ar - dr * ai
            return (
                w_real[...] * dr + w_imag[...] * di,
                w_real[...] * di - w_imag[...] * dr,
            )

        slab_step(7, chunk, syn_t, ana_t, between, send_7)

    def stage_8(chunk):
        to_points(8, chunk, fwd, 1.0 / points, send_8)

    def stage_9(chunk):
        landed(8, chunk, lon_a.at[chunk, pl.ds(0, lon - 1)])
        for k in range(group):
            sample = chunk * group + k

            @pl.when(chunk > 0)
            def _():
                i_store(sample, k).wait()

            @pl.loop(0, rows // half_tile)
            def _(i):
                where = pl.ds(pl.multiple_of(i * half_tile, 8), half_tile)
                normal, scaled = norm_parts(x_all[sample, where, :].astype(jnp.float32))
                low = both(mixed, sample, where)
                grad_normed = dot_t(low, skip[...]) + both(lon_b, sample, where).astype(jnp.float32)
                norm_sums[0] += fold(grad_normed * normal)
                norm_sums[1] += fold(grad_normed)
                i_buf[k, where, :] = low.astype(jnp.float32) + norm_back(
                    grad_normed, normal, scaled, gain_one[...]
                )

            i_store(sample, k).start()

    def weight_copies(start):
        place = lax.rem(my_lon, group)
        held = w_parts.at[:, pl.ds(pl.multiple_of(place * narrow, 8), narrow), :]
        for q in range(group):
            peer = my_lon // group + halves * q

            @pl.when(peer != my_lon)
            def _(peer=peer, q=q):
                copy = pltpu.make_async_remote_copy(
                    src_ref=weight,
                    dst_ref=held,
                    send_sem=w_sem.at[1, q],
                    recv_sem=w_sem.at[0, place],
                    device_id={"lon": peer},
                    device_id_type=MESH,
                )
                if start:
                    copy.start()
                else:
                    copy.wait_send()

            if start:

                @pl.when(peer == my_lon)
                def _():
                    pltpu.make_async_copy(weight, held, w_sem.at[0, place]).start()

    def build():
        acc[...] = jnp.zeros_like(acc)
        spec[...] = jnp.zeros_like(spec)
        norm_sums[...] = jnp.zeros_like(norm_sums)
        norm_own[...] = jnp.zeros_like(norm_own)
        degree = lax.broadcasted_iota(jnp.int32, (lats, degrees), 1)

        @pl.loop(0, slab)
        def _(m):
            kept = degree >= my_lat * slab + m
            for raw, plain, turned in ((raw_ana, ana_t, ana), (raw_syn, syn, syn_t)):
                values = jnp.where(kept, raw[m].astype(jnp.float32), 0.0)
                plain[m] = values.astype(jnp.bfloat16)
                turned[m] = values.T.astype(jnp.bfloat16)

        for q in range(group):
            part = w_parts.at[:, pl.ds(q * narrow, narrow), :]
            pltpu.make_async_copy(part, part, w_sem.at[0, q]).wait()
        w_real[...] = w_parts[0].T
        w_imag[...] = w_parts[1].T

    total_rows = acc.shape[0]
    place_core, place_chip = lax.rem(my_lon, 2), my_lon // 2
    levels = (
        (2, place_core, part_core, lambda p: {"lon": 2 * place_chip + p}),
        (lon // 2, place_chip, part_chip, lambda p: {"lon": 2 * p + place_core}),
        (lat, my_lat, part_lat, lambda p: {"lat": p}),
    )
    bases, sizes = [0], [total_rows]
    for count, place, _, _ in levels:
        sizes.append(sizes[-1] // count)
        bases.append(bases[-1] + place * sizes[-1])

    def row_part(at, count):
        return pl.ds(pl.multiple_of(at, 8), count)

    def fold_start(k):
        count, place, parts, device = levels[k]
        for step in range(1, count):
            peer = lax.rem(place + step, count)
            pltpu.make_async_remote_copy(
                src_ref=acc.at[row_part(bases[k] + peer * sizes[k + 1], sizes[k + 1]), :],
                dst_ref=parts.at[step - 1],
                send_sem=fold_send.at[0, k],
                recv_sem=fold_recv.at[0, k],
                device_id=device(peer),
                device_id_type=MESH,
            ).start()

    def fold_end(k):
        count, _, parts, _ = levels[k]
        pltpu.make_async_copy(parts, parts, fold_recv.at[0, k]).wait()
        got = parts[0]
        for step in range(2, count):
            got = got + parts[step - 1]
        acc[row_part(bases[k + 1], sizes[k + 1]), :] += got

    def spread_start(k):
        count, place, _, device = levels[k]
        own = row_part(bases[k + 1], sizes[k + 1])
        src = acc if k == len(levels) - 1 else total_hbm
        for step in range(1, count):
            pltpu.make_async_remote_copy(
                src_ref=src.at[own, :],
                dst_ref=total_hbm.at[own, :],
                send_sem=fold_send.at[1, k],
                recv_sem=fold_recv.at[1, k],
                device_id=device(lax.rem(place + step, count)),
                device_id_type=MESH,
            ).start()
        if src is acc:
            pltpu.make_async_copy(acc.at[own, :], total_hbm.at[own, :], own_sem).start()

    def spread_end(k):
        count = levels[k][0]
        all_parts = total_hbm.at[pl.ds(0, (count - 1) * sizes[k + 1]), :]
        pltpu.make_async_copy(all_parts, all_parts, fold_recv.at[1, k]).wait()
        if k == len(levels) - 1:
            own = row_part(bases[k + 1], sizes[k + 1])
            pltpu.make_async_copy(acc.at[own, :], total_hbm.at[own, :], own_sem).wait()

    def fold_sent():
        for k, (count, _, _, _) in enumerate(levels):
            for way in range(2):
                part = total_hbm if way and k < len(levels) - 1 else acc
                part = part.at[pl.ds(0, (count - 1) * sizes[k + 1]), :]
                pltpu.make_async_remote_copy(
                    src_ref=part,
                    dst_ref=part,
                    send_sem=fold_send.at[way, k],
                    recv_sem=fold_recv.at[way, k],
                    device_id={"lon": my_lon},
                    device_id_type=MESH,
                ).wait_send()

    spec_rows = spec_sum.shape[0]

    def spec_lat_copies(way, src, dst):
        for step in range(1, lat):
            peer = lax.rem(my_lat + step, lat)
            pltpu.make_async_remote_copy(
                src_ref=src(peer),
                dst_ref=dst(step),
                send_sem=spec_send.at[way],
                recv_sem=spec_recv.at[way],
                device_id={"lat": peer},
                device_id_type=MESH,
            ).start()

    def spec_start():
        spec_lat_copies(
            0, lambda p: spec.at[row_part(p * spec_rows, spec_rows), :], lambda s: spec_lat.at[s - 1]
        )

    def spec_pairs(action):
        half = lax.rem(my_lon, halves)
        for q in range(group):
            target = half * group + q

            @pl.when(target != my_lon)
            def _(target=target, q=q):
                copy = pltpu.make_async_remote_copy(
                    src_ref=spec_sum,
                    dst_ref=spec_lon.at[my_lon // halves],
                    send_sem=spec_pair.at[1, q],
                    recv_sem=spec_pair.at[0, my_lon // halves],
                    device_id={"lon": target},
                    device_id_type=MESH,
                )
                if action == "start":
                    copy.start()
                else:
                    copy.wait_send()

            if action == "start":

                @pl.when(target == my_lon)
                def _():
                    pltpu.make_async_copy(
                        spec_sum, spec_lon.at[my_lon // halves], spec_pair.at[0, my_lon // halves]
                    ).start()

    def spec_middle():
        pltpu.make_async_copy(spec_lat, spec_lat, spec_recv.at[0]).wait()
        got = spec[row_part(my_lat * spec_rows, spec_rows), :]
        for step in range(1, lat):
            got = got + spec_lat[step - 1]
        spec_sum[...] = got
        spec_pairs("start")

    def spec_back():
        for q in range(group):
            pltpu.make_async_copy(spec_lon.at[q], spec_lon.at[q], spec_pair.at[0, q]).wait()
        got = spec_lon[0]
        for q in range(1, group):
            got = got + spec_lon[q]
        own = row_part(my_lat * spec_rows, spec_rows)
        total_spec[own, :] = got
        spec_lat_copies(1, lambda p: total_spec.at[own, :], lambda s: total_spec.at[own, :])

    def spec_end():
        part = total_spec.at[pl.ds(0, (lat - 1) * spec_rows), :]
        pltpu.make_async_copy(part, part, spec_recv.at[1]).wait()
        for way in range(2):
            pltpu.make_async_remote_copy(
                src_ref=part,
                dst_ref=part,
                send_sem=spec_send.at[way],
                recv_sem=spec_recv.at[way],
                device_id={"lat": my_lat},
                device_id_type=MESH,
            ).wait_send()
        spec_pairs("end")

    def norm_copies(way, axis, count, place, src, parts, action):
        for step in range(1, count):
            copy = pltpu.make_async_remote_copy(
                src_ref=src,
                dst_ref=parts.at[step - 1],
                send_sem=norm_send.at[way, step - 1],
                recv_sem=norm_recv.at[way],
                device_id={axis: lax.rem(place + step, count)},
                device_id_type=MESH,
            )
            if action == "start":
                copy.start()
            else:
                copy.wait_send()

    def norm_fold(way, axis, count, place, src, parts, out):
        norm_copies(way, axis, count, place, src, parts, "start")
        pltpu.make_async_copy(parts, parts, norm_recv.at[way]).wait()
        got = src[...]
        for step in range(1, count):
            got = got + parts[step - 1]
        out[...] = got

    def norm_all():
        for which in range(2):
            line = jnp.sum(norm_sums[which], axis=0, keepdims=True)
            for h in range(halves):
                norm_own[0, pl.ds(which * halves + h, 1), :] = line[:, h * LANES : (h + 1) * LANES]
        norm_fold(0, "lon", lon, my_lon, norm_own.at[0], norm_lon, norm_own.at[1])
        norm_fold(1, "lat", lat, my_lat, norm_own.at[1], norm_lat, total_norm)
        norm_copies(0, "lon", lon, my_lon, norm_own.at[0], norm_lon, "end")
        norm_copies(1, "lat", lat, my_lat, norm_own.at[1], norm_lat, "end")

    def run(*steps):
        def go():
            for step, k in steps:
                step() if k is None else step(k)

        return go

    aside = {
        (0, 1): build,
        (chunks + 3, 5): run((fold_start, 0)),
        (chunks + 3, 7): run((fold_end, 0), (fold_start, 1)),
        (chunks + 3, 6): run((fold_end, 1), (fold_start, 2)),
        (chunks + 4, 8): run((fold_end, 2), (spread_start, 2)),
        (chunks + 4, 7): run((spec_start, None)),
        (chunks + 4, 9): run((spread_end, 2), (spread_start, 1)),
        (chunks + 5, 8): run((spread_end, 1), (spread_start, 0), (spec_middle, None)),
        (chunks + 5, 7): run((spec_back, None)),
    }

    stages = (stage_1, stage_2, stage_3, stage_4, stage_5, stage_6, stage_7, stage_8, stage_9)

    for sample in range(batch):
        x_load(sample).start()
    for k in range(group):
        g_load(k, k).start()

    barrier = pltpu.get_barrier_semaphore()
    for step in range(1, lon):
        pl.semaphore_signal(
            barrier, inc=1, device_id={"lon": lax.rem(my_lon + step, lon)}, device_id_type=MESH
        )
    for step in range(1, lat):
        pl.semaphore_signal(
            barrier, inc=1, device_id={"lat": lax.rem(my_lat + step, lat)}, device_id_type=MESH
        )
    pl.semaphore_wait(barrier, lon - 1 + lat - 1)

    weight_copies(True)
    padded = lon_a.shape[2]
    if padded > rows:
        for held in (normed, mixed):
            held[:, :, rows:, :] = jnp.zeros_like(held[:, :, rows:, :])
        for held in (send_4, send_8):
            held[:, rows:, :] = jnp.zeros_like(held[:, rows:, :])

    def tick(now, carry):
        for stage in ORDER:
            chunk = now - OFFSET[stage]

            @pl.when(jnp.logical_and(chunk >= 0, chunk < chunks))
            def _(stage=stage, chunk=chunk):
                stages[stage - 1](chunk)

            for (when, after), action in aside.items():
                if after == stage:
                    pl.when(now == when)(action)

        return carry

    lax.fori_loop(0, chunks + max(OFFSET.values()), tick, 0)

    norm_all()
    spread_end(0)
    spec_end()
    fold_sent()
    weight_copies(False)
    last = chunks - 1
    for stage in (1, 5):
        sent(stage, lon_a.at[last, pl.ds(0, lon - 1)])
    for stage, buffer, count in (
        (2, send_2, lat - 1),
        (3, send_3, lat - 1),
        (4, send_4, lon - 1),
        (6, send_6, lat - 1),
        (7, send_7, lat - 1),
        (8, send_8, lon - 1),
    ):
        sent(stage, buffer.at[pl.ds(0, count)])
    for k in range(group):
        o_store(last * group + k, k).wait()
        i_store(last * group + k, k).wait()


def per_device(
    tables,
    lat,
    lon,
    inputs,
    legendre_forward,
    legendre_inverse,
    spectral_weight,
    skip_weight,
    gain_first,
    bias_first,
    gain_second,
    bias_second,
    mlp_in,
    mlp_in_bias,
    mlp_out,
    mlp_out_bias,
    cotangent,
):
    batch, band, columns, width = inputs.shape
    points = columns * lon
    slab, degrees, lats = legendre_forward.shape
    orders = slab * lat
    hidden = mlp_in.shape[1]
    rows = columns * band
    padded = -(-rows // 16) * 16
    halves = width // LANES
    group = lon // halves
    chunks = batch // group
    block = 2 * slab * band
    waves = 2 * orders

    forward, inverse = tables(points, lat)(orders)
    my_lon = lax.axis_index("lon")
    hidden = mlp_in.shape[1]
    flat_rows = (2 * hidden + width) * width // LANES + 8 * (hidden + 3 * width) // LANES
    share = -(-flat_rows // (8 * lat * lon)) * 8
    total_rows = share * lat * lon
    spec_rows = -(-2 * degrees // (8 * lat)) * 8

    def flat(values):
        return values.transpose(0, 2, 1, 3).reshape(batch, rows, width)

    def row(values):
        return values.reshape(1, -1)

    vmem = pl.BlockSpec(memory_space=pltpu.VMEM)
    hbm = pl.BlockSpec(memory_space=pl.ANY)
    low, full = jnp.bfloat16, jnp.float32
    results = pl.pallas_call(
        functools.partial(block_kernel, lat, lon),
        out_shape=(
            jax.ShapeDtypeStruct((batch, rows, width), low),
            jax.ShapeDtypeStruct((batch, rows, width), full),
            jax.ShapeDtypeStruct((total_rows, LANES), full),
            jax.ShapeDtypeStruct((lat * spec_rows, LANES), full),
            jax.ShapeDtypeStruct((8, LANES), full),
        ),
        in_specs=[hbm, hbm] + [vmem] * 16,
        out_specs=(hbm, hbm, hbm, vmem, vmem),
        scratch_shapes=[
            pltpu.VMEM((batch, rows, width), low),
            pltpu.VMEM((batch, halves, padded, LANES), low),
            pltpu.VMEM((batch, halves, padded, LANES), low),
            pltpu.VMEM((chunks, lon, padded, LANES), low),
            pltpu.VMEM((batch, halves, padded, LANES), low),
            pltpu.VMEM((chunks, lat, block, LANES), low),
            pltpu.VMEM((chunks, lat, block, LANES), low),
            pltpu.VMEM((chunks, slab, degrees, 2 * LANES), low),
            pltpu.VMEM((lat, block, LANES), low),
            pltpu.VMEM((lat, block, LANES), low),
            pltpu.VMEM((lon, padded, LANES), low),
            pltpu.VMEM((lat, block, LANES), low),
            pltpu.VMEM((lat, block, LANES), low),
            pltpu.VMEM((lon, padded, LANES), low),
            pltpu.VMEM((max(points, waves) * band, LANES), full),
            pltpu.VMEM((waves * band, LANES), full),
            pltpu.VMEM((group, rows, width), low),
            pltpu.VMEM((group, rows, width), low),
            pltpu.VMEM((group, rows, width), full),
            pltpu.SemaphoreType.DMA((8, chunks)),
            pltpu.SemaphoreType.DMA((8,)),
            pltpu.SemaphoreType.DMA((batch,)),
            pltpu.SemaphoreType.DMA((group,)),
            pltpu.SemaphoreType.DMA((group,)),
            pltpu.SemaphoreType.DMA((group,)),
            pltpu.VMEM((slab, degrees, lats), low),
            pltpu.VMEM((slab, lats, degrees), low),
            pltpu.VMEM((slab, lats, degrees), low),
            pltpu.VMEM((slab, degrees, lats), low),
            pltpu.VMEM((2, LANES, degrees), full),
            pltpu.VMEM((degrees, LANES), full),
            pltpu.VMEM((degrees, LANES), full),
            pltpu.VMEM((total_rows, LANES), full),
            pltpu.VMEM((1, total_rows // 2, LANES), full),
            pltpu.VMEM((lon // 2 - 1, total_rows // lon, LANES), full),
            pltpu.VMEM((lat - 1, share, LANES), full),
            pltpu.VMEM((lat * spec_rows, LANES), full),
            pltpu.VMEM((lat - 1, spec_rows, LANES), full),
            pltpu.VMEM((group, spec_rows, LANES), full),
            pltpu.VMEM((spec_rows, LANES), full),
            pltpu.VMEM((2, 8, width), full),
            pltpu.VMEM((2, 8, LANES), full),
            pltpu.VMEM((lon - 1, 8, LANES), full),
            pltpu.VMEM((lat - 1, 8, LANES), full),
            pltpu.SemaphoreType.DMA((2, group)),
            pltpu.SemaphoreType.DMA((2, 3)),
            pltpu.SemaphoreType.DMA((2, 3)),
            pltpu.SemaphoreType.DMA((2,)),
            pltpu.SemaphoreType.DMA((2,)),
            pltpu.SemaphoreType.DMA((2, group)),
            pltpu.SemaphoreType.DMA((2,)),
            pltpu.SemaphoreType.DMA((2, max(lat, lon) - 1)),
            pltpu.SemaphoreType.DMA,
        ],
        compiler_params=pltpu.CompilerParams(
            collective_id=0, has_side_effects=True, vmem_limit_bytes=63 * 2**20
        ),
    )(
        flat(inputs),
        flat(cotangent),
        jnp.asarray(forward),
        jnp.asarray(inverse),
        jnp.asarray(inverse.T),
        jnp.asarray(forward.T),
        legendre_forward.transpose(0, 2, 1),
        legendre_inverse,
        spectral_weight.transpose(0, 2, 1),
        skip_weight,
        mlp_in,
        mlp_out,
        row(gain_first),
        row(bias_first),
        row(gain_second),
        row(bias_second),
        row(mlp_in_bias),
        row(mlp_out_bias),
    )
    output, grad_inputs, total, spec, norm = results

    def unflat(values):
        return values.reshape(batch, columns, band, width).transpose(0, 2, 1, 3)

    def wide_part(base, height, across):
        part = total[base : base + height * across // LANES]
        return part.reshape(across // LANES, height, LANES).transpose(1, 0, 2).reshape(height, across)

    hidden_rows = width * hidden // LANES
    vector_rows = 2 * hidden_rows + width * width // LANES
    vectors = total[vector_rows:flat_rows].reshape(-1, 8, LANES).sum(axis=1).reshape(-1)
    spec = spec[: 2 * degrees].reshape(2, degrees, LANES)
    narrow = width // lon
    grad_spec = lax.dynamic_slice_in_dim(spec, lax.rem(my_lon, group) * narrow, narrow, axis=2)
    norm = norm[: 2 * halves].reshape(2, width)
    return (
        unflat(output),
        unflat(grad_inputs),
        grad_spec,
        wide_part(2 * hidden_rows, width, width),
        norm[0],
        norm[1],
        vectors[hidden + width : hidden + 2 * width],
        vectors[hidden + 2 * width :],
        wide_part(0, width, hidden),
        vectors[:hidden],
        wide_part(hidden_rows, width, hidden).T,
        vectors[hidden : hidden + width],
    )


def solution(mesh):
    lat, lon = mesh.shape["lat"], mesh.shape["lon"]
    grid = P(None, "lat", "lon", None)
    table = P("lat", None, None)
    channel = P(None, None, "lon")
    return jax.shard_map(
        functools.partial(per_device, fourier_tables, lat, lon),
        mesh=mesh,
        in_specs=(grid, table, table, channel) + (P(),) * 9 + (grid,),
        out_specs=(grid, grid, channel) + (P(),) * 9,
        check_vma=False,
    )
```

```python
import functools
import math

import jax
import jax.numpy as jnp
import ml_dtypes
import numpy as np
from jax import lax
from jax.experimental import pallas as pl
from jax.experimental.pallas import tpu as pltpu
from jax.sharding import PartitionSpec as P

epsilon = 1e-05
LANES = 128
MESH = pl.DeviceIdType.MESH
root = math.sqrt(2.0 / math.pi)
cubic = 0.044715

OFFSET = {"1": 0, "2": 1, "3": 2, "4": 3, "5a": 4, "5b": 5, "6": 6, "7": 7, "8": 8, "9": 9}
ORDER = ("6", "5b", "1", "2", "7", "3", "8", "9", "5a", "4")


def fourier_tables(points, lat):
    def build(orders):
        waves = np.arange(orders)
        phase = (waves[:, None] * np.arange(points)[None, :] % points).astype(np.float32)
        phase = phase * np.float32(2.0 * math.pi / points)
        cosine, sine = np.cos(phase), np.sin(phase)
        factor = np.where(waves == 0, 1.0, 2.0).astype(np.float32)[:, None]
        slab = orders // lat

        def arrange(parts):
            stacked = np.stack(parts).reshape(2, lat, slab, points).transpose(1, 0, 2, 3)
            return stacked.reshape(2 * orders, points).astype(ml_dtypes.bfloat16)

        forward = arrange([cosine, -sine])
        inverse = arrange([factor * cosine, -factor * sine])
        return forward, inverse

    return build


def row_tile(rows, most):
    fits = [t for t in range(16, most + 1, 16) if rows % t == 0]
    return fits[-1] if fits else rows


def norm_parts(values):
    center = values - jnp.mean(values, axis=-1, keepdims=True)
    spread = jnp.mean(center * center, axis=-1, keepdims=True)
    scaled = lax.rsqrt(spread + epsilon)
    return center * scaled, scaled


def norm_back(grad_out, normal, scaled, gain):
    grad_norm = grad_out * gain
    inner = jnp.mean(grad_norm, axis=-1, keepdims=True)
    cross = jnp.mean(grad_norm * normal, axis=-1, keepdims=True)
    return scaled * (grad_norm - inner - normal * cross)


def fold(values):
    rows, width = values.shape
    return jnp.sum(values.reshape(rows // 8, 8, width), axis=0)


def dot(a, b):
    return jnp.dot(a, b, preferred_element_type=jnp.float32)


def dot_t(a, b):
    return lax.dot_general(a, b, (((1,), (1,)), ((), ())), preferred_element_type=jnp.float32)


def t_dot(a, b):
    return lax.dot_general(a, b, (((0,), (0,)), ((), ())), preferred_element_type=jnp.float32)


def block_kernel(
    lat,
    lon,
    x_hbm,
    g_hbm,
    fwd_t,
    inv_t,
    inv,
    fwd,
    raw_ana,
    raw_syn,
    weight,
    skip,
    mlp_in,
    mlp_out,
    gain_one,
    bias_one,
    gain_two,
    bias_two,
    bias_in,
    bias_out,
    out_hbm,
    gin_hbm,
    total_hbm,
    total_spec,
    total_norm,
    x_all,
    normed,
    mixed,
    lon_a,
    lon_b,
    lat_a,
    lat_b,
    coeffs,
    send_2,
    send_3,
    send_4,
    send_6,
    send_7,
    send_8,
    wide,
    slim,
    g_buf,
    o_buf,
    i_buf,
    recv_sem,
    send_sem,
    x_sem,
    g_sem,
    o_sem,
    i_sem,
    ana,
    ana_t,
    syn,
    syn_t,
    w_parts,
    w_real,
    w_imag,
    acc,
    part_core,
    part_chip,
    part_lat,
    spec,
    spec_lat,
    spec_lon,
    spec_sum,
    norm_sums,
    norm_own,
    norm_lon,
    norm_lat,
    w_sem,
    fold_recv,
    fold_send,
    spec_recv,
    spec_send,
    spec_pair,
    norm_recv,
    norm_send,
    own_sem,
):
    batch, rows, width = x_hbm.shape
    halves = width // LANES
    group = lon // halves
    chunks = batch // group
    points = fwd_t.shape[1]
    slab, lats, degrees = raw_ana.shape
    narrow = width // lon
    hidden = mlp_in.shape[1]
    band = lats // lat
    block = 2 * slab * band
    waves = 2 * slab * lat
    my_lat, my_lon = lax.axis_index("lat"), lax.axis_index("lon")
    half_tile = row_tile(rows, 144)
    full_tile = row_tile(rows, 240)

    def lon_copy(stage, chunk, src, dst, peer):
        return pltpu.make_async_remote_copy(
            src_ref=src,
            dst_ref=dst,
            send_sem=send_sem.at[stage - 1],
            recv_sem=recv_sem.at[stage - 1, chunk],
            device_id={"lon": peer},
            device_id_type=MESH,
        )

    def lat_copy(stage, chunk, src, dst, peer):
        return pltpu.make_async_remote_copy(
            src_ref=src,
            dst_ref=dst,
            send_sem=send_sem.at[stage - 1],
            recv_sem=recv_sem.at[stage - 1, chunk],
            device_id={"lat": peer},
            device_id_type=MESH,
        )

    def own_copy(stage, chunk, src, dst):
        return pltpu.make_async_copy(src, dst, recv_sem.at[stage - 1, chunk])

    def landed(stage, chunk, whole):
        pltpu.make_async_copy(whole, whole, recv_sem.at[stage - 1, chunk]).wait()

    def sent(stage, part):
        lon_copy(stage, 0, part, part, my_lon).wait_send()

    def x_load(sample):
        return pltpu.make_async_copy(x_hbm.at[sample], x_all.at[sample], x_sem.at[sample])

    def g_load(sample, slot):
        return pltpu.make_async_copy(g_hbm.at[sample], g_buf.at[slot], g_sem.at[slot])

    def o_store(sample, slot):
        return pltpu.make_async_copy(o_buf.at[slot], out_hbm.at[sample], o_sem.at[slot])

    def i_store(sample, slot):
        return pltpu.make_async_copy(i_buf.at[slot], gin_hbm.at[sample], i_sem.at[slot])

    def spread_rows(stage, chunk, held, sample):
        src = chunk * group + sample
        for half in range(halves):
            peer = sample * halves + half

            @pl.when(peer != my_lon)
            def _(peer=peer, half=half):
                lon_copy(stage, chunk, held.at[src, half], lon_a.at[chunk, my_lon], peer).start()

            @pl.when(peer == my_lon)
            def _(half=half):
                own_copy(stage, chunk, held.at[src, half], lon_a.at[chunk, my_lon]).start()

    def spread_bands(stage, chunk, buffer, target):
        for step in range(1, lat):
            peer = lax.rem(my_lat + step, lat)
            lat_copy(stage, chunk, buffer.at[peer], target.at[chunk, my_lat], peer).start()

    def pair(values, factor):
        return jnp.concatenate([values(0), values(1)], axis=1).astype(jnp.bfloat16)

    def to_waves(stage, chunk, table, scale, buffer):
        landed(stage - 1, chunk, lon_a.at[chunk])
        for source in range(lon):
            wide[pl.ds(source * rows, rows), :] = lon_a[chunk, source, pl.ds(0, rows), :].astype(jnp.float32)
        for first in range(0, band, 2):
            rhs = jnp.concatenate(
                [wide[pl.ds(first + k, points, stride=band), :] for k in range(2)], axis=1
            ).astype(jnp.bfloat16)
            got = dot(table[...], rhs)
            if scale is not None:
                got = got * scale
            for k in range(2):
                slim[pl.ds(first + k, waves, stride=band), :] = got[:, k * LANES : (k + 1) * LANES]

        @pl.when(chunk > 0)
        def _():
            sent(stage, buffer.at[pl.ds(0, lat - 1)])

        for target in range(lat):
            buffer[target] = slim[pl.ds(target * block, block), :].astype(jnp.bfloat16)
        spread_bands(stage, chunk, buffer, lat_a)
        own = pl.ds(pl.multiple_of(my_lat * block, 8), block)
        lat_a[chunk, my_lat] = slim[own, :].astype(jnp.bfloat16)

    def to_points(stage, chunk, table, scale, buffer):
        landed(stage - 1, chunk, lat_b.at[chunk, pl.ds(0, lat - 1)])
        for source in range(lat):
            slim[pl.ds(source * block, block), :] = lat_b[chunk, source].astype(jnp.float32)
        for first in range(0, band, 2):
            rhs = jnp.concatenate(
                [slim[pl.ds(first + k, waves, stride=band), :] for k in range(2)], axis=1
            ).astype(jnp.bfloat16)
            got = dot(table[...], rhs)
            if scale is not None:
                got = got * scale
            for k in range(2):
                wide[pl.ds(first + k, points, stride=band), :] = got[:, k * LANES : (k + 1) * LANES]

        @pl.when(chunk > 0)
        def _():
            sent(stage, buffer.at[pl.ds(0, lon - 1)])

        for target in range(lon):
            buffer[target, pl.ds(0, rows), :] = wide[pl.ds(target * rows, rows), :].astype(jnp.bfloat16)
        sample, half = chunk * group + my_lon // halves, lax.rem(my_lon, halves)
        for step in range(1, lon):
            peer = lax.rem(my_lon + step, lon)
            lon_copy(stage, chunk, buffer.at[peer], lon_b.at[sample, half], peer).start()
        own = pl.ds(pl.multiple_of(my_lon * rows, 8), rows)
        lon_b[sample, half, pl.ds(0, rows), :] = wide[own, :].astype(jnp.bfloat16)

    def slab_step(stage, chunk, first_table, second_table, between, buffer):
        landed(stage - 1, chunk, lat_a.at[chunk, pl.ds(0, lat - 1)])
        for source in range(lat):
            slim[pl.ds(source * block, block), :] = lat_a[chunk, source].astype(jnp.float32)
        for m in range(slab):
            parts = []
            for r in range(2):
                at = (r * slab + m) * band
                parts.append(
                    jnp.concatenate([slim[pl.ds(s * block + at, band), :] for s in range(lat)], axis=0)
                )
            rhs = jnp.concatenate(parts, axis=1).astype(jnp.bfloat16)
            real, imag = between(m, dot(first_table[m], rhs))
            low = jnp.concatenate([real, imag], axis=1).astype(jnp.bfloat16)
            got = dot(second_table[m], low)
            for r in range(2):
                at = (r * slab + m) * band
                for t in range(lat):
                    wide[pl.ds(t * block + at, band), :] = got[
                        t * band : (t + 1) * band, r * LANES : (r + 1) * LANES
                    ]

        @pl.when(chunk > 0)
        def _():
            sent(stage, buffer.at[pl.ds(0, lat - 1)])

        for target in range(lat):
            buffer[target] = wide[pl.ds(target * block, block), :].astype(jnp.bfloat16)
        spread_bands(stage, chunk, buffer, lat_b)
        own = pl.ds(pl.multiple_of(my_lat * block, 8), block)
        lat_b[chunk, my_lat] = wide[own, :].astype(jnp.bfloat16)

    hidden_rows = width * hidden // LANES
    vector_rows = 2 * hidden_rows + width * width // LANES

    def gather_rows(base, values):
        count = values.shape[0]
        for q in range(values.shape[1] // LANES):
            acc[pl.ds(base + q * count, count), :] += values[:, q * LANES : (q + 1) * LANES]

    def both(held, sample, where):
        return jnp.concatenate([held[sample, h, where, :] for h in range(halves)], axis=1)

    def normalize(sample):
        x_load(sample).wait()

        @pl.loop(0, rows // half_tile)
        def _(i):
            where = pl.ds(pl.multiple_of(i * half_tile, 8), half_tile)
            normal, _ = norm_parts(x_all[sample, where, :].astype(jnp.float32))
            low = (normal * gain_one[...] + bias_one[...]).astype(jnp.bfloat16)
            for h in range(halves):
                normed[sample, h, where, :] = low[:, h * LANES : (h + 1) * LANES]

    def stage_1(chunk):
        @pl.when(chunk > 0)
        def _():
            sent(1, lon_a.at[chunk, pl.ds(0, lon - 1)])

        for k in range(group):

            @pl.when(chunk > 0)
            def _():
                normalize(chunk * group + k)

            spread_rows(1, chunk, normed, k)

    def stage_2(chunk):
        to_waves(2, chunk, fwd_t, 1.0 / points, send_2)

    def stage_3(chunk):
        def between(m, got):
            coeffs[chunk, m] = got.astype(jnp.bfloat16)
            real, imag = got[:, :LANES], got[:, LANES:]
            return (
                w_real[...] * real - w_imag[...] * imag,
                w_real[...] * imag + w_imag[...] * real,
            )

        slab_step(3, chunk, ana, syn, between, send_3)

    def stage_4(chunk):
        to_points(4, chunk, inv, None, send_4)

    def stage_5a(chunk):
        landed(4, chunk, lon_a.at[chunk, pl.ds(0, lon - 1)])

        @pl.when(chunk > 0)
        def _():
            sent(5, lon_a.at[chunk, pl.ds(0, lon - 1)])

        feed_forward(chunk, range(group // 2))

    def stage_5b(chunk):
        feed_forward(chunk, range(group // 2, group))

    def feed_forward(chunk, members):
        for k in members:
            sample = chunk * group + k
            g_load(sample, k).wait()

            @pl.when(chunk > 0)
            def _():
                o_store(sample, k).wait()

            @pl.loop(0, rows // full_tile)
            def _(i):
                where = pl.ds(pl.multiple_of(i * full_tile, 8), full_tile)
                low_one = both(normed, sample, where)
                spatial = both(lon_b, sample, where).astype(jnp.float32)
                resid = x_all[sample, where, :].astype(jnp.float32) + (spatial + dot(low_one, skip[...]))
                normal, scaled = norm_parts(resid)
                low_two = (normal * gain_two[...] + bias_two[...]).astype(jnp.bfloat16)
                pre = dot(low_two, mlp_in[...]) + bias_in[...]
                square = pre * pre
                curve = jnp.tanh(root * pre * (1.0 + cubic * square))
                lifted = 0.5 + 0.5 * curve
                act = (pre * lifted).astype(jnp.bfloat16)
                slope = lifted + (0.5 * root) * pre * (1.0 - curve * curve) * (1.0 + (3.0 * cubic) * square)
                o_buf[k, where, :] = (resid + dot(act, mlp_out[...]) + bias_out[...]).astype(jnp.bfloat16)
                g_low = g_buf[k, where, :]
                gather_rows(hidden_rows, t_dot(g_low, act))
                grad_pre = (dot_t(g_low, mlp_out[...]) * slope).astype(jnp.bfloat16)
                gather_rows(0, t_dot(low_two, grad_pre))
                gather_rows(vector_rows, fold(grad_pre.astype(jnp.float32)))
                grad_second = dot_t(grad_pre, mlp_in[...])
                g_full = g_low.astype(jnp.float32)
                for at, values in enumerate((g_full, grad_second * normal, grad_second)):
                    gather_rows(vector_rows + 8 * (hidden + at * width) // LANES, fold(values))
                grad_mixed = (g_full + norm_back(grad_second, normal, scaled, gain_two[...])).astype(jnp.bfloat16)
                gather_rows(2 * hidden_rows, t_dot(low_one, grad_mixed))
                for h in range(halves):
                    mixed[sample, h, where, :] = grad_mixed[:, h * LANES : (h + 1) * LANES]

            o_store(sample, k).start()

            @pl.when(chunk < chunks - 1)
            def _():
                g_load(sample + group, k).start()

            spread_rows(5, chunk, mixed, k)

    def stage_6(chunk):
        to_waves(6, chunk, inv_t, None, send_6)

    def stage_7(chunk):
        def between(m, got):
            dr, di = got[:, :LANES], got[:, LANES:]
            held = coeffs[chunk, m].astype(jnp.float32)
            ar, ai = held[:, :LANES], held[:, LANES:]
            spec[pl.ds(0, degrees), :] += dr * ar + di * ai
            spec[pl.ds(degrees, degrees), :] += di * ar - dr * ai
            return (
                w_real[...] * dr + w_imag[...] * di,
                w_real[...] * di - w_imag[...] * dr,
            )

        slab_step(7, chunk, syn_t, ana_t, between, send_7)

    def stage_8(chunk):
        to_points(8, chunk, fwd, 1.0 / points, send_8)

    def stage_9(chunk):
        landed(8, chunk, lon_a.at[chunk, pl.ds(0, lon - 1)])
        for k in range(group):
            sample = chunk * group + k

            @pl.when(chunk > 0)
            def _():
                i_store(sample, k).wait()

            @pl.loop(0, rows // half_tile)
            def _(i):
                where = pl.ds(pl.multiple_of(i * half_tile, 8), half_tile)
                normal, scaled = norm_parts(x_all[sample, where, :].astype(jnp.float32))
                low = both(mixed, sample, where)
                grad_normed = dot_t(low, skip[...]) + both(lon_b, sample, where).astype(jnp.float32)
                norm_sums[0] += fold(grad_normed * normal)
                norm_sums[1] += fold(grad_normed)
                i_buf[k, where, :] = low.astype(jnp.float32) + norm_back(
                    grad_normed, normal, scaled, gain_one[...]
                )

            i_store(sample, k).start()

    def weight_copies(start):
        place = lax.rem(my_lon, group)
        held = w_parts.at[:, pl.ds(pl.multiple_of(place * narrow, 8), narrow), :]
        for q in range(group):
            peer = my_lon // group + halves * q

            @pl.when(peer != my_lon)
            def _(peer=peer, q=q):
                copy = pltpu.make_async_remote_copy(
                    src_ref=weight,
                    dst_ref=held,
                    send_sem=w_sem.at[1, q],
                    recv_sem=w_sem.at[0, place],
                    device_id={"lon": peer},
                    device_id_type=MESH,
                )
                if start:
                    copy.start()
                else:
                    copy.wait_send()

            if start:

                @pl.when(peer == my_lon)
                def _():
                    pltpu.make_async_copy(weight, held, w_sem.at[0, place]).start()

    def build():
        acc[...] = jnp.zeros_like(acc)
        spec[...] = jnp.zeros_like(spec)
        norm_sums[...] = jnp.zeros_like(norm_sums)
        norm_own[...] = jnp.zeros_like(norm_own)
        degree = lax.broadcasted_iota(jnp.int32, (lats, degrees), 1)

        @pl.loop(0, slab)
        def _(m):
            kept = degree >= my_lat * slab + m
            for raw, plain, turned in ((raw_ana, ana_t, ana), (raw_syn, syn, syn_t)):
                values = jnp.where(kept, raw[m].astype(jnp.float32), 0.0)
                plain[m] = values.astype(jnp.bfloat16)
                turned[m] = values.T.astype(jnp.bfloat16)

        for q in range(group):
            part = w_parts.at[:, pl.ds(q * narrow, narrow), :]
            pltpu.make_async_copy(part, part, w_sem.at[0, q]).wait()
        w_real[...] = w_parts[0].T
        w_imag[...] = w_parts[1].T

    total_rows = acc.shape[0]
    place_core, place_chip = lax.rem(my_lon, 2), my_lon // 2
    levels = (
        (2, place_core, part_core, lambda p: {"lon": 2 * place_chip + p}),
        (lon // 2, place_chip, part_chip, lambda p: {"lon": 2 * p + place_core}),
        (lat, my_lat, part_lat, lambda p: {"lat": p}),
    )
    bases, sizes = [0], [total_rows]
    for count, place, _, _ in levels:
        sizes.append(sizes[-1] // count)
        bases.append(bases[-1] + place * sizes[-1])

    def row_part(at, count):
        return pl.ds(pl.multiple_of(at, 8), count)

    def fold_start(k):
        count, place, parts, device = levels[k]
        for step in range(1, count):
            peer = lax.rem(place + step, count)
            pltpu.make_async_remote_copy(
                src_ref=acc.at[row_part(bases[k] + peer * sizes[k + 1], sizes[k + 1]), :],
                dst_ref=parts.at[step - 1],
                send_sem=fold_send.at[0, k],
                recv_sem=fold_recv.at[0, k],
                device_id=device(peer),
                device_id_type=MESH,
            ).start()

    def fold_end(k):
        count, _, parts, _ = levels[k]
        pltpu.make_async_copy(parts, parts, fold_recv.at[0, k]).wait()
        got = parts[0]
        for step in range(2, count):
            got = got + parts[step - 1]
        acc[row_part(bases[k + 1], sizes[k + 1]), :] += got

    def spread_start(k):
        count, place, _, device = levels[k]
        own = row_part(bases[k + 1], sizes[k + 1])
        src = acc if k == len(levels) - 1 else total_hbm
        for step in range(1, count):
            pltpu.make_async_remote_copy(
                src_ref=src.at[own, :],
                dst_ref=total_hbm.at[own, :],
                send_sem=fold_send.at[1, k],
                recv_sem=fold_recv.at[1, k],
                device_id=device(lax.rem(place + step, count)),
                device_id_type=MESH,
            ).start()
        if src is acc:
            pltpu.make_async_copy(acc.at[own, :], total_hbm.at[own, :], own_sem).start()

    def spread_end(k):
        count = levels[k][0]
        all_parts = total_hbm.at[pl.ds(0, (count - 1) * sizes[k + 1]), :]
        pltpu.make_async_copy(all_parts, all_parts, fold_recv.at[1, k]).wait()
        if k == len(levels) - 1:
            own = row_part(bases[k + 1], sizes[k + 1])
            pltpu.make_async_copy(acc.at[own, :], total_hbm.at[own, :], own_sem).wait()

    def fold_sent():
        for k, (count, _, _, _) in enumerate(levels):
            for way in range(2):
                part = total_hbm if way and k < len(levels) - 1 else acc
                part = part.at[pl.ds(0, (count - 1) * sizes[k + 1]), :]
                pltpu.make_async_remote_copy(
                    src_ref=part,
                    dst_ref=part,
                    send_sem=fold_send.at[way, k],
                    recv_sem=fold_recv.at[way, k],
                    device_id={"lon": my_lon},
                    device_id_type=MESH,
                ).wait_send()

    spec_rows = spec_sum.shape[0]

    def spec_lat_copies(way, src, dst):
        for step in range(1, lat):
            peer = lax.rem(my_lat + step, lat)
            pltpu.make_async_remote_copy(
                src_ref=src(peer),
                dst_ref=dst(step),
                send_sem=spec_send.at[way],
                recv_sem=spec_recv.at[way],
                device_id={"lat": peer},
                device_id_type=MESH,
            ).start()

    def spec_start():
        spec_lat_copies(
            0, lambda p: spec.at[row_part(p * spec_rows, spec_rows), :], lambda s: spec_lat.at[s - 1]
        )

    def spec_pairs(action):
        half = lax.rem(my_lon, halves)
        for q in range(group):
            target = half * group + q

            @pl.when(target != my_lon)
            def _(target=target, q=q):
                copy = pltpu.make_async_remote_copy(
                    src_ref=spec_sum,
                    dst_ref=spec_lon.at[my_lon // halves],
                    send_sem=spec_pair.at[1, q],
                    recv_sem=spec_pair.at[0, my_lon // halves],
                    device_id={"lon": target},
                    device_id_type=MESH,
                )
                if action == "start":
                    copy.start()
                else:
                    copy.wait_send()

            if action == "start":

                @pl.when(target == my_lon)
                def _():
                    pltpu.make_async_copy(
                        spec_sum, spec_lon.at[my_lon // halves], spec_pair.at[0, my_lon // halves]
                    ).start()

    def spec_middle():
        pltpu.make_async_copy(spec_lat, spec_lat, spec_recv.at[0]).wait()
        got = spec[row_part(my_lat * spec_rows, spec_rows), :]
        for step in range(1, lat):
            got = got + spec_lat[step - 1]
        spec_sum[...] = got
        spec_pairs("start")

    def spec_back():
        for q in range(group):
            pltpu.make_async_copy(spec_lon.at[q], spec_lon.at[q], spec_pair.at[0, q]).wait()
        got = spec_lon[0]
        for q in range(1, group):
            got = got + spec_lon[q]
        own = row_part(my_lat * spec_rows, spec_rows)
        total_spec[own, :] = got
        spec_lat_copies(1, lambda p: total_spec.at[own, :], lambda s: total_spec.at[own, :])

    def spec_end():
        part = total_spec.at[pl.ds(0, (lat - 1) * spec_rows), :]
        pltpu.make_async_copy(part, part, spec_recv.at[1]).wait()
        for way in range(2):
            pltpu.make_async_remote_copy(
                src_ref=part,
                dst_ref=part,
                send_sem=spec_send.at[way],
                recv_sem=spec_recv.at[way],
                device_id={"lat": my_lat},
                device_id_type=MESH,
            ).wait_send()
        spec_pairs("end")

    def norm_copies(way, axis, count, place, src, parts, action):
        for step in range(1, count):
            copy = pltpu.make_async_remote_copy(
                src_ref=src,
                dst_ref=parts.at[step - 1],
                send_sem=norm_send.at[way, step - 1],
                recv_sem=norm_recv.at[way],
                device_id={axis: lax.rem(place + step, count)},
                device_id_type=MESH,
            )
            if action == "start":
                copy.start()
            else:
                copy.wait_send()

    def norm_fold(way, axis, count, place, src, parts, out):
        norm_copies(way, axis, count, place, src, parts, "start")
        pltpu.make_async_copy(parts, parts, norm_recv.at[way]).wait()
        got = src[...]
        for step in range(1, count):
            got = got + parts[step - 1]
        out[...] = got

    def norm_all():
        for which in range(2):
            line = jnp.sum(norm_sums[which], axis=0, keepdims=True)
            for h in range(halves):
                norm_own[0, pl.ds(which * halves + h, 1), :] = line[:, h * LANES : (h + 1) * LANES]
        norm_fold(0, "lon", lon, my_lon, norm_own.at[0], norm_lon, norm_own.at[1])
        norm_fold(1, "lat", lat, my_lat, norm_own.at[1], norm_lat, total_norm)
        norm_copies(0, "lon", lon, my_lon, norm_own.at[0], norm_lon, "end")
        norm_copies(1, "lat", lat, my_lat, norm_own.at[1], norm_lat, "end")

    def run(*steps):
        def go():
            for step, k in steps:
                step() if k is None else step(k)

        return go

    end = chunks - 1
    aside = {
        (0, "1"): build,
        (end + OFFSET["5b"], "5b"): run((fold_start, 0)),
        (end + OFFSET["5b"], "9"): run((fold_end, 0), (fold_start, 1)),
        (end + OFFSET["6"], "8"): run((fold_end, 1), (fold_start, 2)),
        (end + OFFSET["7"], "7"): run((spec_start, None)),
        (end + OFFSET["7"], "8"): run((fold_end, 2), (spread_start, 2)),
        (end + OFFSET["7"], "9"): run((spec_middle, None)),
        (end + OFFSET["8"], "8"): run((spread_end, 2), (spread_start, 1)),
        (end + OFFSET["8"], "9"): run((spec_back, None)),
        (end + OFFSET["9"], "8"): run((spread_end, 1), (spread_start, 0)),
    }

    stages = {
        "1": stage_1,
        "2": stage_2,
        "3": stage_3,
        "4": stage_4,
        "5a": stage_5a,
        "5b": stage_5b,
        "6": stage_6,
        "7": stage_7,
        "8": stage_8,
        "9": stage_9,
    }

    for sample in range(batch):
        x_load(sample).start()
    for k in range(group):
        g_load(k, k).start()

    padded = lon_a.shape[2]
    if padded > rows:
        for held in (normed, mixed):
            held[:, :, rows:, :] = jnp.zeros_like(held[:, :, rows:, :])
        for held in (send_4, send_8):
            held[:, rows:, :] = jnp.zeros_like(held[:, rows:, :])
    barrier = pltpu.get_barrier_semaphore()
    for step in range(1, lon):
        pl.semaphore_signal(
            barrier, inc=1, device_id={"lon": lax.rem(my_lon + step, lon)}, device_id_type=MESH
        )
    for step in range(1, lat):
        pl.semaphore_signal(
            barrier, inc=1, device_id={"lat": lax.rem(my_lat + step, lat)}, device_id_type=MESH
        )
    for k in range(group):
        normalize(k)
    pl.semaphore_wait(barrier, lon - 1 + lat - 1)

    weight_copies(True)

    def tick(now, carry):
        for stage in ORDER:
            chunk = now - OFFSET[stage]

            @pl.when(jnp.logical_and(chunk >= 0, chunk < chunks))
            def _(stage=stage, chunk=chunk):
                stages[stage](chunk)

            for (when, after), action in aside.items():
                if after == stage:
                    pl.when(now == when)(action)

        return carry

    lax.fori_loop(0, chunks + max(OFFSET.values()), tick, 0)

    norm_all()
    spread_end(0)
    spec_end()
    fold_sent()
    weight_copies(False)
    last = chunks - 1
    for stage in (1, 5):
        sent(stage, lon_a.at[last, pl.ds(0, lon - 1)])
    for stage, buffer, count in (
        (2, send_2, lat - 1),
        (3, send_3, lat - 1),
        (4, send_4, lon - 1),
        (6, send_6, lat - 1),
        (7, send_7, lat - 1),
        (8, send_8, lon - 1),
    ):
        sent(stage, buffer.at[pl.ds(0, count)])
    for k in range(group):
        o_store(last * group + k, k).wait()
        i_store(last * group + k, k).wait()


def per_device(
    tables,
    lat,
    lon,
    inputs,
    legendre_forward,
    legendre_inverse,
    spectral_weight,
    skip_weight,
    gain_first,
    bias_first,
    gain_second,
    bias_second,
    mlp_in,
    mlp_in_bias,
    mlp_out,
    mlp_out_bias,
    cotangent,
):
    batch, band, columns, width = inputs.shape
    points = columns * lon
    slab, degrees, lats = legendre_forward.shape
    orders = slab * lat
    hidden = mlp_in.shape[1]
    rows = columns * band
    padded = -(-rows // 16) * 16
    halves = width // LANES
    group = lon // halves
    chunks = batch // group
    block = 2 * slab * band
    waves = 2 * orders

    forward, inverse = tables(points, lat)(orders)
    my_lon = lax.axis_index("lon")
    hidden = mlp_in.shape[1]
    flat_rows = (2 * hidden + width) * width // LANES + 8 * (hidden + 3 * width) // LANES
    share = -(-flat_rows // (8 * lat * lon)) * 8
    total_rows = share * lat * lon
    spec_rows = -(-2 * degrees // (8 * lat)) * 8

    def flat(values):
        return values.transpose(0, 2, 1, 3).reshape(batch, rows, width)

    def row(values):
        return values.reshape(1, -1)

    vmem = pl.BlockSpec(memory_space=pltpu.VMEM)
    hbm = pl.BlockSpec(memory_space=pl.ANY)
    low, full = jnp.bfloat16, jnp.float32
    results = pl.pallas_call(
        functools.partial(block_kernel, lat, lon),
        out_shape=(
            jax.ShapeDtypeStruct((batch, rows, width), low),
            jax.ShapeDtypeStruct((batch, rows, width), full),
            jax.ShapeDtypeStruct((total_rows, LANES), full),
            jax.ShapeDtypeStruct((lat * spec_rows, LANES), full),
            jax.ShapeDtypeStruct((8, LANES), full),
        ),
        in_specs=[hbm, hbm] + [vmem] * 16,
        out_specs=(hbm, hbm, hbm, vmem, vmem),
        scratch_shapes=[
            pltpu.VMEM((batch, rows, width), low),
            pltpu.VMEM((batch, halves, padded, LANES), low),
            pltpu.VMEM((batch, halves, padded, LANES), low),
            pltpu.VMEM((chunks, lon, padded, LANES), low),
            pltpu.VMEM((batch, halves, padded, LANES), low),
            pltpu.VMEM((chunks, lat, block, LANES), low),
            pltpu.VMEM((chunks, lat, block, LANES), low),
            pltpu.VMEM((chunks, slab, degrees, 2 * LANES), low),
            pltpu.VMEM((lat, block, LANES), low),
            pltpu.VMEM((lat, block, LANES), low),
            pltpu.VMEM((lon, padded, LANES), low),
            pltpu.VMEM((lat, block, LANES), low),
            pltpu.VMEM((lat, block, LANES), low),
            pltpu.VMEM((lon, padded, LANES), low),
            pltpu.VMEM((max(points, waves) * band, LANES), full),
            pltpu.VMEM((waves * band, LANES), full),
            pltpu.VMEM((group, rows, width), low),
            pltpu.VMEM((group, rows, width), low),
            pltpu.VMEM((group, rows, width), full),
            pltpu.SemaphoreType.DMA((8, chunks)),
            pltpu.SemaphoreType.DMA((8,)),
            pltpu.SemaphoreType.DMA((batch,)),
            pltpu.SemaphoreType.DMA((group,)),
            pltpu.SemaphoreType.DMA((group,)),
            pltpu.SemaphoreType.DMA((group,)),
            pltpu.VMEM((slab, degrees, lats), low),
            pltpu.VMEM((slab, lats, degrees), low),
            pltpu.VMEM((slab, lats, degrees), low),
            pltpu.VMEM((slab, degrees, lats), low),
            pltpu.VMEM((2, LANES, degrees), full),
            pltpu.VMEM((degrees, LANES), full),
            pltpu.VMEM((degrees, LANES), full),
            pltpu.VMEM((total_rows, LANES), full),
            pltpu.VMEM((1, total_rows // 2, LANES), full),
            pltpu.VMEM((lon // 2 - 1, total_rows // lon, LANES), full),
            pltpu.VMEM((lat - 1, share, LANES), full),
            pltpu.VMEM((lat * spec_rows, LANES), full),
            pltpu.VMEM((lat - 1, spec_rows, LANES), full),
            pltpu.VMEM((group, spec_rows, LANES), full),
            pltpu.VMEM((spec_rows, LANES), full),
            pltpu.VMEM((2, 8, width), full),
            pltpu.VMEM((2, 8, LANES), full),
            pltpu.VMEM((lon - 1, 8, LANES), full),
            pltpu.VMEM((lat - 1, 8, LANES), full),
            pltpu.SemaphoreType.DMA((2, group)),
            pltpu.SemaphoreType.DMA((2, 3)),
            pltpu.SemaphoreType.DMA((2, 3)),
            pltpu.SemaphoreType.DMA((2,)),
            pltpu.SemaphoreType.DMA((2,)),
            pltpu.SemaphoreType.DMA((2, group)),
            pltpu.SemaphoreType.DMA((2,)),
            pltpu.SemaphoreType.DMA((2, max(lat, lon) - 1)),
            pltpu.SemaphoreType.DMA,
        ],
        compiler_params=pltpu.CompilerParams(
            collective_id=0, has_side_effects=True, vmem_limit_bytes=63 * 2**20
        ),
    )(
        flat(inputs),
        flat(cotangent),
        jnp.asarray(forward),
        jnp.asarray(inverse),
        jnp.asarray(inverse.T),
        jnp.asarray(forward.T),
        legendre_forward.transpose(0, 2, 1),
        legendre_inverse,
        spectral_weight.transpose(0, 2, 1),
        skip_weight,
        mlp_in,
        mlp_out,
        row(gain_first),
        row(bias_first),
        row(gain_second),
        row(bias_second),
        row(mlp_in_bias),
        row(mlp_out_bias),
    )
    output, grad_inputs, total, spec, norm = results

    def unflat(values):
        return values.reshape(batch, columns, band, width).transpose(0, 2, 1, 3)

    def wide_part(base, height, across):
        part = total[base : base + height * across // LANES]
        return part.reshape(across // LANES, height, LANES).transpose(1, 0, 2).reshape(height, across)

    hidden_rows = width * hidden // LANES
    vector_rows = 2 * hidden_rows + width * width // LANES
    vectors = total[vector_rows:flat_rows].reshape(-1, 8, LANES).sum(axis=1).reshape(-1)
    spec = spec[: 2 * degrees].reshape(2, degrees, LANES)
    narrow = width // lon
    grad_spec = lax.dynamic_slice_in_dim(spec, lax.rem(my_lon, group) * narrow, narrow, axis=2)
    norm = norm[: 2 * halves].reshape(2, width)
    return (
        unflat(output),
        unflat(grad_inputs),
        grad_spec,
        wide_part(2 * hidden_rows, width, width),
        norm[0],
        norm[1],
        vectors[hidden + width : hidden + 2 * width],
        vectors[hidden + 2 * width :],
        wide_part(0, width, hidden),
        vectors[:hidden],
        wide_part(hidden_rows, width, hidden).T,
        vectors[hidden : hidden + width],
    )


def solution(mesh):
    lat, lon = mesh.shape["lat"], mesh.shape["lon"]
    grid = P(None, "lat", "lon", None)
    table = P("lat", None, None)
    channel = P(None, None, "lon")
    return jax.shard_map(
        functools.partial(per_device, fourier_tables, lat, lon),
        mesh=mesh,
        in_specs=(grid, table, table, channel) + (P(),) * 9 + (grid,),
        out_specs=(grid, grid, channel) + (P(),) * 9,
        check_vma=False,
    )
```

```python
import functools
import math

import jax
import jax.numpy as jnp
import ml_dtypes
import numpy as np
from jax import lax
from jax.experimental import pallas as pl
from jax.experimental.pallas import tpu as pltpu
from jax.sharding import PartitionSpec as P

epsilon = 1e-05
LANES = 128
MESH = pl.DeviceIdType.MESH
root = math.sqrt(2.0 / math.pi)
cubic = 0.044715

OFFSET = {"1": 0, "2": 1, "3": 3, "4": 4, "5a": 5, "5b": 5, "6": 7, "7": 9, "8": 10, "9": 11}
ORDER = ("1", "3", "7", "4", "5a", "6", "2", "5b", "8", "9")


def fourier_tables(points, lat):
    def build(orders):
        waves = np.arange(orders)
        phase = (waves[:, None] * np.arange(points)[None, :] % points).astype(np.float32)
        phase = phase * np.float32(2.0 * math.pi / points)
        cosine, sine = np.cos(phase), np.sin(phase)
        factor = np.where(waves == 0, 1.0, 2.0).astype(np.float32)[:, None]
        slab = orders // lat

        def arrange(parts):
            stacked = np.stack(parts).reshape(2, lat, slab, points).transpose(1, 0, 2, 3)
            return stacked.reshape(2 * orders, points).astype(ml_dtypes.bfloat16)

        forward = arrange([cosine, -sine])
        inverse = arrange([factor * cosine, -factor * sine])
        return forward, inverse

    return build


def row_tile(rows, most):
    fits = [t for t in range(16, most + 1, 16) if rows % t == 0]
    return fits[-1] if fits else rows


def norm_parts(values):
    center = values - jnp.mean(values, axis=-1, keepdims=True)
    spread = jnp.mean(center * center, axis=-1, keepdims=True)
    scaled = lax.rsqrt(spread + epsilon)
    return center * scaled, scaled


def norm_back(grad_out, normal, scaled, gain):
    grad_norm = grad_out * gain
    inner = jnp.mean(grad_norm, axis=-1, keepdims=True)
    cross = jnp.mean(grad_norm * normal, axis=-1, keepdims=True)
    return scaled * (grad_norm - inner - normal * cross)


def fold(values):
    rows, width = values.shape
    return jnp.sum(values.reshape(rows // 8, 8, width), axis=0)


def dot(a, b):
    return jnp.dot(a, b, preferred_element_type=jnp.float32)


def dot_t(a, b):
    return lax.dot_general(a, b, (((1,), (1,)), ((), ())), preferred_element_type=jnp.float32)


def t_dot(a, b):
    return lax.dot_general(a, b, (((0,), (0,)), ((), ())), preferred_element_type=jnp.float32)


def block_kernel(
    lat,
    lon,
    x_hbm,
    g_hbm,
    fwd_t,
    inv_t,
    inv,
    fwd,
    raw_ana,
    raw_syn,
    weight,
    skip,
    mlp_in,
    mlp_out,
    gain_one,
    bias_one,
    gain_two,
    bias_two,
    bias_in,
    bias_out,
    out_hbm,
    gin_hbm,
    total_hbm,
    x_all,
    normed,
    mixed,
    lon_a,
    lon_b,
    lat_a,
    lat_b,
    coeffs,
    send_2,
    send_3,
    send_4,
    send_6,
    send_7,
    send_8,
    wide,
    slim,
    g_buf,
    o_buf,
    i_buf,
    recv_sem,
    send_sem,
    x_sem,
    g_sem,
    o_sem,
    i_sem,
    ana,
    ana_t,
    syn,
    syn_t,
    w_parts,
    w_real,
    w_imag,
    acc,
    part_core,
    part_near,
    part_chip,
    part_far,
    spec,
    spec_lat,
    spec_lon,
    spec_sum,
    spec_own,
    norm_sums,
    norm_own,
    norm_lon,
    norm_lat,
    w_sem,
    fold_recv,
    fold_send,
    spec_recv,
    spec_send,
    spec_pair,
    norm_recv,
    norm_send,
    own_sem,
):
    batch, rows, width = x_hbm.shape
    halves = width // LANES
    group = lon // halves
    chunks = batch // group
    points = fwd_t.shape[1]
    slab, lats, degrees = raw_ana.shape
    narrow = width // lon
    hidden = mlp_in.shape[1]
    band = lats // lat
    block = 2 * slab * band
    waves = 2 * slab * lat
    my_lat, my_lon = lax.axis_index("lat"), lax.axis_index("lon")
    half_tile = row_tile(rows, 144)
    full_tile = row_tile(rows, 240)

    def lon_copy(stage, chunk, src, dst, peer, member=0):
        return pltpu.make_async_remote_copy(
            src_ref=src,
            dst_ref=dst,
            send_sem=send_sem.at[stage - 1],
            recv_sem=recv_sem.at[stage - 1, chunk, member],
            device_id={"lon": peer},
            device_id_type=MESH,
        )

    def lat_copy(stage, chunk, src, dst, peer):
        return pltpu.make_async_remote_copy(
            src_ref=src,
            dst_ref=dst,
            send_sem=send_sem.at[stage - 1],
            recv_sem=recv_sem.at[stage - 1, chunk, 0],
            device_id={"lat": peer},
            device_id_type=MESH,
        )

    def own_copy(stage, chunk, src, dst):
        return pltpu.make_async_copy(src, dst, recv_sem.at[stage - 1, chunk, 0])

    def landed(stage, chunk, whole, member=0):
        pltpu.make_async_copy(whole, whole, recv_sem.at[stage - 1, chunk, member]).wait()

    def member_at(step):
        return lax.rem(my_lon // halves + step, group)

    def member_landed(stage, chunk, step):
        count = halves if step else halves - 1
        landed(stage, chunk, lon_a.at[chunk, pl.ds(0, count)], member_at(step))

    def sent(stage, part):
        lon_copy(stage, 0, part, part, my_lon).wait_send()

    def x_load(sample):
        return pltpu.make_async_copy(x_hbm.at[sample], x_all.at[sample], x_sem.at[sample])

    def g_load(sample, slot):
        return pltpu.make_async_copy(g_hbm.at[sample], g_buf.at[slot], g_sem.at[slot])

    def o_store(sample, slot):
        return pltpu.make_async_copy(o_buf.at[slot], out_hbm.at[sample], o_sem.at[slot])

    def i_store(sample, slot):
        return pltpu.make_async_copy(i_buf.at[slot], gin_hbm.at[sample], i_sem.at[slot])

    def spread_rows(stage, chunk, held, sample):
        src = chunk * group + sample
        for half in range(halves):
            peer = sample * halves + half

            @pl.when(peer != my_lon)
            def _(peer=peer, half=half):
                lon_copy(stage, chunk, held.at[src, half], lon_a.at[chunk, my_lon], peer).start()

            @pl.when(peer == my_lon)
            def _(half=half):
                own_copy(stage, chunk, held.at[src, half], lon_a.at[chunk, my_lon]).start()

    def spread_bands(stage, chunk, buffer, target):
        for step in range(1, lat):
            peer = lax.rem(my_lat + step, lat)
            lat_copy(stage, chunk, buffer.at[peer], target.at[chunk, my_lat], peer).start()

    def pair(values, factor):
        return jnp.concatenate([values(0), values(1)], axis=1).astype(jnp.bfloat16)

    def to_waves(stage, chunk, table, scale, buffer):
        landed(stage - 1, chunk, lon_a.at[chunk])
        for source in range(lon):
            wide[pl.ds(source * rows, rows), :] = lon_a[chunk, source, pl.ds(0, rows), :].astype(jnp.float32)
        for first in range(0, band, 2):
            rhs = jnp.concatenate(
                [wide[pl.ds(first + k, points, stride=band), :] for k in range(2)], axis=1
            ).astype(jnp.bfloat16)
            got = dot(table[...], rhs)
            if scale is not None:
                got = got * scale
            for k in range(2):
                slim[pl.ds(first + k, waves, stride=band), :] = got[:, k * LANES : (k + 1) * LANES]

        @pl.when(chunk > 0)
        def _():
            sent(stage, buffer.at[pl.ds(0, lat - 1)])

        for target in range(lat):
            buffer[target] = slim[pl.ds(target * block, block), :].astype(jnp.bfloat16)
        spread_bands(stage, chunk, buffer, lat_a)
        own = pl.ds(pl.multiple_of(my_lat * block, 8), block)
        lat_a[chunk, my_lat] = slim[own, :].astype(jnp.bfloat16)

    def to_points(stage, chunk, table, scale, buffer):
        landed(stage - 1, chunk, lat_b.at[chunk, pl.ds(0, lat - 1)])
        for source in range(lat):
            slim[pl.ds(source * block, block), :] = lat_b[chunk, source].astype(jnp.float32)
        for first in range(0, band, 2):
            rhs = jnp.concatenate(
                [slim[pl.ds(first + k, waves, stride=band), :] for k in range(2)], axis=1
            ).astype(jnp.bfloat16)
            got = dot(table[...], rhs)
            if scale is not None:
                got = got * scale
            for k in range(2):
                wide[pl.ds(first + k, points, stride=band), :] = got[:, k * LANES : (k + 1) * LANES]

        @pl.when(chunk > 0)
        def _():
            sent(stage, buffer.at[pl.ds(0, lon - 1)])

        for target in range(lon):
            buffer[target, pl.ds(0, rows), :] = wide[pl.ds(target * rows, rows), :].astype(jnp.bfloat16)
        sample, half = chunk * group + my_lon // halves, lax.rem(my_lon, halves)
        for step in range(1, lon):
            peer = lax.rem(my_lon + step, lon)
            lon_copy(stage, chunk, buffer.at[peer], lon_b.at[sample, half], peer, my_lon // halves).start()
        own = pl.ds(pl.multiple_of(my_lon * rows, 8), rows)
        lon_b[sample, half, pl.ds(0, rows), :] = wide[own, :].astype(jnp.bfloat16)

    def slab_step(stage, chunk, first_table, second_table, between, buffer):
        landed(stage - 1, chunk, lat_a.at[chunk, pl.ds(0, lat - 1)])
        for source in range(lat):
            slim[pl.ds(source * block, block), :] = lat_a[chunk, source].astype(jnp.float32)
        for m in range(slab):
            parts = []
            for r in range(2):
                at = (r * slab + m) * band
                parts.append(
                    jnp.concatenate([slim[pl.ds(s * block + at, band), :] for s in range(lat)], axis=0)
                )
            rhs = jnp.concatenate(parts, axis=1).astype(jnp.bfloat16)
            real, imag = between(m, dot(first_table[m], rhs))
            low = jnp.concatenate([real, imag], axis=1).astype(jnp.bfloat16)
            got = dot(second_table[m], low)
            for r in range(2):
                at = (r * slab + m) * band
                for t in range(lat):
                    wide[pl.ds(t * block + at, band), :] = got[
                        t * band : (t + 1) * band, r * LANES : (r + 1) * LANES
                    ]

        @pl.when(chunk > 0)
        def _():
            sent(stage, buffer.at[pl.ds(0, lat - 1)])

        for target in range(lat):
            buffer[target] = wide[pl.ds(target * block, block), :].astype(jnp.bfloat16)
        spread_bands(stage, chunk, buffer, lat_b)
        own = pl.ds(pl.multiple_of(my_lat * block, 8), block)
        lat_b[chunk, my_lat] = wide[own, :].astype(jnp.bfloat16)

    hidden_rows = width * hidden // LANES
    vector_rows = 2 * hidden_rows + width * width // LANES

    def gather_rows(base, values):
        count = values.shape[0]
        for q in range(values.shape[1] // LANES):
            acc[pl.ds(base + q * count, count), :] += values[:, q * LANES : (q + 1) * LANES]

    def both(held, sample, where):
        return jnp.concatenate([held[sample, h, where, :] for h in range(halves)], axis=1)

    def normalize(sample):
        x_load(sample).wait()

        @pl.loop(0, rows // half_tile)
        def _(i):
            where = pl.ds(pl.multiple_of(i * half_tile, 8), half_tile)
            normal, _ = norm_parts(x_all[sample, where, :].astype(jnp.float32))
            low = (normal * gain_one[...] + bias_one[...]).astype(jnp.bfloat16)
            for h in range(halves):
                normed[sample, h, where, :] = low[:, h * LANES : (h + 1) * LANES]

    def stage_1(chunk):
        @pl.when(chunk > 0)
        def _():
            sent(1, lon_a.at[chunk, pl.ds(0, lon - 1)])

        for step in reversed(range(group)):
            k = member_at(step)

            @pl.when(chunk > 0)
            def _(k=k):
                normalize(chunk * group + k)

            spread_rows(1, chunk, normed, k)

    def stage_2(chunk):
        to_waves(2, chunk, fwd_t, 1.0 / points, send_2)

    def stage_3(chunk):
        def between(m, got):
            coeffs[chunk, m] = got.astype(jnp.bfloat16)
            real, imag = got[:, :LANES], got[:, LANES:]
            return (
                w_real[...] * real - w_imag[...] * imag,
                w_real[...] * imag + w_imag[...] * real,
            )

        slab_step(3, chunk, ana, syn, between, send_3)

    def stage_4(chunk):
        to_points(4, chunk, inv, None, send_4)

    def stage_5a(chunk):
        @pl.when(chunk > 0)
        def _():
            sent(5, lon_a.at[chunk, pl.ds(0, lon - 1)])

        feed_forward(chunk, range(group // 2))

    def stage_5b(chunk):
        feed_forward(chunk, range(group // 2, group))

    def feed_forward(chunk, steps):
        for step in steps:
            member_landed(4, chunk, step)
            k = member_at(step)
            sample = chunk * group + k
            g_load(sample, k).wait()

            @pl.when(chunk > 0)
            def _(sample=sample, k=k):
                o_store(sample, k).wait()

            @pl.loop(0, rows // full_tile)
            def _(i):
                where = pl.ds(pl.multiple_of(i * full_tile, 8), full_tile)
                low_one = both(normed, sample, where)
                spatial = both(lon_b, sample, where).astype(jnp.float32)
                resid = x_all[sample, where, :].astype(jnp.float32) + (spatial + dot(low_one, skip[...]))
                normal, scaled = norm_parts(resid)
                low_two = (normal * gain_two[...] + bias_two[...]).astype(jnp.bfloat16)
                pre = dot(low_two, mlp_in[...]) + bias_in[...]
                square = pre * pre
                curve = jnp.tanh(root * pre * (1.0 + cubic * square))
                lifted = 0.5 + 0.5 * curve
                act = (pre * lifted).astype(jnp.bfloat16)
                slope = lifted + (0.5 * root) * pre * (1.0 - curve * curve) * (1.0 + (3.0 * cubic) * square)
                o_buf[k, where, :] = (resid + dot(act, mlp_out[...]) + bias_out[...]).astype(jnp.bfloat16)
                g_low = g_buf[k, where, :]
                gather_rows(hidden_rows, t_dot(g_low, act))
                grad_pre = (dot_t(g_low, mlp_out[...]) * slope).astype(jnp.bfloat16)
                gather_rows(0, t_dot(low_two, grad_pre))
                gather_rows(vector_rows, fold(grad_pre.astype(jnp.float32)))
                grad_second = dot_t(grad_pre, mlp_in[...])
                g_full = g_low.astype(jnp.float32)
                for at, values in enumerate((g_full, grad_second * normal, grad_second)):
                    gather_rows(vector_rows + 8 * (hidden + at * width) // LANES, fold(values))
                grad_mixed = (g_full + norm_back(grad_second, normal, scaled, gain_two[...])).astype(jnp.bfloat16)
                gather_rows(2 * hidden_rows, t_dot(low_one, grad_mixed))
                for h in range(halves):
                    mixed[sample, h, where, :] = grad_mixed[:, h * LANES : (h + 1) * LANES]

            o_store(sample, k).start()

            @pl.when(chunk < chunks - 1)
            def _(sample=sample, k=k):
                g_load(sample + group, k).start()

            spread_rows(5, chunk, mixed, k)

    def stage_6(chunk):
        to_waves(6, chunk, inv_t, None, send_6)

    def stage_7(chunk):
        def between(m, got):
            dr, di = got[:, :LANES], got[:, LANES:]
            held = coeffs[chunk, m].astype(jnp.float32)
            ar, ai = held[:, :LANES], held[:, LANES:]
            spec[pl.ds(0, degrees), :] += dr * ar + di * ai
            spec[pl.ds(degrees, degrees), :] += di * ar - dr * ai
            return (
                w_real[...] * dr + w_imag[...] * di,
                w_real[...] * di - w_imag[...] * dr,
            )

        slab_step(7, chunk, syn_t, ana_t, between, send_7)

    def stage_8(chunk):
        to_points(8, chunk, fwd, 1.0 / points, send_8)

    def stage_9(chunk):
        for step in range(group):
            member_landed(8, chunk, step)
            k = member_at(step)
            sample = chunk * group + k

            @pl.when(chunk > 0)
            def _(sample=sample, k=k):
                i_store(sample, k).wait()

            @pl.loop(0, rows // half_tile)
            def _(i):
                where = pl.ds(pl.multiple_of(i * half_tile, 8), half_tile)
                normal, scaled = norm_parts(x_all[sample, where, :].astype(jnp.float32))
                low = both(mixed, sample, where)
                grad_normed = dot_t(low, skip[...]) + both(lon_b, sample, where).astype(jnp.float32)
                norm_sums[0] += fold(grad_normed * normal)
                norm_sums[1] += fold(grad_normed)
                i_buf[k, where, :] = low.astype(jnp.float32) + norm_back(
                    grad_normed, normal, scaled, gain_one[...]
                )

            i_store(sample, k).start()

    def weight_copies(start):
        place = lax.rem(my_lon, group)
        held = w_parts.at[:, pl.ds(pl.multiple_of(place * narrow, 8), narrow), :]
        for q in range(group):
            peer = my_lon // group + halves * q

            @pl.when(peer != my_lon)
            def _(peer=peer, q=q):
                copy = pltpu.make_async_remote_copy(
                    src_ref=weight,
                    dst_ref=held,
                    send_sem=w_sem.at[1, q],
                    recv_sem=w_sem.at[0, place],
                    device_id={"lon": peer},
                    device_id_type=MESH,
                )
                if start:
                    copy.start()
                else:
                    copy.wait_send()

            if start:

                @pl.when(peer == my_lon)
                def _():
                    pltpu.make_async_copy(weight, held, w_sem.at[0, place]).start()

    def build():
        acc[...] = jnp.zeros_like(acc)
        spec[...] = jnp.zeros_like(spec)
        norm_sums[...] = jnp.zeros_like(norm_sums)
        norm_own[...] = jnp.zeros_like(norm_own)
        degree = lax.broadcasted_iota(jnp.int32, (lats, degrees), 1)

        @pl.loop(0, slab)
        def _(m):
            kept = degree >= my_lat * slab + m
            for raw, plain, turned in ((raw_ana, ana_t, ana), (raw_syn, syn, syn_t)):
                values = jnp.where(kept, raw[m].astype(jnp.float32), 0.0)
                plain[m] = values.astype(jnp.bfloat16)
                turned[m] = values.T.astype(jnp.bfloat16)

        for q in range(group):
            part = w_parts.at[:, pl.ds(q * narrow, narrow), :]
            pltpu.make_async_copy(part, part, w_sem.at[0, q]).wait()
        w_real[...] = w_parts[0].T
        w_imag[...] = w_parts[1].T

    total_rows = acc.shape[0]
    place_core, place_chip = lax.rem(my_lon, 2), my_lon // 2
    place_near, place_far = lax.rem(my_lat, 2), my_lat // 2
    levels = (
        (2, place_core, part_core, lambda p: {"lon": 2 * place_chip + p}),
        (2, place_near, part_near, lambda p: {"lat": 2 * place_far + p}),
        (lon // 2, place_chip, part_chip, lambda p: {"lon": 2 * p + place_core}),
        (lat // 2, place_far, part_far, lambda p: {"lat": 2 * p + place_near}),
    )
    bases, sizes = [0], [total_rows]
    for count, place, _, _ in levels:
        sizes.append(sizes[-1] // count)
        bases.append(bases[-1] + place * sizes[-1])

    def row_part(at, count):
        return pl.ds(pl.multiple_of(at, 8), count)

    def fold_start(k):
        count, place, parts, device = levels[k]
        for step in range(1, count):
            peer = lax.rem(place + step, count)
            pltpu.make_async_remote_copy(
                src_ref=acc.at[row_part(bases[k] + peer * sizes[k + 1], sizes[k + 1]), :],
                dst_ref=parts.at[step - 1],
                send_sem=fold_send.at[0, k],
                recv_sem=fold_recv.at[0, k],
                device_id=device(peer),
                device_id_type=MESH,
            ).start()

    def fold_end(k):
        count, _, parts, _ = levels[k]
        if count == 1:
            return
        pltpu.make_async_copy(parts, parts, fold_recv.at[0, k]).wait()
        got = parts[0]
        for step in range(2, count):
            got = got + parts[step - 1]
        acc[row_part(bases[k + 1], sizes[k + 1]), :] += got

    def spread_start(k):
        count, place, _, device = levels[k]
        own = row_part(bases[k + 1], sizes[k + 1])
        src = acc if k == len(levels) - 1 else total_hbm
        for step in range(1, count):
            pltpu.make_async_remote_copy(
                src_ref=src.at[own, :],
                dst_ref=total_hbm.at[own, :],
                send_sem=fold_send.at[1, k],
                recv_sem=fold_recv.at[1, k],
                device_id=device(lax.rem(place + step, count)),
                device_id_type=MESH,
            ).start()
        if src is acc:
            pltpu.make_async_copy(acc.at[own, :], total_hbm.at[own, :], own_sem.at[0]).start()

    def spread_end(k):
        count = levels[k][0]
        if count > 1:
            all_parts = total_hbm.at[pl.ds(0, (count - 1) * sizes[k + 1]), :]
            pltpu.make_async_copy(all_parts, all_parts, fold_recv.at[1, k]).wait()
        if k == len(levels) - 1:
            own = row_part(bases[k + 1], sizes[k + 1])
            pltpu.make_async_copy(acc.at[own, :], total_hbm.at[own, :], own_sem.at[0]).wait()

    def fold_sent():
        for k, (count, _, _, _) in enumerate(levels):
            for way in range(2 if count > 1 else 0):
                part = total_hbm if way and k < len(levels) - 1 else acc
                part = part.at[pl.ds(0, (count - 1) * sizes[k + 1]), :]
                pltpu.make_async_remote_copy(
                    src_ref=part,
                    dst_ref=part,
                    send_sem=fold_send.at[way, k],
                    recv_sem=fold_recv.at[way, k],
                    device_id={"lon": my_lon},
                    device_id_type=MESH,
                ).wait_send()

    spec_rows = spec_sum.shape[0]

    def spec_lat_copies(way, src, dst):
        for step in range(1, lat):
            peer = lax.rem(my_lat + step, lat)
            pltpu.make_async_remote_copy(
                src_ref=src(peer),
                dst_ref=dst(step),
                send_sem=spec_send.at[way],
                recv_sem=spec_recv.at[way],
                device_id={"lat": peer},
                device_id_type=MESH,
            ).start()

    def spec_start():
        spec_lat_copies(
            0, lambda p: spec.at[row_part(p * spec_rows, spec_rows), :], lambda s: spec_lat.at[s - 1]
        )

    def spec_pairs(action):
        half = lax.rem(my_lon, halves)
        for q in range(group):
            target = half * group + q

            @pl.when(target != my_lon)
            def _(target=target, q=q):
                copy = pltpu.make_async_remote_copy(
                    src_ref=spec_sum,
                    dst_ref=spec_lon.at[my_lon // halves],
                    send_sem=spec_pair.at[1, q],
                    recv_sem=spec_pair.at[0, my_lon // halves],
                    device_id={"lon": target},
                    device_id_type=MESH,
                )
                if action == "start":
                    copy.start()
                else:
                    copy.wait_send()

            if action == "start":

                @pl.when(target == my_lon)
                def _():
                    pltpu.make_async_copy(
                        spec_sum, spec_lon.at[my_lon // halves], spec_pair.at[0, my_lon // halves]
                    ).start()

    def spec_middle():
        pltpu.make_async_copy(spec_lat, spec_lat, spec_recv.at[0]).wait()
        got = spec[row_part(my_lat * spec_rows, spec_rows), :]
        for step in range(1, lat):
            got = got + spec_lat[step - 1]
        spec_sum[...] = got
        spec_pairs("start")

    def spec_back():
        for q in range(group):
            pltpu.make_async_copy(spec_lon.at[q], spec_lon.at[q], spec_pair.at[0, q]).wait()
        got = spec_lon[0]
        for q in range(1, group):
            got = got + spec_lon[q]
        spec_own[...] = got
        own = row_part(total_rows + my_lat * spec_rows, spec_rows)
        spec_lat_copies(1, lambda p: spec_own, lambda s: total_hbm.at[own, :])
        pltpu.make_async_copy(spec_own, total_hbm.at[own, :], own_sem.at[1]).start()

    def spec_end():
        own = row_part(total_rows + my_lat * spec_rows, spec_rows)
        pltpu.make_async_copy(spec_own, total_hbm.at[own, :], own_sem.at[1]).wait()
        part = spec.at[pl.ds(0, (lat - 1) * spec_rows), :]
        pltpu.make_async_copy(part, part, spec_recv.at[1]).wait()
        for way in range(2):
            pltpu.make_async_remote_copy(
                src_ref=part,
                dst_ref=part,
                send_sem=spec_send.at[way],
                recv_sem=spec_recv.at[way],
                device_id={"lat": my_lat},
                device_id_type=MESH,
            ).wait_send()
        spec_pairs("end")

    def norm_copies(way, axis, count, place, src, parts, action):
        for step in range(1, count):
            copy = pltpu.make_async_remote_copy(
                src_ref=src,
                dst_ref=parts.at[step - 1],
                send_sem=norm_send.at[way, step - 1],
                recv_sem=norm_recv.at[way],
                device_id={axis: lax.rem(place + step, count)},
                device_id_type=MESH,
            )
            if action == "start":
                copy.start()
            else:
                copy.wait_send()

    def norm_fold(way, axis, count, place, src, parts, out):
        norm_copies(way, axis, count, place, src, parts, "start")
        pltpu.make_async_copy(parts, parts, norm_recv.at[way]).wait()
        got = src[...]
        for step in range(1, count):
            got = got + parts[step - 1]
        out[...] = got

    def norm_all():
        for which in range(2):
            line = jnp.sum(norm_sums[which], axis=0, keepdims=True)
            for h in range(halves):
                norm_own[0, pl.ds(which * halves + h, 1), :] = line[:, h * LANES : (h + 1) * LANES]
        norm_fold(0, "lon", lon, my_lon, norm_own.at[0], norm_lon, norm_own.at[1])
        norm_fold(1, "lat", lat, my_lat, norm_own.at[1], norm_lat, norm_own.at[2])
        where = pl.ds(total_rows + lat * spec_rows, 8)
        copy = pltpu.make_async_copy(norm_own.at[2], total_hbm.at[where, :], own_sem.at[2])
        copy.start()
        copy.wait()
        norm_copies(0, "lon", lon, my_lon, norm_own.at[0], norm_lon, "end")
        norm_copies(1, "lat", lat, my_lat, norm_own.at[1], norm_lat, "end")

    def run(*steps):
        def go():
            for step, k in steps:
                step() if k is None else step(k)

        return go

    end = chunks - 1
    aside = {
        (0, "1"): build,
        (end + 5, "5b"): run((fold_start, 0)),
        (end + 5, "9"): run((fold_end, 0), (fold_start, 1)),
        (end + 6, "8"): run((fold_end, 1), (fold_start, 2)),
        (end + 7, "7"): run((fold_end, 2), (fold_start, 3)),
        (end + 7, "9"): run((fold_end, 3), (spread_start, 3)),
        (end + 8, "9"): run((spread_end, 3), (spread_start, 2)),
        (end + 9, "9"): run((spread_end, 2), (spread_start, 1), (spec_middle, None)),
        (end + 10, "9"): run((spread_end, 1), (spread_start, 0)),
        (end + 9, "7"): run((spec_start, None)),
        (end + 10, "8"): run((spec_back, None)),
    }

    stages = {
        "1": stage_1,
        "2": stage_2,
        "3": stage_3,
        "4": stage_4,
        "5a": stage_5a,
        "5b": stage_5b,
        "6": stage_6,
        "7": stage_7,
        "8": stage_8,
        "9": stage_9,
    }

    for sample in range(group):
        x_load(sample).start()

    padded = lon_a.shape[2]
    if padded > rows:
        for held in (normed, mixed):
            held[:, :, rows:, :] = jnp.zeros_like(held[:, :, rows:, :])
        for held in (send_4, send_8):
            held[:, rows:, :] = jnp.zeros_like(held[:, rows:, :])
    barrier = pltpu.get_barrier_semaphore()
    for step in range(1, lon):
        pl.semaphore_signal(
            barrier, inc=1, device_id={"lon": lax.rem(my_lon + step, lon)}, device_id_type=MESH
        )
    for step in range(1, lat):
        pl.semaphore_signal(
            barrier, inc=1, device_id={"lat": lax.rem(my_lat + step, lat)}, device_id_type=MESH
        )
    for k in range(group):
        normalize(k)
    for sample in range(group, batch):
        x_load(sample).start()
    for k in range(group):
        g_load(k, k).start()
    pl.semaphore_wait(barrier, lon - 1 + lat - 1)

    weight_copies(True)

    def tick(now, carry):
        for stage in ORDER:
            chunk = now - OFFSET[stage]

            @pl.when(jnp.logical_and(chunk >= 0, chunk < chunks))
            def _(stage=stage, chunk=chunk):
                stages[stage](chunk)

            for (when, after), action in aside.items():
                if after == stage:
                    pl.when(now == when)(action)

        return carry

    lax.fori_loop(0, chunks + max(OFFSET.values()), tick, 0)

    norm_all()
    spread_end(0)
    spec_end()
    fold_sent()
    weight_copies(False)
    last = chunks - 1
    for stage in (1, 5):
        sent(stage, lon_a.at[last, pl.ds(0, lon - 1)])
    for stage, buffer, count in (
        (2, send_2, lat - 1),
        (3, send_3, lat - 1),
        (4, send_4, lon - 1),
        (6, send_6, lat - 1),
        (7, send_7, lat - 1),
        (8, send_8, lon - 1),
    ):
        sent(stage, buffer.at[pl.ds(0, count)])
    for k in range(group):
        o_store(last * group + k, k).wait()
        i_store(last * group + k, k).wait()


def result_kernel(
    group,
    narrow,
    spec_at,
    norm_at,
    out_from,
    gin_from,
    total,
    out_to,
    gin_to,
    grad_spec,
    grad_skip,
    grad_in,
    grad_out,
    in_bias,
    vectors,
    gin_held,
    out_held,
    sems,
):
    batch = out_from.shape[0]
    width, hidden = grad_in.shape
    halves = width // LANES
    degrees = grad_spec.shape[2]

    def reads(sample):
        return (
            pltpu.make_async_copy(gin_from.at[sample], gin_held.at[sample], sems.at[0, sample]),
            pltpu.make_async_copy(out_from.at[sample], out_held.at[sample], sems.at[1, sample]),
        )

    def writes(sample):
        return (
            pltpu.make_async_copy(gin_held.at[sample], gin_to.at[sample], sems.at[2, sample]),
            pltpu.make_async_copy(out_held.at[sample], out_to.at[sample], sems.at[3, sample]),
        )

    for sample in range(batch):
        for copy in reads(sample):
            copy.start()
    for sample in range(batch):
        for read, write in zip(reads(sample), writes(sample)):
            read.wait()
            write.start()

    def tile(base, height, q):
        return total[pl.ds(base + q * height, height), :]

    hidden_rows = width * hidden // LANES
    vector_rows = 2 * hidden_rows + width * width // LANES
    for q in range(hidden // LANES):
        where = pl.ds(q * LANES, LANES)
        grad_in[:, where] = tile(0, width, q)
        grad_out[where, :] = tile(hidden_rows, width, q).T
        in_bias[:, where] = jnp.sum(tile(vector_rows, 8, q), axis=0, keepdims=True)
    for q in range(halves):
        where = pl.ds(q * LANES, LANES)
        grad_skip[:, where] = tile(2 * hidden_rows, width, q)
        for which in range(3):
            at = vector_rows + 8 * (hidden + which * width) // LANES
            vectors[which, :, where] = jnp.sum(tile(at, 8, q), axis=0, keepdims=True)
        for which in range(2):
            vectors[3 + which, :, where] = total[pl.ds(norm_at + which * halves + q, 1), :]
    place = lax.rem(lax.axis_index("lon"), group)
    for which in range(2):
        turned = total[pl.ds(spec_at + which * degrees, degrees), :].T
        for q in range(group):

            @pl.when(place == q)
            def _(q=q, which=which, turned=turned):
                grad_spec[which] = turned[q * narrow : (q + 1) * narrow, :]

    for sample in range(batch):
        for write in writes(sample):
            write.wait()


def per_device(
    tables,
    lat,
    lon,
    inputs,
    legendre_forward,
    legendre_inverse,
    spectral_weight,
    skip_weight,
    gain_first,
    bias_first,
    gain_second,
    bias_second,
    mlp_in,
    mlp_in_bias,
    mlp_out,
    mlp_out_bias,
    cotangent,
):
    batch, band, columns, width = inputs.shape
    points = columns * lon
    slab, degrees, lats = legendre_forward.shape
    orders = slab * lat
    hidden = mlp_in.shape[1]
    rows = columns * band
    padded = -(-rows // 16) * 16
    halves = width // LANES
    group = lon // halves
    chunks = batch // group
    block = 2 * slab * band
    waves = 2 * orders

    forward, inverse = tables(points, lat)(orders)
    my_lon = lax.axis_index("lon")
    hidden = mlp_in.shape[1]
    flat_rows = (2 * hidden + width) * width // LANES + 8 * (hidden + 3 * width) // LANES
    share = -(-flat_rows // (8 * lat * lon)) * 8
    total_rows = share * lat * lon
    spec_rows = -(-2 * degrees // (8 * lat)) * 8

    def flat(values):
        return values.transpose(0, 2, 1, 3).reshape(batch, rows, width)

    def row(values):
        return values.reshape(1, -1)

    vmem = pl.BlockSpec(memory_space=pltpu.VMEM)
    hbm = pl.BlockSpec(memory_space=pl.ANY)
    fixed = pl.BlockSpec(memory_space=pltpu.HBM)
    low, full = jnp.bfloat16, jnp.float32
    results = pl.pallas_call(
        functools.partial(block_kernel, lat, lon),
        out_shape=(
            jax.ShapeDtypeStruct((batch, rows, width), low),
            jax.ShapeDtypeStruct((batch, rows, width), full),
            jax.ShapeDtypeStruct((total_rows + lat * spec_rows + 8, LANES), full),
        ),
        in_specs=[hbm, hbm] + [vmem] * 16,
        out_specs=(hbm, hbm, hbm),
        scratch_shapes=[
            pltpu.VMEM((batch, rows, width), low),
            pltpu.VMEM((batch, halves, padded, LANES), low),
            pltpu.VMEM((batch, halves, padded, LANES), low),
            pltpu.VMEM((chunks, lon, padded, LANES), low),
            pltpu.VMEM((batch, halves, padded, LANES), low),
            pltpu.VMEM((chunks, lat, block, LANES), low),
            pltpu.VMEM((chunks, lat, block, LANES), low),
            pltpu.VMEM((chunks, slab, degrees, 2 * LANES), low),
            pltpu.VMEM((lat, block, LANES), low),
            pltpu.VMEM((lat, block, LANES), low),
            pltpu.VMEM((lon, padded, LANES), low),
            pltpu.VMEM((lat, block, LANES), low),
            pltpu.VMEM((lat, block, LANES), low),
            pltpu.VMEM((lon, padded, LANES), low),
            pltpu.VMEM((max(points, waves) * band, LANES), full),
            pltpu.VMEM((waves * band, LANES), full),
            pltpu.VMEM((group, rows, width), low),
            pltpu.VMEM((group, rows, width), low),
            pltpu.VMEM((group, rows, width), full),
            pltpu.SemaphoreType.DMA((8, chunks, group)),
            pltpu.SemaphoreType.DMA((8,)),
            pltpu.SemaphoreType.DMA((batch,)),
            pltpu.SemaphoreType.DMA((group,)),
            pltpu.SemaphoreType.DMA((group,)),
            pltpu.SemaphoreType.DMA((group,)),
            pltpu.VMEM((slab, degrees, lats), low),
            pltpu.VMEM((slab, lats, degrees), low),
            pltpu.VMEM((slab, lats, degrees), low),
            pltpu.VMEM((slab, degrees, lats), low),
            pltpu.VMEM((2, LANES, degrees), full),
            pltpu.VMEM((degrees, LANES), full),
            pltpu.VMEM((degrees, LANES), full),
            pltpu.VMEM((total_rows, LANES), full),
            pltpu.VMEM((1, total_rows // 2, LANES), full),
            pltpu.VMEM((1, total_rows // 4, LANES), full),
            pltpu.VMEM((max(lon // 2 - 1, 1), total_rows // (2 * lon), LANES), full),
            pltpu.VMEM((max(lat // 2 - 1, 1), share, LANES), full),
            pltpu.VMEM((lat * spec_rows, LANES), full),
            pltpu.VMEM((lat - 1, spec_rows, LANES), full),
            pltpu.VMEM((group, spec_rows, LANES), full),
            pltpu.VMEM((spec_rows, LANES), full),
            pltpu.VMEM((spec_rows, LANES), full),
            pltpu.VMEM((2, 8, width), full),
            pltpu.VMEM((3, 8, LANES), full),
            pltpu.VMEM((lon - 1, 8, LANES), full),
            pltpu.VMEM((lat - 1, 8, LANES), full),
            pltpu.SemaphoreType.DMA((2, group)),
            pltpu.SemaphoreType.DMA((2, 4)),
            pltpu.SemaphoreType.DMA((2, 4)),
            pltpu.SemaphoreType.DMA((2,)),
            pltpu.SemaphoreType.DMA((2,)),
            pltpu.SemaphoreType.DMA((2, group)),
            pltpu.SemaphoreType.DMA((2,)),
            pltpu.SemaphoreType.DMA((2, max(lat, lon) - 1)),
            pltpu.SemaphoreType.DMA((3,)),
        ],
        compiler_params=pltpu.CompilerParams(
            collective_id=0, has_side_effects=True, vmem_limit_bytes=63 * 2**20
        ),
    )(
        flat(inputs),
        flat(cotangent),
        jnp.asarray(forward),
        jnp.asarray(inverse),
        jnp.asarray(inverse.T),
        jnp.asarray(forward.T),
        legendre_forward.transpose(0, 2, 1),
        legendre_inverse,
        spectral_weight.transpose(0, 2, 1),
        skip_weight,
        mlp_in,
        mlp_out,
        row(gain_first),
        row(bias_first),
        row(gain_second),
        row(bias_second),
        row(mlp_in_bias),
        row(mlp_out_bias),
    )
    shapes = (
        ((batch, rows, width), low),
        ((batch, rows, width), full),
        ((2, width // lon, degrees), full),
        ((width, width), full),
        ((width, hidden), full),
        ((hidden, width), full),
        ((1, hidden), full),
        ((5, 1, width), full),
    )
    output, grad_inputs, grad_spec, grad_skip, grad_in, grad_out, in_bias, vectors = pl.pallas_call(
        functools.partial(result_kernel, group, width // lon, total_rows, total_rows + lat * spec_rows),
        out_shape=tuple(jax.ShapeDtypeStruct(*shape) for shape in shapes),
        in_specs=[fixed, fixed, vmem],
        out_specs=(fixed, fixed) + (vmem,) * 6,
        scratch_shapes=[
            pltpu.VMEM((batch, rows, width), full),
            pltpu.VMEM((batch, rows, width), low),
            pltpu.SemaphoreType.DMA((4, batch)),
        ],
        compiler_params=pltpu.CompilerParams(vmem_limit_bytes=48 * 2**20),
    )(*results)

    def unflat(values):
        return values.reshape(batch, columns, band, width).transpose(0, 2, 1, 3)

    return (
        unflat(output),
        unflat(grad_inputs),
        grad_spec.transpose(0, 2, 1),
        grad_skip,
        vectors[3, 0],
        vectors[4, 0],
        vectors[1, 0],
        vectors[2, 0],
        grad_in,
        in_bias[0],
        grad_out,
        vectors[0, 0],
    )


def solution(mesh):
    lat, lon = mesh.shape["lat"], mesh.shape["lon"]
    grid = P(None, "lat", "lon", None)
    table = P("lat", None, None)
    channel = P(None, None, "lon")
    return jax.shard_map(
        functools.partial(per_device, fourier_tables, lat, lon),
        mesh=mesh,
        in_specs=(grid, table, table, channel) + (P(),) * 9 + (grid,),
        out_specs=(grid, grid, channel) + (P(),) * 9,
        check_vma=False,
    )
```

```python
import functools
import math

import jax
import jax.numpy as jnp
import ml_dtypes
import numpy as np
from jax import lax
from jax.experimental import pallas as pl
from jax.experimental.pallas import tpu as pltpu
from jax.sharding import PartitionSpec as P

epsilon = 1e-05
LANES = 128
MESH = pl.DeviceIdType.MESH
root = math.sqrt(2.0 / math.pi)
cubic = 0.044715

OFFSET = {"1": 0, "2": 1, "3": 3, "4": 4, "5a": 5, "5b": 5, "6": 7, "7": 9, "8": 10, "9": 11}
ORDER = ("1", "3", "7", "4", "5a", "6", "2", "5b", "8", "9")


def fourier_tables(points, lat):
    def build(orders):
        waves = np.arange(orders)
        phase = (waves[:, None] * np.arange(points)[None, :] % points).astype(np.float32)
        phase = phase * np.float32(2.0 * math.pi / points)
        cosine, sine = np.cos(phase), np.sin(phase)
        factor = np.where(waves == 0, 1.0, 2.0).astype(np.float32)[:, None]
        slab = orders // lat

        def arrange(parts):
            stacked = np.stack(parts).reshape(2, lat, slab, points).transpose(1, 0, 2, 3)
            return stacked.reshape(2 * orders, points).astype(ml_dtypes.bfloat16)

        forward = arrange([cosine, -sine])
        inverse = arrange([factor * cosine, -factor * sine])
        return forward, inverse

    return build


def row_tile(rows, most):
    fits = [t for t in range(16, most + 1, 16) if rows % t == 0]
    return fits[-1] if fits else rows


def norm_parts(values):
    center = values - jnp.mean(values, axis=-1, keepdims=True)
    spread = jnp.mean(center * center, axis=-1, keepdims=True)
    scaled = lax.rsqrt(spread + epsilon)
    return center * scaled, scaled


def norm_back(grad_out, normal, scaled, gain):
    grad_norm = grad_out * gain
    inner = jnp.mean(grad_norm, axis=-1, keepdims=True)
    cross = jnp.mean(grad_norm * normal, axis=-1, keepdims=True)
    return scaled * (grad_norm - inner - normal * cross)


def norm_step(values, mixed, sent, skip, gain):
    normal, scaled = norm_parts(values.astype(jnp.float32))
    grad_normed = dot_t(mixed, skip) + sent.astype(jnp.float32)
    return mixed.astype(jnp.float32) + norm_back(grad_normed, normal, scaled, gain)


def fold(values):
    rows, width = values.shape
    return jnp.sum(values.reshape(rows // 8, 8, width), axis=0)


def dot(a, b):
    return jnp.dot(a, b, preferred_element_type=jnp.float32)


def dot_t(a, b):
    return lax.dot_general(a, b, (((1,), (1,)), ((), ())), preferred_element_type=jnp.float32)


def t_dot(a, b):
    return lax.dot_general(a, b, (((0,), (0,)), ((), ())), preferred_element_type=jnp.float32)


def block_kernel(
    lat,
    lon,
    x_hbm,
    g_hbm,
    fwd_t,
    inv_t,
    inv,
    fwd,
    raw_ana,
    raw_syn,
    weight,
    skip,
    mlp_in,
    mlp_out,
    gain_one,
    bias_one,
    gain_two,
    bias_two,
    bias_in,
    bias_out,
    out_hbm,
    gin_hbm,
    total_hbm,
    small_hbm,
    last_mixed,
    last_grid,
    x_all,
    normed,
    mixed,
    lon_a,
    lon_c,
    lon_b,
    lat_a,
    lat_b,
    coeffs,
    send_2,
    send_3,
    send_4,
    send_6,
    send_7,
    send_8,
    wide,
    slim,
    g_buf,
    o_buf,
    i_buf,
    recv_sem,
    send_sem,
    x_sem,
    g_sem,
    o_sem,
    i_sem,
    ana,
    ana_t,
    syn,
    syn_t,
    w_parts,
    w_real,
    w_imag,
    acc,
    part_core,
    part_near,
    part_chip,
    part_far,
    wire_chip,
    wire_far,
    share,
    spec,
    spec_lat,
    spec_lon,
    spec_sum,
    spec_own,
    norm_sums,
    mixed_sums,
    norm_own,
    norm_lon,
    norm_lat,
    w_sem,
    fold_recv,
    fold_send,
    spec_recv,
    spec_send,
    spec_pair,
    norm_recv,
    norm_send,
    own_sem,
):
    batch, rows, width = x_hbm.shape
    halves = width // LANES
    group = lon // halves
    chunks = batch // group
    points = fwd_t.shape[1]
    slab, lats, degrees = raw_ana.shape
    narrow = width // lon
    hidden = mlp_in.shape[1]
    band = lats // lat
    block = 2 * slab * band
    waves = 2 * slab * lat
    my_lat, my_lon = lax.axis_index("lat"), lax.axis_index("lon")
    half_tile = row_tile(rows, 144)
    full_tile = row_tile(rows, 240)

    def lon_copy(stage, chunk, src, dst, peer, member=0):
        return pltpu.make_async_remote_copy(
            src_ref=src,
            dst_ref=dst,
            send_sem=send_sem.at[stage - 1],
            recv_sem=recv_sem.at[stage - 1, chunk, member],
            device_id={"lon": peer},
            device_id_type=MESH,
        )

    def lat_copy(stage, chunk, src, dst, peer):
        return pltpu.make_async_remote_copy(
            src_ref=src,
            dst_ref=dst,
            send_sem=send_sem.at[stage - 1],
            recv_sem=recv_sem.at[stage - 1, chunk, 0],
            device_id={"lat": peer},
            device_id_type=MESH,
        )

    def own_copy(stage, chunk, src, dst):
        return pltpu.make_async_copy(src, dst, recv_sem.at[stage - 1, chunk, 0])

    def landed(stage, chunk, whole, member=0):
        pltpu.make_async_copy(whole, whole, recv_sem.at[stage - 1, chunk, member]).wait()

    def member_at(step):
        return lax.rem(my_lon // halves + step, group)

    def member_landed(stage, chunk, step):
        count = halves if step else halves - 1
        landed(stage, chunk, lon_a.at[chunk, pl.ds(0, count)], member_at(step))

    def sent(stage, part):
        lon_copy(stage, 0, part, part, my_lon).wait_send()

    def x_load(sample):
        return pltpu.make_async_copy(x_hbm.at[sample], x_all.at[sample], x_sem.at[sample])

    def g_load(sample, slot):
        return pltpu.make_async_copy(g_hbm.at[sample], g_buf.at[slot], g_sem.at[slot])

    def o_store(sample, slot):
        return pltpu.make_async_copy(o_buf.at[slot], out_hbm.at[sample], o_sem.at[slot])

    def i_store(sample, slot):
        return pltpu.make_async_copy(i_buf.at[slot], gin_hbm.at[sample], i_sem.at[slot])

    def spread_rows(stage, chunk, held, sample, landing):
        src = chunk * group + sample
        for half in range(halves):
            peer = sample * halves + half

            @pl.when(peer != my_lon)
            def _(peer=peer, half=half):
                lon_copy(stage, chunk, held.at[src, half], landing.at[chunk, my_lon], peer).start()

            @pl.when(peer == my_lon)
            def _(half=half):
                own_copy(stage, chunk, held.at[src, half], landing.at[chunk, my_lon]).start()

    def spread_bands(stage, chunk, buffer, target):
        for step in range(1, lat):
            peer = lax.rem(my_lat + step, lat)
            lat_copy(stage, chunk, buffer.at[peer], target.at[chunk, my_lat], peer).start()

    def pair(values, factor):
        return jnp.concatenate([values(0), values(1)], axis=1).astype(jnp.bfloat16)

    def to_waves(stage, chunk, table, scale, buffer, landing):
        landed(stage - 1, chunk, landing.at[chunk])
        for source in range(lon):
            wide[pl.ds(source * rows, rows), :] = landing[chunk, source, pl.ds(0, rows), :].astype(jnp.float32)
        for first in range(0, band, 2):
            rhs = jnp.concatenate(
                [wide[pl.ds(first + k, points, stride=band), :] for k in range(2)], axis=1
            ).astype(jnp.bfloat16)
            got = dot(table[...], rhs)
            if scale is not None:
                got = got * scale
            for k in range(2):
                slim[pl.ds(first + k, waves, stride=band), :] = got[:, k * LANES : (k + 1) * LANES]

        @pl.when(chunk > 0)
        def _():
            sent(stage, buffer.at[pl.ds(0, lat - 1)])

        for target in range(lat):
            buffer[target] = slim[pl.ds(target * block, block), :].astype(jnp.bfloat16)
        spread_bands(stage, chunk, buffer, lat_a)
        own = pl.ds(pl.multiple_of(my_lat * block, 8), block)
        lat_a[chunk, my_lat] = slim[own, :].astype(jnp.bfloat16)

    def to_points(stage, chunk, table, scale, buffer):
        landed(stage - 1, chunk, lat_b.at[chunk, pl.ds(0, lat - 1)])
        for source in range(lat):
            slim[pl.ds(source * block, block), :] = lat_b[chunk, source].astype(jnp.float32)
        for first in range(0, band, 2):
            rhs = jnp.concatenate(
                [slim[pl.ds(first + k, waves, stride=band), :] for k in range(2)], axis=1
            ).astype(jnp.bfloat16)
            got = dot(table[...], rhs)
            if scale is not None:
                got = got * scale
            for k in range(2):
                wide[pl.ds(first + k, points, stride=band), :] = got[:, k * LANES : (k + 1) * LANES]

        @pl.when(chunk > 0)
        def _():
            sent(stage, buffer.at[pl.ds(0, lon - 1)])

        for target in range(lon):
            grid = wide[pl.ds(target * rows, rows), :]
            buffer[target, pl.ds(0, rows), :] = grid.astype(jnp.bfloat16)
            if stage == 8:
                before = lon_a[chunk, target, pl.ds(0, rows), :].astype(jnp.float32)
                norm_sums[0] += fold(grid * before)
                norm_sums[1] += fold(grid)
        member, half = my_lon // halves, lax.rem(my_lon, halves)

        def send(landing):
            for step in range(1, lon):
                peer = lax.rem(my_lon + step, lon)
                lon_copy(stage, chunk, buffer.at[peer], landing, peer, member).start()

        def send_here():
            send(lon_b.at[chunk * group + member, half])
            own = pl.ds(pl.multiple_of(my_lon * rows, 8), rows)
            lon_b[chunk * group + member, half, pl.ds(0, rows), :] = wide[own, :].astype(jnp.bfloat16)

        if stage == 4:
            send_here()
        else:
            pl.when(chunk < chunks - 1)(send_here)

            @pl.when(chunk == chunks - 1)
            def _():
                norm_start()
                send(last_grid.at[member, half])
                last_own().start()

    def last_own():
        held = last_grid.at[my_lon // halves, lax.rem(my_lon, halves)]
        return pltpu.make_async_copy(send_8.at[my_lon], held, own_sem.at[3])

    def last_mixed_copy():
        part = mixed.at[pl.ds((chunks - 1) * group, group)]
        return pltpu.make_async_copy(part, last_mixed, own_sem.at[4])

    def slab_step(stage, chunk, first_table, second_table, between, buffer):
        landed(stage - 1, chunk, lat_a.at[chunk, pl.ds(0, lat - 1)])
        for source in range(lat):
            slim[pl.ds(source * block, block), :] = lat_a[chunk, source].astype(jnp.float32)
        for m in range(slab):
            parts = []
            for r in range(2):
                at = (r * slab + m) * band
                parts.append(
                    jnp.concatenate([slim[pl.ds(s * block + at, band), :] for s in range(lat)], axis=0)
                )
            rhs = jnp.concatenate(parts, axis=1).astype(jnp.bfloat16)
            real, imag = between(m, dot(first_table[m], rhs))
            low = jnp.concatenate([real, imag], axis=1).astype(jnp.bfloat16)
            got = dot(second_table[m], low)
            for r in range(2):
                at = (r * slab + m) * band
                for t in range(lat):
                    wide[pl.ds(t * block + at, band), :] = got[
                        t * band : (t + 1) * band, r * LANES : (r + 1) * LANES
                    ]

        @pl.when(chunk > 0)
        def _():
            sent(stage, buffer.at[pl.ds(0, lat - 1)])

        for target in range(lat):
            buffer[target] = wide[pl.ds(target * block, block), :].astype(jnp.bfloat16)
        spread_bands(stage, chunk, buffer, lat_b)
        own = pl.ds(pl.multiple_of(my_lat * block, 8), block)
        lat_b[chunk, my_lat] = wide[own, :].astype(jnp.bfloat16)

    hidden_rows = width * hidden // LANES
    vector_rows = 2 * hidden_rows + width * width // LANES

    def gather_rows(base, values):
        count = values.shape[0]
        for q in range(values.shape[1] // LANES):
            acc[pl.ds(base + q * count, count), :] += values[:, q * LANES : (q + 1) * LANES]

    def both(held, sample, where):
        return jnp.concatenate([held[sample, h, where, :] for h in range(halves)], axis=1)

    def normalize(sample):
        x_load(sample).wait()

        @pl.loop(0, rows // half_tile)
        def _(i):
            where = pl.ds(pl.multiple_of(i * half_tile, 8), half_tile)
            normal, _ = norm_parts(x_all[sample, where, :].astype(jnp.float32))
            low = (normal * gain_one[...] + bias_one[...]).astype(jnp.bfloat16)
            for h in range(halves):
                normed[sample, h, where, :] = low[:, h * LANES : (h + 1) * LANES]

    def stage_1(chunk):
        @pl.when(chunk > 0)
        def _():
            sent(1, lon_a.at[chunk, pl.ds(0, lon - 1)])

        for step in reversed(range(group)):
            k = member_at(step)

            @pl.when(chunk > 0)
            def _(k=k):
                normalize(chunk * group + k)

            spread_rows(1, chunk, normed, k, lon_a)

    def stage_2(chunk):
        to_waves(2, chunk, fwd_t, 1.0 / points, send_2, lon_a)

    def stage_3(chunk):
        def between(m, got):
            coeffs[chunk, m] = got.astype(jnp.bfloat16)
            real, imag = got[:, :LANES], got[:, LANES:]
            return (
                w_real[...] * real - w_imag[...] * imag,
                w_real[...] * imag + w_imag[...] * real,
            )

        slab_step(3, chunk, ana, syn, between, send_3)

    def stage_4(chunk):
        to_points(4, chunk, inv, None, send_4)

    def stage_5a(chunk):
        @pl.when(chunk > 0)
        def _():
            sent(5, lon_a.at[chunk, pl.ds(0, lon - 1)])

        feed_forward(chunk, range(group // 2))

    def stage_5b(chunk):
        feed_forward(chunk, range(group // 2, group))

    def feed_forward(chunk, steps):
        for step in steps:
            member_landed(4, chunk, step)
            k = member_at(step)
            sample = chunk * group + k
            g_load(sample, k).wait()

            @pl.when(chunk > 0)
            def _(sample=sample, k=k):
                o_store(sample, k).wait()

            @pl.loop(0, rows // full_tile)
            def _(i):
                where = pl.ds(pl.multiple_of(i * full_tile, 8), full_tile)
                low_one = both(normed, sample, where)
                spatial = both(lon_b, sample, where).astype(jnp.float32)
                resid = x_all[sample, where, :].astype(jnp.float32) + (spatial + dot(low_one, skip[...]))
                normal, scaled = norm_parts(resid)
                low_two = (normal * gain_two[...] + bias_two[...]).astype(jnp.bfloat16)
                pre = dot(low_two, mlp_in[...]) + bias_in[...]
                square = pre * pre
                curve = jnp.tanh(root * pre * (1.0 + cubic * square))
                lifted = 0.5 + 0.5 * curve
                act = (pre * lifted).astype(jnp.bfloat16)
                slope = lifted + (0.5 * root) * pre * (1.0 - curve * curve) * (1.0 + (3.0 * cubic) * square)
                o_buf[k, where, :] = (resid + dot(act, mlp_out[...]) + bias_out[...]).astype(jnp.bfloat16)
                g_low = g_buf[k, where, :]
                gather_rows(hidden_rows, t_dot(g_low, act))
                grad_pre = (dot_t(g_low, mlp_out[...]) * slope).astype(jnp.bfloat16)
                gather_rows(0, t_dot(low_two, grad_pre))
                gather_rows(vector_rows, fold(grad_pre.astype(jnp.float32)))
                grad_second = dot_t(grad_pre, mlp_in[...])
                g_full = g_low.astype(jnp.float32)
                for at, values in enumerate((g_full, grad_second * normal, grad_second)):
                    gather_rows(vector_rows + 8 * (hidden + at * width) // LANES, fold(values))
                grad_mixed = (g_full + norm_back(grad_second, normal, scaled, gain_two[...])).astype(jnp.bfloat16)
                gather_rows(2 * hidden_rows, t_dot(low_one, grad_mixed))
                mixed_sums[...] += fold(grad_mixed.astype(jnp.float32))
                for h in range(halves):
                    mixed[sample, h, where, :] = grad_mixed[:, h * LANES : (h + 1) * LANES]

            o_store(sample, k).start()

            @pl.when(chunk < chunks - 1)
            def _(sample=sample, k=k):
                g_load(sample + group, k).start()

            spread_rows(5, chunk, mixed, k, lon_c)

    def stage_6(chunk):
        to_waves(6, chunk, inv_t, None, send_6, lon_c)

    def stage_7(chunk):
        def between(m, got):
            dr, di = got[:, :LANES], got[:, LANES:]
            held = coeffs[chunk, m].astype(jnp.float32)
            ar, ai = held[:, :LANES], held[:, LANES:]
            spec[pl.ds(0, degrees), :] += dr * ar + di * ai
            spec[pl.ds(degrees, degrees), :] += di * ar - dr * ai
            return (
                w_real[...] * dr + w_imag[...] * di,
                w_real[...] * di - w_imag[...] * dr,
            )

        slab_step(7, chunk, syn_t, ana_t, between, send_7)

    def stage_8(chunk):
        to_points(8, chunk, fwd, 1.0 / points, send_8)

    def stage_9(chunk):
        for step in range(group):
            member_landed(8, chunk, step)
            k = member_at(step)
            sample = chunk * group + k

            @pl.when(chunk > 0)
            def _(sample=sample, k=k):
                i_store(sample, k).wait()

            @pl.loop(0, rows // half_tile)
            def _(i):
                where = pl.ds(pl.multiple_of(i * half_tile, 8), half_tile)
                i_buf[k, where, :] = norm_step(
                    x_all[sample, where, :],
                    both(mixed, sample, where),
                    both(lon_b, sample, where),
                    skip[...],
                    gain_one[...],
                )

            i_store(sample, k).start()

    def weight_copies(start):
        place = lax.rem(my_lon, group)
        held = w_parts.at[:, pl.ds(pl.multiple_of(place * narrow, 8), narrow), :]
        for q in range(group):
            peer = my_lon // group + halves * q

            @pl.when(peer != my_lon)
            def _(peer=peer, q=q):
                copy = pltpu.make_async_remote_copy(
                    src_ref=weight,
                    dst_ref=held,
                    send_sem=w_sem.at[1, q],
                    recv_sem=w_sem.at[0, place],
                    device_id={"lon": peer},
                    device_id_type=MESH,
                )
                if start:
                    copy.start()
                else:
                    copy.wait_send()

            if start:

                @pl.when(peer == my_lon)
                def _():
                    pltpu.make_async_copy(weight, held, w_sem.at[0, place]).start()

    def build():
        acc[...] = jnp.zeros_like(acc)
        spec[...] = jnp.zeros_like(spec)
        norm_sums[...] = jnp.zeros_like(norm_sums)
        mixed_sums[...] = jnp.zeros_like(mixed_sums)
        norm_own[...] = jnp.zeros_like(norm_own)
        degree = lax.broadcasted_iota(jnp.int32, (lats, degrees), 1)

        @pl.loop(0, slab)
        def _(m):
            kept = degree >= my_lat * slab + m
            for raw, plain, turned in ((raw_ana, ana_t, ana), (raw_syn, syn, syn_t)):
                values = jnp.where(kept, raw[m].astype(jnp.float32), 0.0)
                plain[m] = values.astype(jnp.bfloat16)
                turned[m] = values.T.astype(jnp.bfloat16)

        for q in range(group):
            part = w_parts.at[:, pl.ds(q * narrow, narrow), :]
            pltpu.make_async_copy(part, part, w_sem.at[0, q]).wait()
        w_real[...] = w_parts[0].T
        w_imag[...] = w_parts[1].T

    total_rows = acc.shape[0]
    place_core, place_chip = lax.rem(my_lon, 2), my_lon // 2
    place_near, place_far = lax.rem(my_lat, 2), my_lat // 2
    levels = (
        (2, place_core, part_core, None, lambda p: {"lon": 2 * place_chip + p}),
        (2, place_near, part_near, None, lambda p: {"lat": 2 * place_far + p}),
        (lon // 2, place_chip, part_chip, wire_chip, lambda p: {"lon": 2 * p + place_core}),
        (lat // 2, place_far, part_far, wire_far, lambda p: {"lat": 2 * p + place_near}),
    )
    bases, sizes = [0], [total_rows]
    for count, place, _, _, _ in levels:
        sizes.append(sizes[-1] // count)
        bases.append(bases[-1] + place * sizes[-1])

    def row_part(at, count):
        return pl.ds(pl.multiple_of(at, 16), count)

    def fold_start(k):
        count, place, parts, wire, device = levels[k]
        if wire is not None:
            wire[...] = acc[row_part(bases[k], sizes[k]), :].astype(jnp.bfloat16)
        for step in range(1, count):
            peer = lax.rem(place + step, count)
            if wire is None:
                src = acc.at[row_part(bases[k] + peer * sizes[k + 1], sizes[k + 1]), :]
            else:
                src = wire.at[row_part(peer * sizes[k + 1], sizes[k + 1]), :]
            pltpu.make_async_remote_copy(
                src_ref=src,
                dst_ref=parts.at[step - 1],
                send_sem=fold_send.at[0, k],
                recv_sem=fold_recv.at[0, k],
                device_id=device(peer),
                device_id_type=MESH,
            ).start()

    def fold_end(k):
        count, _, parts, _, _ = levels[k]
        if count == 1:
            return
        pltpu.make_async_copy(parts, parts, fold_recv.at[0, k]).wait()
        got = parts[0].astype(jnp.float32)
        for step in range(2, count):
            got = got + parts[step - 1].astype(jnp.float32)
        acc[row_part(bases[k + 1], sizes[k + 1]), :] += got

    def spread_start(k):
        count, place, _, _, device = levels[k]
        own = row_part(bases[k + 1], sizes[k + 1])
        src = total_hbm.at[own, :]
        if k == len(levels) - 1:
            share[...] = acc[own, :].astype(jnp.bfloat16)
            src = share
            pltpu.make_async_copy(share, total_hbm.at[own, :], own_sem.at[0]).start()
        for step in range(1, count):
            pltpu.make_async_remote_copy(
                src_ref=src,
                dst_ref=total_hbm.at[own, :],
                send_sem=fold_send.at[1, k],
                recv_sem=fold_recv.at[1, k],
                device_id=device(lax.rem(place + step, count)),
                device_id_type=MESH,
            ).start()

    def spread_end(k):
        count = levels[k][0]
        if count > 1:
            all_parts = total_hbm.at[pl.ds(0, (count - 1) * sizes[k + 1]), :]
            pltpu.make_async_copy(all_parts, all_parts, fold_recv.at[1, k]).wait()
        if k == len(levels) - 1:
            own = row_part(bases[k + 1], sizes[k + 1])
            pltpu.make_async_copy(share, total_hbm.at[own, :], own_sem.at[0]).wait()

    def fold_sent():
        for k, (count, _, _, wire, _) in enumerate(levels):
            for way, held in ((0, acc if wire is None else wire), (1, total_hbm)):
                if count == 1:
                    continue
                part = held.at[pl.ds(0, (count - 1) * sizes[k + 1]), :]
                pltpu.make_async_remote_copy(
                    src_ref=part,
                    dst_ref=part,
                    send_sem=fold_send.at[way, k],
                    recv_sem=fold_recv.at[way, k],
                    device_id={"lon": my_lon},
                    device_id_type=MESH,
                ).wait_send()

    spec_rows = spec_sum.shape[0]

    def spec_part(at):
        return pl.ds(pl.multiple_of(at * spec_rows, 8), spec_rows)

    def spec_lat_copies(way, src, dst):
        for step in range(1, lat):
            peer = lax.rem(my_lat + step, lat)
            pltpu.make_async_remote_copy(
                src_ref=src(peer),
                dst_ref=dst(step),
                send_sem=spec_send.at[way],
                recv_sem=spec_recv.at[way],
                device_id={"lat": peer},
                device_id_type=MESH,
            ).start()

    def spec_start():
        spec_lat_copies(
            0, lambda p: spec.at[spec_part(p), :], lambda s: spec_lat.at[s - 1]
        )

    def spec_pairs(action):
        half = lax.rem(my_lon, halves)
        for q in range(group):
            target = half * group + q

            @pl.when(target != my_lon)
            def _(target=target, q=q):
                copy = pltpu.make_async_remote_copy(
                    src_ref=spec_sum,
                    dst_ref=spec_lon.at[my_lon // halves],
                    send_sem=spec_pair.at[1, q],
                    recv_sem=spec_pair.at[0, my_lon // halves],
                    device_id={"lon": target},
                    device_id_type=MESH,
                )
                if action == "start":
                    copy.start()
                else:
                    copy.wait_send()

            if action == "start":

                @pl.when(target == my_lon)
                def _():
                    pltpu.make_async_copy(
                        spec_sum, spec_lon.at[my_lon // halves], spec_pair.at[0, my_lon // halves]
                    ).start()

    def spec_middle():
        pltpu.make_async_copy(spec_lat, spec_lat, spec_recv.at[0]).wait()
        got = spec[spec_part(my_lat), :]
        for step in range(1, lat):
            got = got + spec_lat[step - 1]
        spec_sum[...] = got
        spec_pairs("start")

    def spec_back():
        for q in range(group):
            pltpu.make_async_copy(spec_lon.at[q], spec_lon.at[q], spec_pair.at[0, q]).wait()
        got = spec_lon[0]
        for q in range(1, group):
            got = got + spec_lon[q]
        spec_own[...] = got
        own = spec_part(my_lat)
        spec_lat_copies(1, lambda p: spec_own, lambda s: small_hbm.at[own, :])
        pltpu.make_async_copy(spec_own, small_hbm.at[own, :], own_sem.at[1]).start()

    def spec_end():
        pltpu.make_async_copy(spec_own, small_hbm.at[spec_part(my_lat), :], own_sem.at[1]).wait()
        part = spec.at[pl.ds(0, (lat - 1) * spec_rows), :]
        pltpu.make_async_copy(part, part, spec_recv.at[1]).wait()
        for way in range(2):
            pltpu.make_async_remote_copy(
                src_ref=part,
                dst_ref=part,
                send_sem=spec_send.at[way],
                recv_sem=spec_recv.at[way],
                device_id={"lat": my_lat},
                device_id_type=MESH,
            ).wait_send()
        spec_pairs("end")

    def norm_copies(way, axis, count, place, src, parts, action):
        for step in range(1, count):
            copy = pltpu.make_async_remote_copy(
                src_ref=src,
                dst_ref=parts.at[step - 1],
                send_sem=norm_send.at[way, step - 1],
                recv_sem=norm_recv.at[way],
                device_id={axis: lax.rem(place + step, count)},
                device_id_type=MESH,
            )
            if action == "start":
                copy.start()
            else:
                copy.wait_send()

    def norm_end(way, parts, count):
        pltpu.make_async_copy(parts, parts, norm_recv.at[way]).wait()
        got = norm_own[way]
        for step in range(1, count):
            got = got + parts[step - 1]
        norm_own[way + 1] = got

    def norm_skip():
        lines = [jnp.zeros((1, width), jnp.float32) for _ in range(2)]
        all_mixed = jnp.sum(mixed_sums[...], axis=0, keepdims=True)
        for q in range(halves):
            lanes = slice(q * LANES, (q + 1) * LANES)
            part = skip[:, lanes].astype(jnp.float32)
            held = acc[pl.ds(2 * hidden_rows + q * width, width), :]
            for which, values in enumerate((held, all_mixed[:, lanes])):
                lines[which] += jnp.sum((part * values).T, axis=0, keepdims=True)
        for which in range(2):
            for half in range(halves):
                norm_own[0, pl.ds(which * halves + half, 1), :] = lines[which][
                    :, half * LANES : (half + 1) * LANES
                ]

    def norm_start():
        for half in range(halves):

            @pl.when(lax.rem(my_lon, halves) == half)
            def _(half=half):
                for which in range(2):
                    line = jnp.sum(norm_sums[which], axis=0, keepdims=True)
                    norm_own[0, pl.ds(which * halves + half, 1), :] += line

        norm_copies(0, "lon", lon, my_lon, norm_own.at[0], norm_lon, "start")

    def norm_middle():
        norm_end(0, norm_lon, lon)
        norm_copies(1, "lat", lat, my_lat, norm_own.at[1], norm_lat, "start")

    def norm_finish():
        norm_end(1, norm_lat, lat)
        where = pl.ds(lat * spec_rows, 8)
        copy = pltpu.make_async_copy(norm_own.at[2], small_hbm.at[where, :], own_sem.at[2])
        copy.start()
        norm_copies(0, "lon", lon, my_lon, norm_own.at[0], norm_lon, "end")
        norm_copies(1, "lat", lat, my_lat, norm_own.at[1], norm_lat, "end")
        copy.wait()

    def last_mixed_start():
        last_mixed_copy().start()

    def run(*steps):
        def go():
            for step, k in steps:
                step() if k is None else step(k)

        return go

    end = chunks - 1
    aside = {
        (0, "1"): build,
        (end + 5, "5b"): run((last_mixed_start, None), (norm_skip, None), (fold_start, 0)),
        (end + 5, "9"): run((fold_end, 0), (fold_start, 1)),
        (end + 6, "8"): run((fold_end, 1), (fold_start, 2)),
        (end + 7, "7"): run((fold_end, 2), (fold_start, 3)),
        (end + 7, "9"): run((fold_end, 3), (spread_start, 3)),
        (end + 8, "9"): run((spread_end, 3), (spread_start, 2)),
        (end + 9, "8"): run((spread_end, 2), (spread_start, 1)),
        (end + 9, "9"): run((spread_end, 1), (spread_start, 0), (spec_middle, None)),
        (end + 9, "7"): run((spec_start, None)),
        (end + 10, "8"): run((norm_middle, None), (spec_back, None)),
    }

    stages = {
        "1": stage_1,
        "2": stage_2,
        "3": stage_3,
        "4": stage_4,
        "5a": stage_5a,
        "5b": stage_5b,
        "6": stage_6,
        "7": stage_7,
        "8": stage_8,
        "9": stage_9,
    }

    for sample in range(group):
        x_load(sample).start()

    padded = lon_a.shape[2]
    if padded > rows:
        for held in (normed, mixed):
            held[:, :, rows:, :] = jnp.zeros_like(held[:, :, rows:, :])
        for held in (send_4, send_8):
            held[:, rows:, :] = jnp.zeros_like(held[:, rows:, :])
    barrier = pltpu.get_barrier_semaphore()
    for step in range(1, lon):
        pl.semaphore_signal(
            barrier, inc=1, device_id={"lon": lax.rem(my_lon + step, lon)}, device_id_type=MESH
        )
    for step in range(1, lat):
        pl.semaphore_signal(
            barrier, inc=1, device_id={"lat": lax.rem(my_lat + step, lat)}, device_id_type=MESH
        )
    for k in range(group):
        normalize(k)
    for sample in range(group, batch):
        x_load(sample).start()
    for k in range(group):
        g_load(k, k).start()
    pl.semaphore_wait(barrier, lon - 1 + lat - 1)

    weight_copies(True)

    def tick(now, carry):
        for stage in ORDER:
            chunk = now - OFFSET[stage]

            @pl.when(jnp.logical_and(chunk >= 0, chunk < (end if stage == "9" else chunks)))
            def _(stage=stage, chunk=chunk):
                stages[stage](chunk)

            for (when, after), action in aside.items():
                if after == stage:
                    pl.when(now == when)(action)

        return carry

    lax.fori_loop(0, chunks + max(OFFSET.values()), tick, 0)

    spread_end(0)
    norm_finish()
    spec_end()
    fold_sent()
    for step in range(group):
        member_landed(8, end, step)
    last_own().wait()
    last_mixed_copy().wait()
    weight_copies(False)
    last = chunks - 1
    for stage in (1, 5):
        sent(stage, lon_a.at[last, pl.ds(0, lon - 1)])
    for stage, buffer, count in (
        (2, send_2, lat - 1),
        (3, send_3, lat - 1),
        (4, send_4, lon - 1),
        (6, send_6, lat - 1),
        (7, send_7, lat - 1),
        (8, send_8, lon - 1),
    ):
        sent(stage, buffer.at[pl.ds(0, count)])
    for k in range(group):
        o_store(last * group + k, k).wait()
        if chunks > 1:
            i_store((last - 1) * group + k, k).wait()


def result_kernel(
    group,
    narrow,
    norm_at,
    out_from,
    gin_from,
    total,
    small,
    last_mixed,
    last_grid,
    x_hbm,
    skip,
    gain,
    bias,
    out_to,
    gin_to,
    grad_spec,
    grad_skip,
    grad_in,
    grad_out,
    in_bias,
    vectors,
    gin_held,
    out_held,
    x_held,
    mixed_held,
    grid_held,
    sems,
    last_sems,
):
    batch, rows, width = out_from.shape
    hidden = grad_in.shape[1]
    halves = width // LANES
    degrees = grad_spec.shape[2]
    first = batch - group

    def reads(sample):
        out = pltpu.make_async_copy(out_from.at[sample], out_held.at[sample], sems.at[1, sample])
        if sample >= first:
            return (out,)
        return (pltpu.make_async_copy(gin_from.at[sample], gin_held.at[sample], sems.at[0, sample]), out)

    def gin_write(sample):
        return pltpu.make_async_copy(gin_held.at[sample], gin_to.at[sample], sems.at[2, sample])

    def writes(sample):
        out = pltpu.make_async_copy(out_held.at[sample], out_to.at[sample], sems.at[3, sample])
        return (out,) if sample >= first else (gin_write(sample), out)

    last = [
        pltpu.make_async_copy(source, held, last_sems.at[at])
        for at, (source, held) in enumerate(
            ((x_hbm.at[pl.ds(first, group)], x_held), (last_mixed, mixed_held), (last_grid, grid_held))
        )
    ]
    for copy in last:
        copy.start()
    for sample in range(batch):
        for copy in reads(sample):
            copy.start()
    for copy in last:
        copy.wait()

    back_tile = row_tile(rows, 144)
    for k in range(group):

        @pl.loop(0, rows // back_tile)
        def _(i, k=k):
            where = pl.ds(pl.multiple_of(i * back_tile, 8), back_tile)
            gin_held[first + k, where, :] = norm_step(
                x_held[k, where, :],
                jnp.concatenate([mixed_held[k, h, where, :] for h in range(halves)], axis=1),
                jnp.concatenate([grid_held[k, h, where, :] for h in range(halves)], axis=1),
                skip[...],
                gain[...],
            )

        gin_write(first + k).start()

    for sample in range(batch):
        for read, write in zip(reads(sample), writes(sample)):
            read.wait()
            write.start()

    def tile(base, height, q):
        return total[pl.ds(base + q * height, height), :].astype(jnp.float32)

    hidden_rows = width * hidden // LANES
    vector_rows = 2 * hidden_rows + width * width // LANES

    for q in range(hidden // LANES):
        where = pl.ds(q * LANES, LANES)
        grad_in[:, where] = tile(0, width, q)
        grad_out[where, :] = tile(hidden_rows, width, q).T
        in_bias[:, where] = jnp.sum(tile(vector_rows, 8, q), axis=0, keepdims=True)
    for q in range(halves):
        where = pl.ds(q * LANES, LANES)
        grad_skip[:, where] = tile(2 * hidden_rows, width, q)
        for which in range(3):
            at = vector_rows + 8 * (hidden + which * width) // LANES
            vectors[which, :, where] = jnp.sum(tile(at, 8, q), axis=0, keepdims=True)
        all_normed, everything = (small[pl.ds(norm_at + which * halves + q, 1), :] for which in range(2))
        vectors[3, :, where] = (all_normed - bias[:, where] * everything) / gain[:, where]
        vectors[4, :, where] = everything
    place = lax.rem(lax.axis_index("lon"), group)
    for which in range(2):
        turned = small[pl.ds(which * degrees, degrees), :].T
        for q in range(group):

            @pl.when(place == q)
            def _(q=q, which=which, turned=turned):
                grad_spec[which] = turned[q * narrow : (q + 1) * narrow, :]

    for sample in range(batch):
        for write in writes(sample):
            write.wait()
    for k in range(group):
        gin_write(first + k).wait()


def per_device(
    tables,
    lat,
    lon,
    inputs,
    legendre_forward,
    legendre_inverse,
    spectral_weight,
    skip_weight,
    gain_first,
    bias_first,
    gain_second,
    bias_second,
    mlp_in,
    mlp_in_bias,
    mlp_out,
    mlp_out_bias,
    cotangent,
):
    batch, band, columns, width = inputs.shape
    points = columns * lon
    slab, degrees, lats = legendre_forward.shape
    orders = slab * lat
    hidden = mlp_in.shape[1]
    rows = columns * band
    padded = -(-rows // 16) * 16
    halves = width // LANES
    group = lon // halves
    chunks = batch // group
    block = 2 * slab * band
    waves = 2 * orders

    forward, inverse = tables(points, lat)(orders)
    my_lon = lax.axis_index("lon")
    hidden = mlp_in.shape[1]
    flat_rows = (2 * hidden + width) * width // LANES + 8 * (hidden + 3 * width) // LANES
    share = -(-flat_rows // (16 * lat * lon)) * 16
    total_rows = share * lat * lon
    spec_rows = -(-2 * degrees // (8 * lat)) * 8

    def flat(values):
        return values.transpose(0, 2, 1, 3).reshape(batch, rows, width)

    def row(values):
        return values.reshape(1, -1)

    vmem = pl.BlockSpec(memory_space=pltpu.VMEM)
    hbm = pl.BlockSpec(memory_space=pl.ANY)
    fixed = pl.BlockSpec(memory_space=pltpu.HBM)
    low, full = jnp.bfloat16, jnp.float32
    results = pl.pallas_call(
        functools.partial(block_kernel, lat, lon),
        out_shape=(
            jax.ShapeDtypeStruct((batch, rows, width), low),
            jax.ShapeDtypeStruct((max(batch - group, 1), rows, width), full),
            jax.ShapeDtypeStruct((total_rows, LANES), low),
            jax.ShapeDtypeStruct((lat * spec_rows + 8, LANES), full),
            jax.ShapeDtypeStruct((group, halves, padded, LANES), low),
            jax.ShapeDtypeStruct((group, halves, padded, LANES), low),
        ),
        in_specs=[hbm, hbm] + [vmem] * 16,
        out_specs=(hbm,) * 6,
        scratch_shapes=[
            pltpu.VMEM((batch, rows, width), low),
            pltpu.VMEM((batch, halves, padded, LANES), low),
            pltpu.VMEM((batch, halves, padded, LANES), low),
            pltpu.VMEM((chunks, lon, padded, LANES), low),
            pltpu.VMEM((chunks, lon, padded, LANES), low),
            pltpu.VMEM((batch, halves, padded, LANES), low),
            pltpu.VMEM((chunks, lat, block, LANES), low),
            pltpu.VMEM((chunks, lat, block, LANES), low),
            pltpu.VMEM((chunks, slab, degrees, 2 * LANES), low),
            pltpu.VMEM((lat, block, LANES), low),
            pltpu.VMEM((lat, block, LANES), low),
            pltpu.VMEM((lon, padded, LANES), low),
            pltpu.VMEM((lat, block, LANES), low),
            pltpu.VMEM((lat, block, LANES), low),
            pltpu.VMEM((lon, padded, LANES), low),
            pltpu.VMEM((max(points, waves) * band, LANES), full),
            pltpu.VMEM((waves * band, LANES), full),
            pltpu.VMEM((group, rows, width), low),
            pltpu.VMEM((group, rows, width), low),
            pltpu.VMEM((group, rows, width), full),
            pltpu.SemaphoreType.DMA((8, chunks, group)),
            pltpu.SemaphoreType.DMA((8,)),
            pltpu.SemaphoreType.DMA((batch,)),
            pltpu.SemaphoreType.DMA((group,)),
            pltpu.SemaphoreType.DMA((group,)),
            pltpu.SemaphoreType.DMA((group,)),
            pltpu.VMEM((slab, degrees, lats), low),
            pltpu.VMEM((slab, lats, degrees), low),
            pltpu.VMEM((slab, lats, degrees), low),
            pltpu.VMEM((slab, degrees, lats), low),
            pltpu.VMEM((2, LANES, degrees), full),
            pltpu.VMEM((degrees, LANES), full),
            pltpu.VMEM((degrees, LANES), full),
            pltpu.VMEM((total_rows, LANES), full),
            pltpu.VMEM((1, total_rows // 2, LANES), full),
            pltpu.VMEM((1, total_rows // 4, LANES), full),
            pltpu.VMEM((max(lon // 2 - 1, 1), total_rows // (2 * lon), LANES), low),
            pltpu.VMEM((max(lat // 2 - 1, 1), share, LANES), low),
            pltpu.VMEM((total_rows // 4, LANES), low),
            pltpu.VMEM((total_rows // (2 * lon), LANES), low),
            pltpu.VMEM((share, LANES), low),
            pltpu.VMEM((lat * spec_rows, LANES), full),
            pltpu.VMEM((lat - 1, spec_rows, LANES), full),
            pltpu.VMEM((group, spec_rows, LANES), full),
            pltpu.VMEM((spec_rows, LANES), full),
            pltpu.VMEM((spec_rows, LANES), full),
            pltpu.VMEM((2, 8, LANES), full),
            pltpu.VMEM((8, width), full),
            pltpu.VMEM((3, 8, LANES), full),
            pltpu.VMEM((lon - 1, 8, LANES), full),
            pltpu.VMEM((lat - 1, 8, LANES), full),
            pltpu.SemaphoreType.DMA((2, group)),
            pltpu.SemaphoreType.DMA((2, 4)),
            pltpu.SemaphoreType.DMA((2, 4)),
            pltpu.SemaphoreType.DMA((2,)),
            pltpu.SemaphoreType.DMA((2,)),
            pltpu.SemaphoreType.DMA((2, group)),
            pltpu.SemaphoreType.DMA((2,)),
            pltpu.SemaphoreType.DMA((2, max(lat, lon) - 1)),
            pltpu.SemaphoreType.DMA((5,)),
        ],
        compiler_params=pltpu.CompilerParams(
            collective_id=0, has_side_effects=True, vmem_limit_bytes=63 * 2**20
        ),
    )(
        flat(inputs),
        flat(cotangent),
        jnp.asarray(forward),
        jnp.asarray(inverse),
        jnp.asarray(inverse.T),
        jnp.asarray(forward.T),
        legendre_forward.transpose(0, 2, 1),
        legendre_inverse,
        spectral_weight.transpose(0, 2, 1),
        skip_weight,
        mlp_in,
        mlp_out,
        row(gain_first),
        row(bias_first),
        row(gain_second),
        row(bias_second),
        row(mlp_in_bias),
        row(mlp_out_bias),
    )
    shapes = (
        ((batch, rows, width), low),
        ((batch, rows, width), full),
        ((2, width // lon, degrees), full),
        ((width, width), full),
        ((width, hidden), full),
        ((hidden, width), full),
        ((1, hidden), full),
        ((5, 1, width), full),
    )
    output, grad_inputs, grad_spec, grad_skip, grad_in, grad_out, in_bias, vectors = pl.pallas_call(
        functools.partial(result_kernel, group, width // lon, lat * spec_rows),
        out_shape=tuple(jax.ShapeDtypeStruct(*shape) for shape in shapes),
        in_specs=[fixed, fixed, vmem, vmem, fixed, fixed, fixed, vmem, vmem, vmem],
        out_specs=(fixed, fixed) + (vmem,) * 6,
        scratch_shapes=[
            pltpu.VMEM((batch, rows, width), full),
            pltpu.VMEM((batch, rows, width), low),
            pltpu.VMEM((group, rows, width), low),
            pltpu.VMEM((group, halves, padded, LANES), low),
            pltpu.VMEM((group, halves, padded, LANES), low),
            pltpu.SemaphoreType.DMA((4, batch)),
            pltpu.SemaphoreType.DMA((3,)),
        ],
        compiler_params=pltpu.CompilerParams(vmem_limit_bytes=48 * 2**20),
    )(*results, flat(inputs), skip_weight, row(gain_first), row(bias_first))

    def unflat(values):
        return values.reshape(batch, columns, band, width).transpose(0, 2, 1, 3)

    return (
        unflat(output),
        unflat(grad_inputs),
        grad_spec.transpose(0, 2, 1),
        grad_skip,
        vectors[3, 0],
        vectors[4, 0],
        vectors[1, 0],
        vectors[2, 0],
        grad_in,
        in_bias[0],
        grad_out,
        vectors[0, 0],
    )


def solution(mesh):
    lat, lon = mesh.shape["lat"], mesh.shape["lon"]
    grid = P(None, "lat", "lon", None)
    table = P("lat", None, None)
    channel = P(None, None, "lon")
    return jax.shard_map(
        functools.partial(per_device, fourier_tables, lat, lon),
        mesh=mesh,
        in_specs=(grid, table, table, channel) + (P(),) * 9 + (grid,),
        out_specs=(grid, grid, channel) + (P(),) * 9,
        check_vma=False,
    )
```

```python
import functools
import math

import jax
import jax.numpy as jnp
import ml_dtypes
import numpy as np
from jax import lax
from jax.experimental import pallas as pl
from jax.experimental.pallas import tpu as pltpu
from jax.sharding import PartitionSpec as P

epsilon = 1e-05
LANES = 128
MESH = pl.DeviceIdType.MESH
root = math.sqrt(2.0 / math.pi)
cubic = 0.044715

OFFSET = {"1": 0, "2": 1, "3a": 3, "3b": 4, "4": 5, "5a": 6, "5b": 6, "6": 8, "7a": 10, "7b": 11, "8": 12, "9": 13}
ORDER = ("1", "3b", "3a", "7b", "7a", "4", "5a", "6", "2", "5b", "8", "9")


def split_orders(orders, lat):
    high = 2 * orders // 3
    each = high // lat
    assert each * lat == high and 3 * high == 2 * orders
    return high, each


def fourier_tables(points, orders, lat):
    waves = np.arange(orders)
    phase = (waves[:, None] * np.arange(points)[None, :] % points).astype(np.float32)
    phase = phase * np.float32(2.0 * math.pi / points)
    cosine, sine = np.cos(phase), np.sin(phase)
    factor = np.where(waves == 0, 1.0, 2.0).astype(np.float32)[:, None]
    high, each = split_orders(orders, lat)
    near = lat // 2
    owned = [[t * each + i for i in range(each)] for t in range(lat)]
    owned += [[high + near * i + d for i in range(each)] for d in range(near)]

    def arrange(*parts):
        stacked = [part[waves] for waves in owned for part in parts]
        return np.concatenate(stacked).astype(ml_dtypes.bfloat16)

    return arrange(cosine, -sine), arrange(factor * cosine, -factor * sine)


def row_tile(rows, most):
    fits = [t for t in range(16, most + 1, 16) if rows % t == 0]
    return fits[-1] if fits else rows


def norm_parts(values):
    center = values - jnp.mean(values, axis=-1, keepdims=True)
    spread = jnp.mean(center * center, axis=-1, keepdims=True)
    scaled = lax.rsqrt(spread + epsilon)
    return center * scaled, scaled


def norm_back(grad_out, normal, scaled, gain):
    grad_norm = grad_out * gain
    inner = jnp.mean(grad_norm, axis=-1, keepdims=True)
    cross = jnp.mean(grad_norm * normal, axis=-1, keepdims=True)
    return scaled * (grad_norm - inner - normal * cross)


def norm_step(values, mixed, sent, skip, gain):
    normal, scaled = norm_parts(values.astype(jnp.float32))
    grad_normed = dot_t(mixed, skip) + sent.astype(jnp.float32)
    return mixed.astype(jnp.float32) + norm_back(grad_normed, normal, scaled, gain)


def fold(values):
    rows, width = values.shape
    return jnp.sum(values.reshape(rows // 8, 8, width), axis=0)


def dot(a, b):
    return jnp.dot(a, b, preferred_element_type=jnp.float32)


def dot_t(a, b):
    return lax.dot_general(a, b, (((1,), (1,)), ((), ())), preferred_element_type=jnp.float32)


def t_dot(a, b):
    return lax.dot_general(a, b, (((0,), (0,)), ((), ())), preferred_element_type=jnp.float32)


def block_kernel(
    lat,
    lon,
    x_hbm,
    g_hbm,
    fwd_t,
    inv_t,
    inv,
    fwd,
    raw_ana,
    raw_syn,
    weight,
    skip,
    mlp_in,
    mlp_out,
    gain_one,
    bias_one,
    gain_two,
    bias_two,
    bias_in,
    bias_out,
    out_hbm,
    gin_hbm,
    total_hbm,
    small_hbm,
    last_mixed,
    last_grid,
    x_all,
    normed,
    lon_a,
    lon_c,
    lon_b,
    lat_a,
    lat_b,
    coeffs,
    coeffs_high,
    pack_own,
    pack_far,
    stack,
    stack_held,
    send_2,
    send_3,
    send_4,
    send_6,
    send_7,
    send_8,
    wide,
    slim,
    g_buf,
    o_buf,
    i_buf,
    recv_sem,
    send_sem,
    x_sem,
    g_sem,
    o_sem,
    i_sem,
    tabs,
    ana,
    ana_t,
    syn,
    syn_t,
    ana_high,
    ana_high_t,
    syn_high,
    syn_high_t,
    tab_recv,
    tab_send,
    w_parts,
    w_real,
    w_imag,
    acc,
    part_core,
    part_near,
    part_chip,
    part_far,
    wire_chip,
    wire_far,
    share,
    spec,
    spec_lat,
    spec_lon,
    spec_sum,
    spec_own,
    norm_sums,
    mixed_sums,
    norm_own,
    norm_lon,
    norm_lat,
    w_sem,
    fold_recv,
    fold_send,
    spec_recv,
    spec_send,
    spec_pair,
    norm_recv,
    norm_send,
    own_sem,
):
    batch, rows, width = x_hbm.shape
    halves = width // LANES
    group = lon // halves
    chunks = batch // group
    points = fwd_t.shape[1]
    slab, lats, degrees = raw_ana.shape
    narrow = width // lon
    hidden = mlp_in.shape[1]
    band = lats // lat
    waves = 2 * slab * lat
    high, each = split_orders(slab * lat, lat)
    near = lat // 2
    block = 2 * each * band
    slots = lat + near
    low_rows = degrees - high
    starts = [near * i // 8 * 8 for i in range(each)]
    packs = [sum(low_rows - start for start in starts[:i]) for i in range(each)]
    my_lat, my_lon = lax.axis_index("lat"), lax.axis_index("lon")
    mixed = normed
    my_side, my_near = my_lat // near, lax.rem(my_lat, near)
    half_tile = row_tile(rows, 144)
    full_tile = row_tile(rows, 240)

    def lon_copy(stage, chunk, src, dst, peer, member=0):
        return pltpu.make_async_remote_copy(
            src_ref=src,
            dst_ref=dst,
            send_sem=send_sem.at[stage - 1],
            recv_sem=recv_sem.at[stage - 1, chunk, member],
            device_id={"lon": peer},
            device_id_type=MESH,
        )

    def lat_copy(send_at, recv_at, chunk, src, dst, peer):
        return pltpu.make_async_remote_copy(
            src_ref=src,
            dst_ref=dst,
            send_sem=send_sem.at[send_at],
            recv_sem=recv_sem.at[recv_at, chunk, 0],
            device_id={"lat": peer},
            device_id_type=MESH,
        )

    def own_copy(stage, chunk, src, dst):
        return pltpu.make_async_copy(src, dst, recv_sem.at[stage - 1, chunk, 0])

    def landed(stage, chunk, whole, member=0):
        pltpu.make_async_copy(whole, whole, recv_sem.at[stage - 1, chunk, member]).wait()

    def member_at(step):
        return lax.rem(my_lon // halves + step, group)

    def member_landed(stage, chunk, step):
        count = halves if step else halves - 1
        landed(stage, chunk, lon_a.at[chunk, pl.ds(0, count)], member_at(step))

    def sent(stage, part):
        lon_copy(stage, 0, part, part, my_lon).wait_send()

    def x_load(sample):
        return pltpu.make_async_copy(x_hbm.at[sample], x_all.at[sample], x_sem.at[sample])

    def g_load(sample, slot):
        return pltpu.make_async_copy(g_hbm.at[sample], g_buf.at[slot], g_sem.at[slot])

    def o_store(sample, slot):
        return pltpu.make_async_copy(o_buf.at[slot], out_hbm.at[sample], o_sem.at[slot])

    def i_store(sample, slot):
        return pltpu.make_async_copy(i_buf.at[slot], gin_hbm.at[sample], i_sem.at[slot])

    def spread_rows(stage, chunk, held, sample, landing):
        src = chunk * group + sample
        for half in range(halves):
            peer = sample * halves + half

            @pl.when(peer != my_lon)
            def _(peer=peer, half=half):
                lon_copy(stage, chunk, held.at[src, half], landing.at[chunk, my_lon], peer).start()

            @pl.when(peer == my_lon)
            def _(half=half):
                own_copy(stage, chunk, held.at[src, half], landing.at[chunk, my_lon]).start()

    def spread_low(send_at, recv_at, chunk, buffer, target):
        for step in range(1, lat):
            peer = lax.rem(my_lat + step, lat)
            lat_copy(send_at, recv_at, chunk, buffer.at[peer], target.at[chunk, my_lat], peer).start()

    def spread_high(send_at, recv_at, chunk, buffer, target):
        for step in range(1, near):
            peer = lax.rem(my_near + step, near)
            src, dst = buffer.at[lat + peer], target.at[chunk, lat + my_near]
            lat_copy(send_at, recv_at, chunk, src, dst, my_side * near + peer).start()

    def own_rows(at):
        return pl.ds(pl.multiple_of(at * block, 16), block)

    def to_waves(stage, chunk, table, scale, buffer, landing):
        landed(stage - 1, chunk, landing.at[chunk])
        for source in range(lon):
            wide[pl.ds(source * rows, rows), :] = landing[chunk, source, pl.ds(0, rows), :].astype(jnp.float32)
        for first in range(0, band, 2):
            rhs = jnp.concatenate(
                [wide[pl.ds(first + k, points, stride=band), :] for k in range(2)], axis=1
            ).astype(jnp.bfloat16)
            got = dot(table[...], rhs)
            if scale is not None:
                got = got * scale
            for k in range(2):
                slim[pl.ds(first + k, waves, stride=band), :] = got[:, k * LANES : (k + 1) * LANES]

        @pl.when(chunk > 0)
        def _():
            sent(stage, buffer.at[pl.ds(0, slots - 2)])

        for target in range(slots):
            buffer[target] = slim[pl.ds(target * block, block), :].astype(jnp.bfloat16)
        spread_low(stage - 1, stage - 1, chunk, buffer, lat_a)
        spread_high(stage - 1, stage - 1, chunk, buffer, lat_a)
        lat_a[chunk, my_lat] = slim[own_rows(my_lat), :].astype(jnp.bfloat16)
        lat_a[chunk, lat + my_near] = slim[own_rows(lat + my_near), :].astype(jnp.bfloat16)

    def to_points(stage, chunk, table, scale, buffer):
        landed(stage - 1, chunk, lat_b.at[chunk, pl.ds(0, slots - 2)])
        for source in range(slots):
            slim[pl.ds(source * block, block), :] = lat_b[chunk, source].astype(jnp.float32)
        for first in range(0, band, 2):
            rhs = jnp.concatenate(
                [slim[pl.ds(first + k, waves, stride=band), :] for k in range(2)], axis=1
            ).astype(jnp.bfloat16)
            got = dot(table[...], rhs)
            if scale is not None:
                got = got * scale
            for k in range(2):
                wide[pl.ds(first + k, points, stride=band), :] = got[:, k * LANES : (k + 1) * LANES]

        @pl.when(chunk > 0)
        def _():
            sent(stage, buffer.at[pl.ds(0, lon - 1)])

        for target in range(lon):
            grid = wide[pl.ds(target * rows, rows), :]
            buffer[target, pl.ds(0, rows), :] = grid.astype(jnp.bfloat16)
            if stage == 8:
                before = lon_a[chunk, target, pl.ds(0, rows), :].astype(jnp.float32)
                norm_sums[0] += fold(grid * before)
                norm_sums[1] += fold(grid)
        member, half = my_lon // halves, lax.rem(my_lon, halves)

        def send(landing):
            for step in range(1, lon):
                peer = lax.rem(my_lon + step, lon)
                lon_copy(stage, chunk, buffer.at[peer], landing, peer, member).start()

        def send_here():
            send(lon_b.at[chunk * group + member, half])
            own = pl.ds(pl.multiple_of(my_lon * rows, 8), rows)
            lon_b[chunk * group + member, half, pl.ds(0, rows), :] = wide[own, :].astype(jnp.bfloat16)

        if stage == 4:
            send_here()
        else:
            pl.when(chunk < chunks - 1)(send_here)

            @pl.when(chunk == chunks - 1)
            def _():
                norm_start()
                send(last_grid.at[member, half])
                last_own().start()

    def last_own():
        held = last_grid.at[my_lon // halves, lax.rem(my_lon, halves)]
        return pltpu.make_async_copy(send_8.at[my_lon], held, own_sem.at[3])

    def last_mixed_copy():
        part = mixed.at[pl.ds((chunks - 1) * group, group)]
        return pltpu.make_async_copy(part, last_mixed, own_sem.at[4])

    def wave_rows(first, count, i):
        parts = []
        for r in range(2):
            at = (r * each + i) * band
            held = [slim[pl.ds(s * block + at, band), :] for s in range(first, first + count)]
            parts.append(jnp.concatenate(held, axis=0))
        return jnp.concatenate(parts, axis=1).astype(jnp.bfloat16)

    def put_rows(got, count, i):
        for r in range(2):
            at = (r * each + i) * band
            for t in range(count):
                wide[pl.ds(t * block + at, band), :] = got[
                    t * band : (t + 1) * band, r * LANES : (r + 1) * LANES
                ]

    def pack_copy(k, chunk):
        peer = lax.rem(my_lat + near, lat)
        return lat_copy(10 + k, 8 + k, chunk, pack_own.at[k, chunk], pack_far.at[k, chunk], peer)

    def slab_first(stage, k, chunk, tables, between, buffer):
        first_table, second_table, high_table = tables
        landed(stage - 1, chunk, lat_a.at[chunk, pl.ds(0, slots - 2)])
        for source in range(slots):
            slim[pl.ds(source * block, block), :] = lat_a[chunk, source].astype(jnp.float32)
        for i in range(each):
            got = dot(high_table[i], wave_rows(lat, near, i))
            stack[pl.ds(packs[i], low_rows - starts[i]), :] = got[starts[i] :, :]

        @pl.when(chunk > 0)
        def _():
            pack_copy(k, chunk).wait_send()

        pack_own[k, chunk] = stack[...].astype(jnp.bfloat16)
        pack_copy(k, chunk).start()
        for m in range(each):
            real, imag = between(m, dot(first_table[m], wave_rows(0, lat, m)))
            low = jnp.concatenate([real, imag], axis=1).astype(jnp.bfloat16)
            put_rows(dot(second_table[m], low), lat, m)

        @pl.when(chunk > 0)
        def _():
            sent(stage, buffer.at[pl.ds(0, lat - 1)])

        for target in range(lat):
            buffer[target] = wide[pl.ds(target * block, block), :].astype(jnp.bfloat16)
        spread_low(stage - 1, stage - 1, chunk, buffer, lat_b)
        lat_b[chunk, my_lat] = wide[own_rows(my_lat), :].astype(jnp.bfloat16)

    def slab_second(stage, k, chunk, table, before, between, buffer):
        landed(9 + k, chunk, pack_far.at[k, chunk])
        stack[...] = pack_own[k, chunk].astype(jnp.float32) + pack_far[k, chunk].astype(jnp.float32)
        before()
        for i in range(each):
            count = low_rows - starts[i]
            real, imag = between(pl.ds(packs[i], count), high + starts[i], count)
            low = jnp.concatenate([real, imag], axis=1)
            if starts[i]:
                low = jnp.concatenate([jnp.zeros((starts[i], 2 * LANES), jnp.float32), low], axis=0)
            put_rows(dot(table[i], low.astype(jnp.bfloat16)), near, i)

        if near > 1:

            @pl.when(chunk > 0)
            def _():
                sent(9 + k, buffer.at[pl.ds(lat, near - 1)])

        for target in range(near):
            buffer[lat + target] = wide[pl.ds(target * block, block), :].astype(jnp.bfloat16)
        spread_high(8 + k, stage - 1, chunk, buffer, lat_b)
        lat_b[chunk, lat + my_near] = wide[own_rows(my_near), :].astype(jnp.bfloat16)

    hidden_rows = width * hidden // LANES
    vector_rows = 2 * hidden_rows + width * width // LANES

    def gather_rows(base, values):
        count = values.shape[0]
        for q in range(values.shape[1] // LANES):
            acc[pl.ds(base + q * count, count), :] += values[:, q * LANES : (q + 1) * LANES]

    def both(held, sample, where):
        return jnp.concatenate([held[sample, h, where, :] for h in range(halves)], axis=1)

    def normalize(sample):
        x_load(sample).wait()

        @pl.loop(0, rows // half_tile)
        def _(i):
            where = pl.ds(pl.multiple_of(i * half_tile, 8), half_tile)
            normal, _ = norm_parts(x_all[sample, where, :].astype(jnp.float32))
            low = (normal * gain_one[...] + bias_one[...]).astype(jnp.bfloat16)
            for h in range(halves):
                normed[sample, h, where, :] = low[:, h * LANES : (h + 1) * LANES]

    def stage_1(chunk):
        @pl.when(chunk > 0)
        def _():
            sent(1, lon_a.at[chunk, pl.ds(0, lon - 1)])

        for step in reversed(range(group)):
            k = member_at(step)

            @pl.when(chunk > 0)
            def _(k=k):
                normalize(chunk * group + k)

            spread_rows(1, chunk, normed, k, lon_a)

    def stage_2(chunk):
        to_waves(2, chunk, fwd_t, 1.0 / points, send_2, lon_a)

    def filtered(real, imag, rows):
        wr, wi = w_real[rows, :], w_imag[rows, :]
        return wr * real - wi * imag, wr * imag + wi * real

    def stage_3a(chunk):
        def between(m, got):
            coeffs[chunk, m] = got.astype(jnp.bfloat16)
            return filtered(got[:, :LANES], got[:, LANES:], pl.ds(0, degrees))

        slab_first(3, 0, chunk, (ana, syn, ana_high), between, send_3)

    def stage_3b(chunk):
        def before():
            coeffs_high[chunk] = stack[...].astype(jnp.bfloat16)

        def between(where, degree, count):
            got = stack[where, :]
            return filtered(got[:, :LANES], got[:, LANES:], pl.ds(degree, count))

        slab_second(3, 0, chunk, syn_high, before, between, send_3)

    def stage_4(chunk):
        to_points(4, chunk, inv, None, send_4)

    def stage_5a(chunk):
        @pl.when(chunk > 0)
        def _():
            sent(5, lon_a.at[chunk, pl.ds(0, lon - 1)])

        @pl.when(chunk == chunks - 1)
        def _():
            sent(1, lon_a.at[chunk, pl.ds(0, lon - 1)])

        feed_forward(chunk, range(group // 2))

    def stage_5b(chunk):
        feed_forward(chunk, range(group // 2, group))

    def feed_forward(chunk, steps):
        for step in steps:
            member_landed(4, chunk, step)
            k = member_at(step)
            sample = chunk * group + k
            g_load(sample, k).wait()

            @pl.when(chunk > 0)
            def _(sample=sample, k=k):
                o_store(sample, k).wait()

            @pl.loop(0, rows // full_tile)
            def _(i):
                where = pl.ds(pl.multiple_of(i * full_tile, 8), full_tile)
                low_one = both(normed, sample, where)
                spatial = both(lon_b, sample, where).astype(jnp.float32)
                resid = x_all[sample, where, :].astype(jnp.float32) + (spatial + dot(low_one, skip[...]))
                normal, scaled = norm_parts(resid)
                low_two = (normal * gain_two[...] + bias_two[...]).astype(jnp.bfloat16)
                pre = dot(low_two, mlp_in[...]) + bias_in[...]
                square = pre * pre
                curve = jnp.tanh(root * pre * (1.0 + cubic * square))
                lifted = 0.5 + 0.5 * curve
                act = (pre * lifted).astype(jnp.bfloat16)
                slope = lifted + (0.5 * root) * pre * (1.0 - curve * curve) * (1.0 + (3.0 * cubic) * square)
                o_buf[k, where, :] = (resid + dot(act, mlp_out[...]) + bias_out[...]).astype(jnp.bfloat16)
                g_low = g_buf[k, where, :]
                gather_rows(hidden_rows, t_dot(g_low, act))
                grad_pre = (dot_t(g_low, mlp_out[...]) * slope).astype(jnp.bfloat16)
                gather_rows(0, t_dot(low_two, grad_pre))
                gather_rows(vector_rows, fold(grad_pre.astype(jnp.float32)))
                grad_second = dot_t(grad_pre, mlp_in[...])
                g_full = g_low.astype(jnp.float32)
                for at, values in enumerate((g_full, grad_second * normal, grad_second)):
                    gather_rows(vector_rows + 8 * (hidden + at * width) // LANES, fold(values))
                grad_mixed = (g_full + norm_back(grad_second, normal, scaled, gain_two[...])).astype(jnp.bfloat16)
                gather_rows(2 * hidden_rows, t_dot(low_one, grad_mixed))
                mixed_sums[...] += fold(grad_mixed.astype(jnp.float32))
                for h in range(halves):
                    mixed[sample, h, where, :] = grad_mixed[:, h * LANES : (h + 1) * LANES]

            o_store(sample, k).start()

            @pl.when(chunk < chunks - 1)
            def _(sample=sample, k=k):
                g_load(sample + group, k).start()

            spread_rows(5, chunk, mixed, k, lon_c)

    def stage_6(chunk):
        to_waves(6, chunk, inv_t, None, send_6, lon_c)

    def unfiltered(got, held, degree, count, share_of):
        dr, di = got[:, :LANES], got[:, LANES:]
        ar, ai = held[:, :LANES], held[:, LANES:]
        spec[pl.ds(degree, count), :] += share_of * (dr * ar + di * ai)
        spec[pl.ds(degrees + degree, count), :] += share_of * (di * ar - dr * ai)
        wr, wi = w_real[pl.ds(degree, count), :], w_imag[pl.ds(degree, count), :]
        return wr * dr + wi * di, wr * di - wi * dr

    def stage_7a(chunk):
        def between(m, got):
            return unfiltered(got, coeffs[chunk, m].astype(jnp.float32), 0, degrees, 1.0)

        slab_first(7, 1, chunk, (syn_t, ana_t, syn_high_t), between, send_7)

    def stage_7b(chunk):
        def before():
            stack_held[...] = coeffs_high[chunk].astype(jnp.float32)

        def between(where, degree, count):
            return unfiltered(stack[where, :], stack_held[where, :], degree, count, 0.5)

        slab_second(7, 1, chunk, ana_high_t, before, between, send_7)

    def stage_8(chunk):
        to_points(8, chunk, fwd, 1.0 / points, send_8)

    def stage_9(chunk):
        for step in range(group):
            member_landed(8, chunk, step)
            k = member_at(step)
            sample = chunk * group + k

            @pl.when(chunk > 0)
            def _(sample=sample, k=k):
                i_store(sample, k).wait()

            @pl.loop(0, rows // half_tile)
            def _(i):
                where = pl.ds(pl.multiple_of(i * half_tile, 8), half_tile)
                i_buf[k, where, :] = norm_step(
                    x_all[sample, where, :],
                    both(mixed, sample, where),
                    both(lon_b, sample, where),
                    skip[...],
                    gain_one[...],
                )

            i_store(sample, k).start()

    def weight_copies(start):
        place = lax.rem(my_lon, group)
        held = w_parts.at[:, pl.ds(pl.multiple_of(place * narrow, 8), narrow), :]
        for q in range(group):
            peer = my_lon // group + halves * q

            @pl.when(peer != my_lon)
            def _(peer=peer, q=q):
                copy = pltpu.make_async_remote_copy(
                    src_ref=weight,
                    dst_ref=held,
                    send_sem=w_sem.at[1, q],
                    recv_sem=w_sem.at[0, place],
                    device_id={"lon": peer},
                    device_id_type=MESH,
                )
                if start:
                    copy.start()
                else:
                    copy.wait_send()

            if start:

                @pl.when(peer == my_lon)
                def _():
                    pltpu.make_async_copy(weight, held, w_sem.at[0, place]).start()

    def table_copies(start):
        def one(i, carry):
            wave = my_lat * slab + i

            def give(peer, slot, way):
                for which, raw in enumerate((raw_ana, raw_syn)):

                    @pl.when(peer != my_lat)
                    def _(which=which, raw=raw):
                        copy = pltpu.make_async_remote_copy(
                            src_ref=raw.at[i],
                            dst_ref=tabs.at[which, slot],
                            send_sem=tab_send.at[which, i, way],
                            recv_sem=tab_recv.at[which],
                            device_id={"lat": peer},
                            device_id_type=MESH,
                        )
                        if start:
                            copy.start()
                        else:
                            copy.wait_send()

                    if start:

                        @pl.when(peer == my_lat)
                        def _(which=which, raw=raw):
                            pltpu.make_async_copy(raw.at[i], tabs.at[which, slot], tab_recv.at[which]).start()

            @pl.when(wave < high)
            def _():
                give(lax.div(wave, each), lax.rem(wave, each), 0)

            @pl.when(wave >= high)
            def _():
                above = wave - high
                for side in range(2):
                    give(side * near + lax.rem(above, near), each + lax.div(above, near), side)

            return carry

        lax.fori_loop(0, slab, one, 0)

    def build():
        acc[...] = jnp.zeros_like(acc)
        spec[...] = jnp.zeros_like(spec)
        norm_sums[...] = jnp.zeros_like(norm_sums)
        mixed_sums[...] = jnp.zeros_like(mixed_sums)
        norm_own[...] = jnp.zeros_like(norm_own)
        degree = lax.broadcasted_iota(jnp.int32, (lats, degrees), 1)
        for which in range(2):
            pltpu.make_async_copy(tabs.at[which], tabs.at[which], tab_recv.at[which]).wait()
        kinds = ((ana_t, ana, ana_high_t, ana_high), (syn, syn_t, syn_high, syn_high_t))

        @pl.loop(0, each)
        def _(i):
            half = pl.ds(pl.multiple_of(my_side * near * band, 16), near * band)
            for which, (plain, turned, part, part_turned) in enumerate(kinds):
                values = tabs[which, i].astype(jnp.float32)
                values = jnp.where(degree >= my_lat * each + i, values, 0.0)
                plain[i] = values.astype(jnp.bfloat16)
                turned[i] = values.T.astype(jnp.bfloat16)
                values = tabs[which, each + i, half, :].astype(jnp.float32)
                values = jnp.where(degree[: near * band] >= high + near * i + my_near, values, 0.0)
                values = values.T[high:, :]
                part_turned[i] = values.astype(jnp.bfloat16)
                part[i] = values.T.astype(jnp.bfloat16)

        for q in range(group):
            part = w_parts.at[:, pl.ds(q * narrow, narrow), :]
            pltpu.make_async_copy(part, part, w_sem.at[0, q]).wait()
        w_real[...] = w_parts[0].T
        w_imag[...] = w_parts[1].T

    total_rows = acc.shape[0]
    place_core, place_chip = lax.rem(my_lon, 2), my_lon // 2
    place_near, place_far = lax.rem(my_lat, 2), my_lat // 2
    levels = (
        (2, place_core, part_core, None, lambda p: {"lon": 2 * place_chip + p}),
        (2, place_near, part_near, None, lambda p: {"lat": 2 * place_far + p}),
        (lon // 2, place_chip, part_chip, wire_chip, lambda p: {"lon": 2 * p + place_core}),
        (lat // 2, place_far, part_far, wire_far, lambda p: {"lat": 2 * p + place_near}),
    )
    bases, sizes = [0], [total_rows]
    for count, place, _, _, _ in levels:
        sizes.append(sizes[-1] // count)
        bases.append(bases[-1] + place * sizes[-1])

    def row_part(at, count):
        return pl.ds(pl.multiple_of(at, 16), count)

    def fold_start(k):
        count, place, parts, wire, device = levels[k]
        if wire is not None:
            wire[...] = acc[row_part(bases[k], sizes[k]), :].astype(jnp.bfloat16)
        for step in range(1, count):
            peer = lax.rem(place + step, count)
            if wire is None:
                src = acc.at[row_part(bases[k] + peer * sizes[k + 1], sizes[k + 1]), :]
            else:
                src = wire.at[row_part(peer * sizes[k + 1], sizes[k + 1]), :]
            pltpu.make_async_remote_copy(
                src_ref=src,
                dst_ref=parts.at[step - 1],
                send_sem=fold_send.at[0, k],
                recv_sem=fold_recv.at[0, k],
                device_id=device(peer),
                device_id_type=MESH,
            ).start()

    def fold_end(k):
        count, _, parts, _, _ = levels[k]
        if count == 1:
            return
        pltpu.make_async_copy(parts, parts, fold_recv.at[0, k]).wait()
        got = parts[0].astype(jnp.float32)
        for step in range(2, count):
            got = got + parts[step - 1].astype(jnp.float32)
        acc[row_part(bases[k + 1], sizes[k + 1]), :] += got

    def spread_start(k):
        count, place, _, _, device = levels[k]
        own = row_part(bases[k + 1], sizes[k + 1])
        src = total_hbm.at[own, :]
        if k == len(levels) - 1:
            share[...] = acc[own, :].astype(jnp.bfloat16)
            src = share
            pltpu.make_async_copy(share, total_hbm.at[own, :], own_sem.at[0]).start()
        for step in range(1, count):
            pltpu.make_async_remote_copy(
                src_ref=src,
                dst_ref=total_hbm.at[own, :],
                send_sem=fold_send.at[1, k],
                recv_sem=fold_recv.at[1, k],
                device_id=device(lax.rem(place + step, count)),
                device_id_type=MESH,
            ).start()

    def spread_end(k):
        count = levels[k][0]
        if count > 1:
            all_parts = total_hbm.at[pl.ds(0, (count - 1) * sizes[k + 1]), :]
            pltpu.make_async_copy(all_parts, all_parts, fold_recv.at[1, k]).wait()
        if k == len(levels) - 1:
            own = row_part(bases[k + 1], sizes[k + 1])
            pltpu.make_async_copy(share, total_hbm.at[own, :], own_sem.at[0]).wait()

    def fold_sent():
        for k, (count, _, _, wire, _) in enumerate(levels):
            for way, held in ((0, acc if wire is None else wire), (1, total_hbm)):
                if count == 1:
                    continue
                part = held.at[pl.ds(0, (count - 1) * sizes[k + 1]), :]
                pltpu.make_async_remote_copy(
                    src_ref=part,
                    dst_ref=part,
                    send_sem=fold_send.at[way, k],
                    recv_sem=fold_recv.at[way, k],
                    device_id={"lon": my_lon},
                    device_id_type=MESH,
                ).wait_send()

    spec_rows = spec_sum.shape[0]

    def spec_part(at):
        return pl.ds(pl.multiple_of(at * spec_rows, 8), spec_rows)

    def spec_lat_copies(way, src, dst):
        for step in range(1, lat):
            peer = lax.rem(my_lat + step, lat)
            pltpu.make_async_remote_copy(
                src_ref=src(peer),
                dst_ref=dst(step),
                send_sem=spec_send.at[way],
                recv_sem=spec_recv.at[way],
                device_id={"lat": peer},
                device_id_type=MESH,
            ).start()

    def spec_start():
        spec_lat_copies(
            0, lambda p: spec.at[spec_part(p), :], lambda s: spec_lat.at[s - 1]
        )

    def spec_pairs(action):
        half = lax.rem(my_lon, halves)
        for q in range(group):
            target = half * group + q

            @pl.when(target != my_lon)
            def _(target=target, q=q):
                copy = pltpu.make_async_remote_copy(
                    src_ref=spec_sum,
                    dst_ref=spec_lon.at[my_lon // halves],
                    send_sem=spec_pair.at[1, q],
                    recv_sem=spec_pair.at[0, my_lon // halves],
                    device_id={"lon": target},
                    device_id_type=MESH,
                )
                if action == "start":
                    copy.start()
                else:
                    copy.wait_send()

            if action == "start":

                @pl.when(target == my_lon)
                def _():
                    pltpu.make_async_copy(
                        spec_sum, spec_lon.at[my_lon // halves], spec_pair.at[0, my_lon // halves]
                    ).start()

    def spec_middle():
        pltpu.make_async_copy(spec_lat, spec_lat, spec_recv.at[0]).wait()
        got = spec[spec_part(my_lat), :]
        for step in range(1, lat):
            got = got + spec_lat[step - 1]
        spec_sum[...] = got
        spec_pairs("start")

    def spec_back():
        for q in range(group):
            pltpu.make_async_copy(spec_lon.at[q], spec_lon.at[q], spec_pair.at[0, q]).wait()
        got = spec_lon[0]
        for q in range(1, group):
            got = got + spec_lon[q]
        spec_own[...] = got
        own = spec_part(my_lat)
        spec_lat_copies(1, lambda p: spec_own, lambda s: small_hbm.at[own, :])
        pltpu.make_async_copy(spec_own, small_hbm.at[own, :], own_sem.at[1]).start()

    def spec_end():
        pltpu.make_async_copy(spec_own, small_hbm.at[spec_part(my_lat), :], own_sem.at[1]).wait()
        part = spec.at[pl.ds(0, (lat - 1) * spec_rows), :]
        pltpu.make_async_copy(part, part, spec_recv.at[1]).wait()
        for way in range(2):
            pltpu.make_async_remote_copy(
                src_ref=part,
                dst_ref=part,
                send_sem=spec_send.at[way],
                recv_sem=spec_recv.at[way],
                device_id={"lat": my_lat},
                device_id_type=MESH,
            ).wait_send()
        spec_pairs("end")

    def norm_copies(way, axis, count, place, src, parts, action):
        for step in range(1, count):
            copy = pltpu.make_async_remote_copy(
                src_ref=src,
                dst_ref=parts.at[step - 1],
                send_sem=norm_send.at[way, step - 1],
                recv_sem=norm_recv.at[way],
                device_id={axis: lax.rem(place + step, count)},
                device_id_type=MESH,
            )
            if action == "start":
                copy.start()
            else:
                copy.wait_send()

    def norm_end(way, parts, count):
        pltpu.make_async_copy(parts, parts, norm_recv.at[way]).wait()
        got = norm_own[way]
        for step in range(1, count):
            got = got + parts[step - 1]
        norm_own[way + 1] = got

    def norm_skip():
        lines = [jnp.zeros((1, width), jnp.float32) for _ in range(2)]
        all_mixed = jnp.sum(mixed_sums[...], axis=0, keepdims=True)
        for q in range(halves):
            lanes = slice(q * LANES, (q + 1) * LANES)
            part = skip[:, lanes].astype(jnp.float32)
            held = acc[pl.ds(2 * hidden_rows + q * width, width), :]
            for which, values in enumerate((held, all_mixed[:, lanes])):
                lines[which] += jnp.sum((part * values).T, axis=0, keepdims=True)
        for which in range(2):
            for half in range(halves):
                norm_own[0, pl.ds(which * halves + half, 1), :] = lines[which][
                    :, half * LANES : (half + 1) * LANES
                ]

    def norm_start():
        for half in range(halves):

            @pl.when(lax.rem(my_lon, halves) == half)
            def _(half=half):
                for which in range(2):
                    line = jnp.sum(norm_sums[which], axis=0, keepdims=True)
                    norm_own[0, pl.ds(which * halves + half, 1), :] += line

        norm_copies(0, "lon", lon, my_lon, norm_own.at[0], norm_lon, "start")

    def norm_middle():
        norm_end(0, norm_lon, lon)
        norm_copies(1, "lat", lat, my_lat, norm_own.at[1], norm_lat, "start")

    def norm_finish():
        norm_end(1, norm_lat, lat)
        where = pl.ds(lat * spec_rows, 8)
        copy = pltpu.make_async_copy(norm_own.at[2], small_hbm.at[where, :], own_sem.at[2])
        copy.start()
        norm_copies(0, "lon", lon, my_lon, norm_own.at[0], norm_lon, "end")
        norm_copies(1, "lat", lat, my_lat, norm_own.at[1], norm_lat, "end")
        copy.wait()

    def last_mixed_start():
        last_mixed_copy().start()

    def run(*steps):
        def go():
            for step, k in steps:
                step() if k is None else step(k)

        return go

    end = chunks - 1
    aside = {
        (0, "1"): build,
        (end + 6, "5b"): run((last_mixed_start, None), (norm_skip, None), (fold_start, 0)),
        (end + 7, "7b"): run((fold_end, 0), (fold_start, 1)),
        (end + 7, "9"): run((fold_end, 1), (fold_start, 2)),
        (end + 8, "6"): run((fold_end, 2), (fold_start, 3)),
        (end + 9, "7a"): run((fold_end, 3), (spread_start, 3)),
        (end + 10, "7b"): run((spread_end, 3), (spread_start, 2)),
        (end + 11, "7b"): run((spread_end, 2), (spread_start, 1), (spec_start, None)),
        (end + 12, "8"): run((spread_end, 1), (spread_start, 0), (norm_middle, None), (spec_back, None)),
        (end + 11, "9"): run((spec_middle, None)),
    }

    stages = {
        "1": stage_1,
        "2": stage_2,
        "3a": stage_3a,
        "3b": stage_3b,
        "4": stage_4,
        "5a": stage_5a,
        "5b": stage_5b,
        "6": stage_6,
        "7a": stage_7a,
        "7b": stage_7b,
        "8": stage_8,
        "9": stage_9,
    }

    for sample in range(group):
        x_load(sample).start()

    padded = lon_a.shape[2]
    if padded > rows:
        normed[:, :, rows:, :] = jnp.zeros_like(normed[:, :, rows:, :])
        for held in (send_4, send_8):
            held[:, rows:, :] = jnp.zeros_like(held[:, rows:, :])
    barrier = pltpu.get_barrier_semaphore()
    for step in range(1, lon):
        pl.semaphore_signal(
            barrier, inc=1, device_id={"lon": lax.rem(my_lon + step, lon)}, device_id_type=MESH
        )
    for step in range(1, lat):
        pl.semaphore_signal(
            barrier, inc=1, device_id={"lat": lax.rem(my_lat + step, lat)}, device_id_type=MESH
        )
    for k in range(group):
        normalize(k)
    for sample in range(group, batch):
        x_load(sample).start()
    for k in range(group):
        g_load(k, k).start()
    pl.semaphore_wait(barrier, lon - 1 + lat - 1)

    weight_copies(True)
    table_copies(True)

    def tick(now, carry):
        for stage in ORDER:
            chunk = now - OFFSET[stage]

            @pl.when(jnp.logical_and(chunk >= 0, chunk < (end if stage == "9" else chunks)))
            def _(stage=stage, chunk=chunk):
                stages[stage](chunk)

            for (when, after), action in aside.items():
                if after == stage:
                    pl.when(now == when)(action)

        return carry

    lax.fori_loop(0, chunks + max(OFFSET.values()), tick, 0)

    spread_end(0)
    norm_finish()
    spec_end()
    fold_sent()
    for step in range(group):
        member_landed(8, end, step)
    last_own().wait()
    last_mixed_copy().wait()
    weight_copies(False)
    table_copies(False)
    last = chunks - 1
    sent(5, lon_a.at[last, pl.ds(0, lon - 1)])
    for stage, buffer, count in (
        (2, send_2, slots - 2),
        (3, send_3, lat - 1),
        (4, send_4, lon - 1),
        (6, send_6, slots - 2),
        (7, send_7, lat - 1),
        (8, send_8, lon - 1),
        (9, send_3, near - 1),
        (10, send_7, near - 1),
    ):
        if count:
            sent(stage, buffer.at[pl.ds(0, count)])
    for k in range(2):
        pack_copy(k, last).wait_send()
    for k in range(group):
        o_store(last * group + k, k).wait()
        if chunks > 1:
            i_store((last - 1) * group + k, k).wait()


def result_kernel(
    group,
    narrow,
    norm_at,
    out_from,
    gin_from,
    total,
    small,
    last_mixed,
    last_grid,
    x_hbm,
    skip,
    gain,
    bias,
    out_to,
    gin_to,
    grad_spec,
    grad_skip,
    grad_in,
    grad_out,
    in_bias,
    vectors,
    gin_held,
    out_held,
    x_held,
    mixed_held,
    grid_held,
    sems,
    last_sems,
):
    batch, rows, width = out_from.shape
    hidden = grad_in.shape[1]
    halves = width // LANES
    degrees = grad_spec.shape[2]
    first = batch - group

    def reads(sample):
        out = pltpu.make_async_copy(out_from.at[sample], out_held.at[sample], sems.at[1, sample])
        if sample >= first:
            return (out,)
        return (pltpu.make_async_copy(gin_from.at[sample], gin_held.at[sample], sems.at[0, sample]), out)

    def gin_write(sample):
        return pltpu.make_async_copy(gin_held.at[sample], gin_to.at[sample], sems.at[2, sample])

    def writes(sample):
        out = pltpu.make_async_copy(out_held.at[sample], out_to.at[sample], sems.at[3, sample])
        return (out,) if sample >= first else (gin_write(sample), out)

    last = [
        pltpu.make_async_copy(source, held, last_sems.at[at])
        for at, (source, held) in enumerate(
            ((x_hbm.at[pl.ds(first, group)], x_held), (last_mixed, mixed_held), (last_grid, grid_held))
        )
    ]
    for copy in last:
        copy.start()
    for sample in range(batch):
        for copy in reads(sample):
            copy.start()
    for copy in last:
        copy.wait()

    back_tile = row_tile(rows, 144)
    for k in range(group):

        @pl.loop(0, rows // back_tile)
        def _(i, k=k):
            where = pl.ds(pl.multiple_of(i * back_tile, 8), back_tile)
            gin_held[first + k, where, :] = norm_step(
                x_held[k, where, :],
                jnp.concatenate([mixed_held[k, h, where, :] for h in range(halves)], axis=1),
                jnp.concatenate([grid_held[k, h, where, :] for h in range(halves)], axis=1),
                skip[...],
                gain[...],
            )

        gin_write(first + k).start()

    for sample in range(batch):
        for read, write in zip(reads(sample), writes(sample)):
            read.wait()
            write.start()

    def tile(base, height, q):
        return total[pl.ds(base + q * height, height), :].astype(jnp.float32)

    hidden_rows = width * hidden // LANES
    vector_rows = 2 * hidden_rows + width * width // LANES

    for q in range(hidden // LANES):
        where = pl.ds(q * LANES, LANES)
        grad_in[:, where] = tile(0, width, q)
        grad_out[where, :] = tile(hidden_rows, width, q).T
        in_bias[:, where] = jnp.sum(tile(vector_rows, 8, q), axis=0, keepdims=True)
    for q in range(halves):
        where = pl.ds(q * LANES, LANES)
        grad_skip[:, where] = tile(2 * hidden_rows, width, q)
        for which in range(3):
            at = vector_rows + 8 * (hidden + which * width) // LANES
            vectors[which, :, where] = jnp.sum(tile(at, 8, q), axis=0, keepdims=True)
        all_normed, everything = (small[pl.ds(norm_at + which * halves + q, 1), :] for which in range(2))
        vectors[3, :, where] = (all_normed - bias[:, where] * everything) / gain[:, where]
        vectors[4, :, where] = everything
    place = lax.rem(lax.axis_index("lon"), group)
    for which in range(2):
        turned = small[pl.ds(which * degrees, degrees), :].T
        for q in range(group):

            @pl.when(place == q)
            def _(q=q, which=which, turned=turned):
                grad_spec[which] = turned[q * narrow : (q + 1) * narrow, :]

    for sample in range(batch):
        for write in writes(sample):
            write.wait()
    for k in range(group):
        gin_write(first + k).wait()


def per_device(
    lat,
    lon,
    inputs,
    legendre_forward,
    legendre_inverse,
    spectral_weight,
    skip_weight,
    gain_first,
    bias_first,
    gain_second,
    bias_second,
    mlp_in,
    mlp_in_bias,
    mlp_out,
    mlp_out_bias,
    cotangent,
):
    batch, band, columns, width = inputs.shape
    points = columns * lon
    slab, degrees, lats = legendre_forward.shape
    orders = slab * lat
    hidden = mlp_in.shape[1]
    rows = columns * band
    padded = -(-rows // 16) * 16
    halves = width // LANES
    group = lon // halves
    chunks = batch // group

    forward, inverse = fourier_tables(points, orders, lat)
    high, each = split_orders(orders, lat)
    near = lat // 2
    low_rows = degrees - high
    block = 2 * each * band
    waves = 2 * orders
    pack_rows = sum(low_rows - near * i // 8 * 8 for i in range(each))
    my_lon = lax.axis_index("lon")
    hidden = mlp_in.shape[1]
    flat_rows = (2 * hidden + width) * width // LANES + 8 * (hidden + 3 * width) // LANES
    share = -(-flat_rows // (16 * lat * lon)) * 16
    total_rows = share * lat * lon
    spec_rows = -(-2 * degrees // (8 * lat)) * 8

    def flat(values):
        return values.transpose(0, 2, 1, 3).reshape(batch, rows, width)

    def row(values):
        return values.reshape(1, -1)

    vmem = pl.BlockSpec(memory_space=pltpu.VMEM)
    hbm = pl.BlockSpec(memory_space=pl.ANY)
    fixed = pl.BlockSpec(memory_space=pltpu.HBM)
    low, full = jnp.bfloat16, jnp.float32
    results = pl.pallas_call(
        functools.partial(block_kernel, lat, lon),
        out_shape=(
            jax.ShapeDtypeStruct((batch, rows, width), low),
            jax.ShapeDtypeStruct((max(batch - group, 1), rows, width), full),
            jax.ShapeDtypeStruct((total_rows, LANES), low),
            jax.ShapeDtypeStruct((lat * spec_rows + 8, LANES), full),
            jax.ShapeDtypeStruct((group, halves, padded, LANES), low),
            jax.ShapeDtypeStruct((group, halves, padded, LANES), low),
        ),
        in_specs=[hbm, hbm] + [vmem] * 16,
        out_specs=(hbm,) * 6,
        scratch_shapes=[
            pltpu.VMEM((batch, rows, width), low),
            pltpu.VMEM((batch, halves, padded, LANES), low),
            pltpu.VMEM((chunks, lon, padded, LANES), low),
            pltpu.VMEM((chunks, lon, padded, LANES), low),
            pltpu.VMEM((batch, halves, padded, LANES), low),
            pltpu.VMEM((chunks, lat + near, block, LANES), low),
            pltpu.VMEM((chunks, lat + near, block, LANES), low),
            pltpu.VMEM((chunks, each, degrees, 2 * LANES), low),
            pltpu.VMEM((chunks, pack_rows, 2 * LANES), low),
            pltpu.VMEM((2, chunks, pack_rows, 2 * LANES), low),
            pltpu.VMEM((2, chunks, pack_rows, 2 * LANES), low),
            pltpu.VMEM((pack_rows, 2 * LANES), full),
            pltpu.VMEM((pack_rows, 2 * LANES), full),
            pltpu.VMEM((lat + near, block, LANES), low),
            pltpu.VMEM((lat + near, block, LANES), low),
            pltpu.VMEM((lon, padded, LANES), low),
            pltpu.VMEM((lat + near, block, LANES), low),
            pltpu.VMEM((lat + near, block, LANES), low),
            pltpu.VMEM((lon, padded, LANES), low),
            pltpu.VMEM((max(points, waves) * band, LANES), full),
            pltpu.VMEM((waves * band, LANES), full),
            pltpu.VMEM((group, rows, width), low),
            pltpu.VMEM((group, rows, width), low),
            pltpu.VMEM((group, rows, width), full),
            pltpu.SemaphoreType.DMA((10, chunks, group)),
            pltpu.SemaphoreType.DMA((12,)),
            pltpu.SemaphoreType.DMA((batch,)),
            pltpu.SemaphoreType.DMA((group,)),
            pltpu.SemaphoreType.DMA((group,)),
            pltpu.SemaphoreType.DMA((group,)),
            pltpu.VMEM((2, 2 * each, lats, degrees), low),
            pltpu.VMEM((each, degrees, lats), low),
            pltpu.VMEM((each, lats, degrees), low),
            pltpu.VMEM((each, lats, degrees), low),
            pltpu.VMEM((each, degrees, lats), low),
            pltpu.VMEM((each, low_rows, near * band), low),
            pltpu.VMEM((each, near * band, low_rows), low),
            pltpu.VMEM((each, near * band, low_rows), low),
            pltpu.VMEM((each, low_rows, near * band), low),
            pltpu.SemaphoreType.DMA((2,)),
            pltpu.SemaphoreType.DMA((2, slab, 2)),
            pltpu.VMEM((2, LANES, degrees), full),
            pltpu.VMEM((degrees, LANES), full),
            pltpu.VMEM((degrees, LANES), full),
            pltpu.VMEM((total_rows, LANES), full),
            pltpu.VMEM((1, total_rows // 2, LANES), full),
            pltpu.VMEM((1, total_rows // 4, LANES), full),
            pltpu.VMEM((max(lon // 2 - 1, 1), total_rows // (2 * lon), LANES), low),
            pltpu.VMEM((max(lat // 2 - 1, 1), share, LANES), low),
            pltpu.VMEM((total_rows // 4, LANES), low),
            pltpu.VMEM((total_rows // (2 * lon), LANES), low),
            pltpu.VMEM((share, LANES), low),
            pltpu.VMEM((lat * spec_rows, LANES), full),
            pltpu.VMEM((lat - 1, spec_rows, LANES), full),
            pltpu.VMEM((group, spec_rows, LANES), full),
            pltpu.VMEM((spec_rows, LANES), full),
            pltpu.VMEM((spec_rows, LANES), full),
            pltpu.VMEM((2, 8, LANES), full),
            pltpu.VMEM((8, width), full),
            pltpu.VMEM((3, 8, LANES), full),
            pltpu.VMEM((lon - 1, 8, LANES), full),
            pltpu.VMEM((lat - 1, 8, LANES), full),
            pltpu.SemaphoreType.DMA((2, group)),
            pltpu.SemaphoreType.DMA((2, 4)),
            pltpu.SemaphoreType.DMA((2, 4)),
            pltpu.SemaphoreType.DMA((2,)),
            pltpu.SemaphoreType.DMA((2,)),
            pltpu.SemaphoreType.DMA((2, group)),
            pltpu.SemaphoreType.DMA((2,)),
            pltpu.SemaphoreType.DMA((2, max(lat, lon) - 1)),
            pltpu.SemaphoreType.DMA((5,)),
        ],
        compiler_params=pltpu.CompilerParams(
            collective_id=0, has_side_effects=True, vmem_limit_bytes=63 * 2**20
        ),
    )(
        flat(inputs),
        flat(cotangent),
        jnp.asarray(forward),
        jnp.asarray(inverse),
        jnp.asarray(inverse.T),
        jnp.asarray(forward.T),
        legendre_forward.transpose(0, 2, 1),
        legendre_inverse,
        spectral_weight.transpose(0, 2, 1),
        skip_weight,
        mlp_in,
        mlp_out,
        row(gain_first),
        row(bias_first),
        row(gain_second),
        row(bias_second),
        row(mlp_in_bias),
        row(mlp_out_bias),
    )
    shapes = (
        ((batch, rows, width), low),
        ((batch, rows, width), full),
        ((2, width // lon, degrees), full),
        ((width, width), full),
        ((width, hidden), full),
        ((hidden, width), full),
        ((1, hidden), full),
        ((5, 1, width), full),
    )
    output, grad_inputs, grad_spec, grad_skip, grad_in, grad_out, in_bias, vectors = pl.pallas_call(
        functools.partial(result_kernel, group, width // lon, lat * spec_rows),
        out_shape=tuple(jax.ShapeDtypeStruct(*shape) for shape in shapes),
        in_specs=[fixed, fixed, vmem, vmem, fixed, fixed, fixed, vmem, vmem, vmem],
        out_specs=(fixed, fixed) + (vmem,) * 6,
        scratch_shapes=[
            pltpu.VMEM((batch, rows, width), full),
            pltpu.VMEM((batch, rows, width), low),
            pltpu.VMEM((group, rows, width), low),
            pltpu.VMEM((group, halves, padded, LANES), low),
            pltpu.VMEM((group, halves, padded, LANES), low),
            pltpu.SemaphoreType.DMA((4, batch)),
            pltpu.SemaphoreType.DMA((3,)),
        ],
        compiler_params=pltpu.CompilerParams(vmem_limit_bytes=48 * 2**20),
    )(*results, flat(inputs), skip_weight, row(gain_first), row(bias_first))

    def unflat(values):
        return values.reshape(batch, columns, band, width).transpose(0, 2, 1, 3)

    return (
        unflat(output),
        unflat(grad_inputs),
        grad_spec.transpose(0, 2, 1),
        grad_skip,
        vectors[3, 0],
        vectors[4, 0],
        vectors[1, 0],
        vectors[2, 0],
        grad_in,
        in_bias[0],
        grad_out,
        vectors[0, 0],
    )


def solution(mesh):
    lat, lon = mesh.shape["lat"], mesh.shape["lon"]
    grid = P(None, "lat", "lon", None)
    table = P("lat", None, None)
    channel = P(None, None, "lon")
    return jax.shard_map(
        functools.partial(per_device, lat, lon),
        mesh=mesh,
        in_specs=(grid, table, table, channel) + (P(),) * 9 + (grid,),
        out_specs=(grid, grid, channel) + (P(),) * 9,
        check_vma=False,
    )
```

```python
import functools
import math

import jax
import jax.numpy as jnp
import ml_dtypes
import numpy as np
from jax import lax
from jax.experimental import pallas as pl
from jax.experimental.pallas import tpu as pltpu
from jax.sharding import PartitionSpec as P

epsilon = 1e-05
LANES = 128
MESH = pl.DeviceIdType.MESH
root = math.sqrt(2.0 / math.pi)
cubic = 0.044715

OFFSET = {"1": 0, "2": 1, "3a": 3, "3b": 4, "4": 5, "5a": 6, "5b": 6, "6": 8, "7a": 10, "7b": 11, "8": 12, "9": 13}
ORDER = ("1", "3b", "3a", "7b", "7a", "4", "5a", "6", "2", "5b", "8", "9")


def split_orders(orders, lat):
    high = 2 * orders // 3
    each = high // lat
    assert each * lat == high and 3 * high == 2 * orders
    return high, each


def fourier_tables(points, orders, lat):
    waves = np.arange(orders)
    phase = (waves[:, None] * np.arange(points)[None, :] % points).astype(np.float32)
    phase = phase * np.float32(2.0 * math.pi / points)
    cosine, sine = np.cos(phase), np.sin(phase)
    factor = np.where(waves == 0, 1.0, 2.0).astype(np.float32)[:, None]
    high, each = split_orders(orders, lat)
    near = lat // 2
    owned = [[t * each + i for i in range(each)] for t in range(lat)]
    owned += [[high + near * i + d for i in range(each)] for d in range(near)]

    def arrange(*parts):
        stacked = [part[waves] for waves in owned for part in parts]
        return np.concatenate(stacked).astype(ml_dtypes.bfloat16)

    return arrange(cosine, -sine), arrange(factor * cosine, -factor * sine)


def row_tile(rows, most):
    fits = [t for t in range(16, most + 1, 16) if rows % t == 0]
    return fits[-1] if fits else rows


def norm_parts(values):
    center = values - jnp.mean(values, axis=-1, keepdims=True)
    spread = jnp.mean(center * center, axis=-1, keepdims=True)
    scaled = lax.rsqrt(spread + epsilon)
    return center * scaled, scaled


def norm_back(grad_out, normal, scaled, gain):
    grad_norm = grad_out * gain
    inner = jnp.mean(grad_norm, axis=-1, keepdims=True)
    cross = jnp.mean(grad_norm * normal, axis=-1, keepdims=True)
    return scaled * (grad_norm - inner - normal * cross)


def norm_step(values, mixed, sent, skip, gain):
    normal, scaled = norm_parts(values.astype(jnp.float32))
    grad_normed = dot_t(mixed, skip) + sent.astype(jnp.float32)
    return mixed.astype(jnp.float32) + norm_back(grad_normed, normal, scaled, gain)


def fold(values):
    rows, width = values.shape
    return jnp.sum(values.reshape(rows // 8, 8, width), axis=0)


def dot(a, b):
    return jnp.dot(a, b, preferred_element_type=jnp.float32)


def dot_t(a, b):
    return lax.dot_general(a, b, (((1,), (1,)), ((), ())), preferred_element_type=jnp.float32)


def t_dot(a, b):
    return lax.dot_general(a, b, (((0,), (0,)), ((), ())), preferred_element_type=jnp.float32)


def block_kernel(
    lat,
    lon,
    x_hbm,
    g_hbm,
    fwd_t,
    inv_t,
    inv,
    fwd,
    raw_ana,
    raw_syn,
    weight,
    skip,
    mlp_in,
    mlp_out,
    gain_one,
    bias_one,
    gain_two,
    bias_two,
    bias_in,
    bias_out,
    out_hbm,
    gin_hbm,
    total_hbm,
    small_hbm,
    last_mixed,
    last_grid,
    x_all,
    normed,
    lon_a,
    lon_c,
    lon_b,
    lat_a,
    lat_b,
    coeffs,
    coeffs_high,
    pack_own,
    pack_far,
    stack,
    stack_held,
    send_2,
    send_3,
    send_4,
    send_6,
    send_7,
    send_8,
    wide,
    slim,
    g_buf,
    o_buf,
    i_buf,
    recv_sem,
    send_sem,
    rows_sem,
    x_sem,
    g_sem,
    o_sem,
    i_sem,
    tabs,
    ana,
    ana_t,
    syn,
    syn_t,
    ana_high,
    ana_high_t,
    syn_high,
    syn_high_t,
    tab_recv,
    tab_send,
    w_parts,
    w_real,
    w_imag,
    acc,
    part_core,
    part_near,
    part_chip,
    part_far,
    wire_chip,
    wire_far,
    share,
    spec,
    spec_lat,
    spec_lon,
    spec_sum,
    spec_own,
    norm_sums,
    mixed_sums,
    norm_own,
    norm_lon,
    norm_lat,
    w_sem,
    fold_recv,
    fold_send,
    spec_recv,
    spec_send,
    spec_pair,
    norm_recv,
    norm_send,
    own_sem,
):
    batch, rows, width = x_hbm.shape
    halves = width // LANES
    group = lon // halves
    chunks = batch // group
    points = fwd_t.shape[1]
    slab, lats, degrees = raw_ana.shape
    narrow = width // lon
    hidden = mlp_in.shape[1]
    band = lats // lat
    waves = 2 * slab * lat
    high, each = split_orders(slab * lat, lat)
    near = lat // 2
    block = 2 * each * band
    slots = lat + near
    low_rows = degrees - high
    starts = [near * i // 8 * 8 for i in range(each)]
    packs = [sum(low_rows - start for start in starts[:i]) for i in range(each)]
    my_lat, my_lon = lax.axis_index("lat"), lax.axis_index("lon")
    mixed = normed
    my_side, my_near = my_lat // near, lax.rem(my_lat, near)
    half_tile = row_tile(rows, 144)
    full_tile = row_tile(rows, 240)

    def slot_of(chunk):
        return lax.rem(chunk, 2)

    def lon_copy(stage, chunk, src, dst, peer, member=0):
        return pltpu.make_async_remote_copy(
            src_ref=src,
            dst_ref=dst,
            send_sem=rows_sem.at[stage // 4, chunk] if stage in (1, 5) else send_sem.at[stage - 1, slot_of(chunk)],
            recv_sem=recv_sem.at[stage - 1, chunk, member],
            device_id={"lon": peer},
            device_id_type=MESH,
        )

    def lat_copy(send_at, recv_at, chunk, src, dst, peer):
        return pltpu.make_async_remote_copy(
            src_ref=src,
            dst_ref=dst,
            send_sem=send_sem.at[send_at, slot_of(chunk)],
            recv_sem=recv_sem.at[recv_at, chunk, 0],
            device_id={"lat": peer},
            device_id_type=MESH,
        )

    def own_copy(stage, chunk, src, dst):
        return pltpu.make_async_copy(src, dst, recv_sem.at[stage - 1, chunk, 0])

    def landed(stage, chunk, whole, member=0):
        pltpu.make_async_copy(whole, whole, recv_sem.at[stage - 1, chunk, member]).wait()

    def member_at(step):
        return lax.rem(my_lon // halves + step, group)

    def member_landed(stage, chunk, step):
        count = halves if step else halves - 1
        landed(stage, chunk, lon_a.at[chunk, pl.ds(0, count)], member_at(step))

    def sent(stage, chunk, part):
        lon_copy(stage, chunk, part, part, my_lon).wait_send()

    def x_load(sample):
        return pltpu.make_async_copy(x_hbm.at[sample], x_all.at[sample], x_sem.at[sample])

    def g_load(sample, slot):
        return pltpu.make_async_copy(g_hbm.at[sample], g_buf.at[slot], g_sem.at[slot])

    def o_store(sample, slot):
        return pltpu.make_async_copy(o_buf.at[slot], out_hbm.at[sample], o_sem.at[slot])

    def i_store(sample, slot):
        return pltpu.make_async_copy(i_buf.at[slot], gin_hbm.at[sample], i_sem.at[slot])

    def spread_rows(stage, chunk, held, sample, landing):
        src = chunk * group + sample
        for half in range(halves):
            peer = sample * halves + half

            @pl.when(peer != my_lon)
            def _(peer=peer, half=half):
                lon_copy(stage, chunk, held.at[src, half], landing.at[chunk, my_lon], peer).start()

            @pl.when(peer == my_lon)
            def _(half=half):
                own_copy(stage, chunk, held.at[src, half], landing.at[chunk, my_lon]).start()

    def spread_low(send_at, recv_at, chunk, buffer, target):
        for step in range(1, lat):
            peer = lax.rem(my_lat + step, lat)
            lat_copy(send_at, recv_at, chunk, buffer.at[peer], target.at[chunk, my_lat], peer).start()

    def spread_high(send_at, recv_at, chunk, buffer, target):
        for step in range(1, near):
            peer = lax.rem(my_near + step, near)
            src, dst = buffer.at[lat + peer], target.at[chunk, lat + my_near]
            lat_copy(send_at, recv_at, chunk, src, dst, my_side * near + peer).start()

    def own_rows(at):
        return pl.ds(pl.multiple_of(at * block, 16), block)

    def to_waves(stage, chunk, table, scale, buffer, landing):
        slot = slot_of(chunk)
        landed(stage - 1, chunk, landing.at[chunk])
        for source in range(lon):
            wide[pl.ds(source * rows, rows), :] = landing[chunk, source, pl.ds(0, rows), :].astype(jnp.float32)
        for first in range(0, band, 2):
            rhs = jnp.concatenate(
                [wide[pl.ds(first + k, points, stride=band), :] for k in range(2)], axis=1
            ).astype(jnp.bfloat16)
            got = dot(table[...], rhs)
            if scale is not None:
                got = got * scale
            for k in range(2):
                slim[pl.ds(first + k, waves, stride=band), :] = got[:, k * LANES : (k + 1) * LANES]

        @pl.when(chunk > 1)
        def _():
            sent(stage, chunk, buffer.at[slot, pl.ds(0, slots - 2)])

        for target in range(slots):
            buffer[slot, target] = slim[pl.ds(target * block, block), :].astype(jnp.bfloat16)
        spread_low(stage - 1, stage - 1, chunk, buffer.at[slot], lat_a)
        spread_high(stage - 1, stage - 1, chunk, buffer.at[slot], lat_a)
        lat_a[chunk, my_lat] = slim[own_rows(my_lat), :].astype(jnp.bfloat16)
        lat_a[chunk, lat + my_near] = slim[own_rows(lat + my_near), :].astype(jnp.bfloat16)

    def to_points(stage, chunk, table, scale, buffer):
        slot = slot_of(chunk)
        landed(stage - 1, chunk, lat_b.at[chunk, pl.ds(0, slots - 2)])
        for source in range(slots):
            slim[pl.ds(source * block, block), :] = lat_b[chunk, source].astype(jnp.float32)
        for first in range(0, band, 2):
            rhs = jnp.concatenate(
                [slim[pl.ds(first + k, waves, stride=band), :] for k in range(2)], axis=1
            ).astype(jnp.bfloat16)
            got = dot(table[...], rhs)
            if scale is not None:
                got = got * scale
            for k in range(2):
                wide[pl.ds(first + k, points, stride=band), :] = got[:, k * LANES : (k + 1) * LANES]

        @pl.when(chunk > 1)
        def _():
            sent(stage, chunk, buffer.at[slot, pl.ds(0, lon - 1)])

        for target in range(lon):
            grid = wide[pl.ds(target * rows, rows), :]
            buffer[slot, target, pl.ds(0, rows), :] = grid.astype(jnp.bfloat16)
            if stage == 8:
                before = lon_a[chunk, target, pl.ds(0, rows), :].astype(jnp.float32)
                norm_sums[0] += fold(grid * before)
                norm_sums[1] += fold(grid)
        member, half = my_lon // halves, lax.rem(my_lon, halves)

        def send(landing):
            for step in range(1, lon):
                peer = lax.rem(my_lon + step, lon)
                lon_copy(stage, chunk, buffer.at[slot, peer], landing, peer, member).start()

        def send_here():
            send(lon_b.at[chunk * group + member, half])
            own = pl.ds(pl.multiple_of(my_lon * rows, 8), rows)
            lon_b[chunk * group + member, half, pl.ds(0, rows), :] = wide[own, :].astype(jnp.bfloat16)

        if stage == 4:
            send_here()
        else:
            pl.when(chunk < chunks - 1)(send_here)

            @pl.when(chunk == chunks - 1)
            def _():
                norm_start()
                send(last_grid.at[member, half])
                last_own().start()

    def last_own():
        held = last_grid.at[my_lon // halves, lax.rem(my_lon, halves)]
        return pltpu.make_async_copy(send_8.at[(chunks - 1) % 2, my_lon], held, own_sem.at[3])

    def last_mixed_copy():
        part = mixed.at[pl.ds((chunks - 1) * group, group)]
        return pltpu.make_async_copy(part, last_mixed, own_sem.at[4])

    def wave_rows(first, count, i):
        parts = []
        for r in range(2):
            at = (r * each + i) * band
            held = [slim[pl.ds(s * block + at, band), :] for s in range(first, first + count)]
            parts.append(jnp.concatenate(held, axis=0))
        return jnp.concatenate(parts, axis=1).astype(jnp.bfloat16)

    def put_rows(got, count, i):
        for r in range(2):
            at = (r * each + i) * band
            for t in range(count):
                wide[pl.ds(t * block + at, band), :] = got[
                    t * band : (t + 1) * band, r * LANES : (r + 1) * LANES
                ]

    def pack_copy(k, chunk):
        peer = lax.rem(my_lat + near, lat)
        return lat_copy(10 + k, 8 + k, chunk, pack_own.at[k, chunk], pack_far.at[k, chunk], peer)

    def slab_first(stage, k, chunk, tables, between, buffer):
        first_table, second_table, high_table = tables
        slot = slot_of(chunk)
        landed(stage - 1, chunk, lat_a.at[chunk, pl.ds(0, slots - 2)])
        for source in range(slots):
            slim[pl.ds(source * block, block), :] = lat_a[chunk, source].astype(jnp.float32)
        for i in range(each):
            got = dot(high_table[i], wave_rows(lat, near, i))
            stack[pl.ds(packs[i], low_rows - starts[i]), :] = got[starts[i] :, :]

        @pl.when(chunk > 1)
        def _():
            pack_copy(k, chunk).wait_send()

        pack_own[k, chunk] = stack[...].astype(jnp.bfloat16)
        pack_copy(k, chunk).start()
        for m in range(each):
            real, imag = between(m, dot(first_table[m], wave_rows(0, lat, m)))
            low = jnp.concatenate([real, imag], axis=1).astype(jnp.bfloat16)
            put_rows(dot(second_table[m], low), lat, m)

        @pl.when(chunk > 1)
        def _():
            sent(stage, chunk, buffer.at[slot, pl.ds(0, lat - 1)])

        for target in range(lat):
            buffer[slot, target] = wide[pl.ds(target * block, block), :].astype(jnp.bfloat16)
        spread_low(stage - 1, stage - 1, chunk, buffer.at[slot], lat_b)
        lat_b[chunk, my_lat] = wide[own_rows(my_lat), :].astype(jnp.bfloat16)

    def slab_second(stage, k, chunk, table, before, between, buffer):
        slot = slot_of(chunk)
        landed(9 + k, chunk, pack_far.at[k, chunk])
        stack[...] = pack_own[k, chunk].astype(jnp.float32) + pack_far[k, chunk].astype(jnp.float32)
        before()
        for i in range(each):
            count = low_rows - starts[i]
            real, imag = between(pl.ds(packs[i], count), high + starts[i], count)
            low = jnp.concatenate([real, imag], axis=1)
            if starts[i]:
                low = jnp.concatenate([jnp.zeros((starts[i], 2 * LANES), jnp.float32), low], axis=0)
            put_rows(dot(table[i], low.astype(jnp.bfloat16)), near, i)

        if near > 1:

            @pl.when(chunk > 1)
            def _():
                sent(9 + k, chunk, buffer.at[slot, pl.ds(lat, near - 1)])

        for target in range(near):
            buffer[slot, lat + target] = wide[pl.ds(target * block, block), :].astype(jnp.bfloat16)
        spread_high(8 + k, stage - 1, chunk, buffer.at[slot], lat_b)
        lat_b[chunk, lat + my_near] = wide[own_rows(my_near), :].astype(jnp.bfloat16)

    hidden_rows = width * hidden // LANES
    vector_rows = 2 * hidden_rows + width * width // LANES

    def gather_rows(base, values):
        count = values.shape[0]
        for q in range(values.shape[1] // LANES):
            acc[pl.ds(base + q * count, count), :] += values[:, q * LANES : (q + 1) * LANES]

    def both(held, sample, where):
        return jnp.concatenate([held[sample, h, where, :] for h in range(halves)], axis=1)

    def normalize(sample):
        x_load(sample).wait()

        @pl.loop(0, rows // half_tile)
        def _(i):
            where = pl.ds(pl.multiple_of(i * half_tile, 8), half_tile)
            normal, _ = norm_parts(x_all[sample, where, :].astype(jnp.float32))
            low = (normal * gain_one[...] + bias_one[...]).astype(jnp.bfloat16)
            for h in range(halves):
                normed[sample, h, where, :] = low[:, h * LANES : (h + 1) * LANES]

    def stage_1(chunk):
        for step in reversed(range(group)):
            k = member_at(step)

            @pl.when(chunk > 0)
            def _(k=k):
                normalize(chunk * group + k)

            spread_rows(1, chunk, normed, k, lon_a)

    def stage_2(chunk):
        to_waves(2, chunk, fwd_t, 1.0 / points, send_2, lon_a)

    def filtered(real, imag, rows):
        wr, wi = w_real[rows, :], w_imag[rows, :]
        return wr * real - wi * imag, wr * imag + wi * real

    def stage_3a(chunk):
        def between(m, got):
            coeffs[chunk, m] = got.astype(jnp.bfloat16)
            return filtered(got[:, :LANES], got[:, LANES:], pl.ds(0, degrees))

        slab_first(3, 0, chunk, (ana, syn, ana_high), between, send_3)

    def stage_3b(chunk):
        def before():
            coeffs_high[chunk] = stack[...].astype(jnp.bfloat16)

        def between(where, degree, count):
            got = stack[where, :]
            return filtered(got[:, :LANES], got[:, LANES:], pl.ds(degree, count))

        slab_second(3, 0, chunk, syn_high, before, between, send_3)

    def stage_4(chunk):
        to_points(4, chunk, inv, None, send_4)

    def stage_5a(chunk):
        sent(1, chunk, lon_a.at[chunk, pl.ds(0, lon - 1)])
        feed_forward(chunk, range(group // 2))

    def stage_5b(chunk):
        feed_forward(chunk, range(group // 2, group))

    def feed_forward(chunk, steps):
        for step in steps:
            member_landed(4, chunk, step)
            k = member_at(step)
            sample = chunk * group + k
            g_load(sample, k).wait()

            @pl.when(chunk > 0)
            def _(sample=sample, k=k):
                o_store(sample, k).wait()

            @pl.loop(0, rows // full_tile)
            def _(i):
                where = pl.ds(pl.multiple_of(i * full_tile, 8), full_tile)
                low_one = both(normed, sample, where)
                spatial = both(lon_b, sample, where).astype(jnp.float32)
                resid = x_all[sample, where, :].astype(jnp.float32) + (spatial + dot(low_one, skip[...]))
                normal, scaled = norm_parts(resid)
                low_two = (normal * gain_two[...] + bias_two[...]).astype(jnp.bfloat16)
                pre = dot(low_two, mlp_in[...]) + bias_in[...]
                square = pre * pre
                curve = jnp.tanh(root * pre * (1.0 + cubic * square))
                lifted = 0.5 + 0.5 * curve
                act = (pre * lifted).astype(jnp.bfloat16)
                slope = lifted + (0.5 * root) * pre * (1.0 - curve * curve) * (1.0 + (3.0 * cubic) * square)
                o_buf[k, where, :] = (resid + dot(act, mlp_out[...]) + bias_out[...]).astype(jnp.bfloat16)
                g_low = g_buf[k, where, :]
                gather_rows(hidden_rows, t_dot(g_low, act))
                grad_pre = (dot_t(g_low, mlp_out[...]) * slope).astype(jnp.bfloat16)
                gather_rows(0, t_dot(low_two, grad_pre))
                gather_rows(vector_rows, fold(grad_pre.astype(jnp.float32)))
                grad_second = dot_t(grad_pre, mlp_in[...])
                g_full = g_low.astype(jnp.float32)
                for at, values in enumerate((g_full, grad_second * normal, grad_second)):
                    gather_rows(vector_rows + 8 * (hidden + at * width) // LANES, fold(values))
                grad_mixed = (g_full + norm_back(grad_second, normal, scaled, gain_two[...])).astype(jnp.bfloat16)
                gather_rows(2 * hidden_rows, t_dot(low_one, grad_mixed))
                mixed_sums[...] += fold(grad_mixed.astype(jnp.float32))
                for h in range(halves):
                    mixed[sample, h, where, :] = grad_mixed[:, h * LANES : (h + 1) * LANES]

            o_store(sample, k).start()

            @pl.when(chunk < chunks - 1)
            def _(sample=sample, k=k):
                g_load(sample + group, k).start()

            spread_rows(5, chunk, mixed, k, lon_c)

    def stage_6(chunk):
        to_waves(6, chunk, inv_t, None, send_6, lon_c)

    def unfiltered(got, held, degree, count, share_of):
        dr, di = got[:, :LANES], got[:, LANES:]
        ar, ai = held[:, :LANES], held[:, LANES:]
        spec[pl.ds(degree, count), :] += share_of * (dr * ar + di * ai)
        spec[pl.ds(degrees + degree, count), :] += share_of * (di * ar - dr * ai)
        wr, wi = w_real[pl.ds(degree, count), :], w_imag[pl.ds(degree, count), :]
        return wr * dr + wi * di, wr * di - wi * dr

    def stage_7a(chunk):
        def between(m, got):
            return unfiltered(got, coeffs[chunk, m].astype(jnp.float32), 0, degrees, 1.0)

        slab_first(7, 1, chunk, (syn_t, ana_t, syn_high_t), between, send_7)

    def stage_7b(chunk):
        def before():
            stack_held[...] = coeffs_high[chunk].astype(jnp.float32)

        def between(where, degree, count):
            return unfiltered(stack[where, :], stack_held[where, :], degree, count, 0.5)

        slab_second(7, 1, chunk, ana_high_t, before, between, send_7)

    def stage_8(chunk):
        to_points(8, chunk, fwd, 1.0 / points, send_8)

    def stage_9(chunk):
        for step in range(group):
            member_landed(8, chunk, step)
            k = member_at(step)
            sample = chunk * group + k

            @pl.when(chunk > 0)
            def _(sample=sample, k=k):
                i_store(sample, k).wait()

            @pl.loop(0, rows // half_tile)
            def _(i):
                where = pl.ds(pl.multiple_of(i * half_tile, 8), half_tile)
                i_buf[k, where, :] = norm_step(
                    x_all[sample, where, :],
                    both(mixed, sample, where),
                    both(lon_b, sample, where),
                    skip[...],
                    gain_one[...],
                )

            i_store(sample, k).start()

    def weight_copies(start):
        place = lax.rem(my_lon, group)
        held = w_parts.at[:, pl.ds(pl.multiple_of(place * narrow, 8), narrow), :]
        for q in range(group):
            peer = my_lon // group + halves * q

            @pl.when(peer != my_lon)
            def _(peer=peer, q=q):
                copy = pltpu.make_async_remote_copy(
                    src_ref=weight,
                    dst_ref=held,
                    send_sem=w_sem.at[1, q],
                    recv_sem=w_sem.at[0, place],
                    device_id={"lon": peer},
                    device_id_type=MESH,
                )
                if start:
                    copy.start()
                else:
                    copy.wait_send()

            if start:

                @pl.when(peer == my_lon)
                def _():
                    pltpu.make_async_copy(weight, held, w_sem.at[0, place]).start()

    def table_copies(start):
        def one(i, carry):
            wave = my_lat * slab + i

            def give(peer, slot, way):
                for which, raw in enumerate((raw_ana, raw_syn)):

                    @pl.when(peer != my_lat)
                    def _(which=which, raw=raw):
                        copy = pltpu.make_async_remote_copy(
                            src_ref=raw.at[i],
                            dst_ref=tabs.at[which, slot],
                            send_sem=tab_send.at[which, i, way],
                            recv_sem=tab_recv.at[which],
                            device_id={"lat": peer},
                            device_id_type=MESH,
                        )
                        if start:
                            copy.start()
                        else:
                            copy.wait_send()

                    if start:

                        @pl.when(peer == my_lat)
                        def _(which=which, raw=raw):
                            pltpu.make_async_copy(raw.at[i], tabs.at[which, slot], tab_recv.at[which]).start()

            @pl.when(wave < high)
            def _():
                give(lax.div(wave, each), lax.rem(wave, each), 0)

            @pl.when(wave >= high)
            def _():
                above = wave - high
                for side in range(2):
                    give(side * near + lax.rem(above, near), each + lax.div(above, near), side)

            return carry

        lax.fori_loop(0, slab, one, 0)

    def build():
        acc[...] = jnp.zeros_like(acc)
        spec[...] = jnp.zeros_like(spec)
        norm_sums[...] = jnp.zeros_like(norm_sums)
        mixed_sums[...] = jnp.zeros_like(mixed_sums)
        norm_own[...] = jnp.zeros_like(norm_own)
        degree = lax.broadcasted_iota(jnp.int32, (lats, degrees), 1)
        for which in range(2):
            pltpu.make_async_copy(tabs.at[which], tabs.at[which], tab_recv.at[which]).wait()
        kinds = ((ana_t, ana, ana_high_t, ana_high), (syn, syn_t, syn_high, syn_high_t))

        @pl.loop(0, each)
        def _(i):
            half = pl.ds(pl.multiple_of(my_side * near * band, 16), near * band)
            for which, (plain, turned, part, part_turned) in enumerate(kinds):
                values = tabs[which, i].astype(jnp.float32)
                values = jnp.where(degree >= my_lat * each + i, values, 0.0)
                plain[i] = values.astype(jnp.bfloat16)
                turned[i] = values.T.astype(jnp.bfloat16)
                values = tabs[which, each + i, half, :].astype(jnp.float32)
                values = jnp.where(degree[: near * band] >= high + near * i + my_near, values, 0.0)
                values = values.T[high:, :]
                part_turned[i] = values.astype(jnp.bfloat16)
                part[i] = values.T.astype(jnp.bfloat16)

        for q in range(group):
            part = w_parts.at[:, pl.ds(q * narrow, narrow), :]
            pltpu.make_async_copy(part, part, w_sem.at[0, q]).wait()
        w_real[...] = w_parts[0].T
        w_imag[...] = w_parts[1].T

    total_rows = acc.shape[0]
    place_core, place_chip = lax.rem(my_lon, 2), my_lon // 2
    place_near, place_far = lax.rem(my_lat, 2), my_lat // 2
    levels = (
        (2, place_core, part_core, None, lambda p: {"lon": 2 * place_chip + p}),
        (2, place_near, part_near, None, lambda p: {"lat": 2 * place_far + p}),
        (lon // 2, place_chip, part_chip, wire_chip, lambda p: {"lon": 2 * p + place_core}),
        (lat // 2, place_far, part_far, wire_far, lambda p: {"lat": 2 * p + place_near}),
    )
    bases, sizes = [0], [total_rows]
    for count, place, _, _, _ in levels:
        sizes.append(sizes[-1] // count)
        bases.append(bases[-1] + place * sizes[-1])

    def row_part(at, count):
        return pl.ds(pl.multiple_of(at, 16), count)

    def fold_start(k):
        count, place, parts, wire, device = levels[k]
        if wire is not None:
            wire[...] = acc[row_part(bases[k], sizes[k]), :].astype(jnp.bfloat16)
        for step in range(1, count):
            peer = lax.rem(place + step, count)
            if wire is None:
                src = acc.at[row_part(bases[k] + peer * sizes[k + 1], sizes[k + 1]), :]
            else:
                src = wire.at[row_part(peer * sizes[k + 1], sizes[k + 1]), :]
            pltpu.make_async_remote_copy(
                src_ref=src,
                dst_ref=parts.at[step - 1],
                send_sem=fold_send.at[0, k],
                recv_sem=fold_recv.at[0, k],
                device_id=device(peer),
                device_id_type=MESH,
            ).start()

    def fold_end(k):
        count, _, parts, _, _ = levels[k]
        if count == 1:
            return
        pltpu.make_async_copy(parts, parts, fold_recv.at[0, k]).wait()
        got = parts[0].astype(jnp.float32)
        for step in range(2, count):
            got = got + parts[step - 1].astype(jnp.float32)
        acc[row_part(bases[k + 1], sizes[k + 1]), :] += got

    def spread_start(k):
        count, place, _, _, device = levels[k]
        own = row_part(bases[k + 1], sizes[k + 1])
        src = total_hbm.at[own, :]
        if k == len(levels) - 1:
            share[...] = acc[own, :].astype(jnp.bfloat16)
            src = share
            pltpu.make_async_copy(share, total_hbm.at[own, :], own_sem.at[0]).start()
        for step in range(1, count):
            pltpu.make_async_remote_copy(
                src_ref=src,
                dst_ref=total_hbm.at[own, :],
                send_sem=fold_send.at[1, k],
                recv_sem=fold_recv.at[1, k],
                device_id=device(lax.rem(place + step, count)),
                device_id_type=MESH,
            ).start()

    def spread_end(k):
        count = levels[k][0]
        if count > 1:
            all_parts = total_hbm.at[pl.ds(0, (count - 1) * sizes[k + 1]), :]
            pltpu.make_async_copy(all_parts, all_parts, fold_recv.at[1, k]).wait()
        if k == len(levels) - 1:
            own = row_part(bases[k + 1], sizes[k + 1])
            pltpu.make_async_copy(share, total_hbm.at[own, :], own_sem.at[0]).wait()

    def fold_sent():
        for k, (count, _, _, wire, _) in enumerate(levels):
            for way, held in ((0, acc if wire is None else wire), (1, total_hbm)):
                if count == 1:
                    continue
                part = held.at[pl.ds(0, (count - 1) * sizes[k + 1]), :]
                pltpu.make_async_remote_copy(
                    src_ref=part,
                    dst_ref=part,
                    send_sem=fold_send.at[way, k],
                    recv_sem=fold_recv.at[way, k],
                    device_id={"lon": my_lon},
                    device_id_type=MESH,
                ).wait_send()

    spec_rows = spec_sum.shape[0]

    def spec_part(at):
        return pl.ds(pl.multiple_of(at * spec_rows, 8), spec_rows)

    def spec_lat_copies(way, src, dst):
        for step in range(1, lat):
            peer = lax.rem(my_lat + step, lat)
            pltpu.make_async_remote_copy(
                src_ref=src(peer),
                dst_ref=dst(step),
                send_sem=spec_send.at[way],
                recv_sem=spec_recv.at[way],
                device_id={"lat": peer},
                device_id_type=MESH,
            ).start()

    def spec_start():
        spec_lat_copies(
            0, lambda p: spec.at[spec_part(p), :], lambda s: spec_lat.at[s - 1]
        )

    def spec_pairs(action):
        half = lax.rem(my_lon, halves)
        for q in range(group):
            target = half * group + q

            @pl.when(target != my_lon)
            def _(target=target, q=q):
                copy = pltpu.make_async_remote_copy(
                    src_ref=spec_sum,
                    dst_ref=spec_lon.at[my_lon // halves],
                    send_sem=spec_pair.at[1, q],
                    recv_sem=spec_pair.at[0, my_lon // halves],
                    device_id={"lon": target},
                    device_id_type=MESH,
                )
                if action == "start":
                    copy.start()
                else:
                    copy.wait_send()

            if action == "start":

                @pl.when(target == my_lon)
                def _():
                    pltpu.make_async_copy(
                        spec_sum, spec_lon.at[my_lon // halves], spec_pair.at[0, my_lon // halves]
                    ).start()

    def spec_middle():
        pltpu.make_async_copy(spec_lat, spec_lat, spec_recv.at[0]).wait()
        got = spec[spec_part(my_lat), :]
        for step in range(1, lat):
            got = got + spec_lat[step - 1]
        spec_sum[...] = got
        spec_pairs("start")

    def spec_back():
        for q in range(group):
            pltpu.make_async_copy(spec_lon.at[q], spec_lon.at[q], spec_pair.at[0, q]).wait()
        got = spec_lon[0]
        for q in range(1, group):
            got = got + spec_lon[q]
        spec_own[...] = got
        own = spec_part(my_lat)
        spec_lat_copies(1, lambda p: spec_own, lambda s: small_hbm.at[own, :])
        pltpu.make_async_copy(spec_own, small_hbm.at[own, :], own_sem.at[1]).start()

    def spec_end():
        pltpu.make_async_copy(spec_own, small_hbm.at[spec_part(my_lat), :], own_sem.at[1]).wait()
        part = spec.at[pl.ds(0, (lat - 1) * spec_rows), :]
        pltpu.make_async_copy(part, part, spec_recv.at[1]).wait()
        for way in range(2):
            pltpu.make_async_remote_copy(
                src_ref=part,
                dst_ref=part,
                send_sem=spec_send.at[way],
                recv_sem=spec_recv.at[way],
                device_id={"lat": my_lat},
                device_id_type=MESH,
            ).wait_send()
        spec_pairs("end")

    def norm_copies(way, axis, count, place, src, parts, action):
        for step in range(1, count):
            copy = pltpu.make_async_remote_copy(
                src_ref=src,
                dst_ref=parts.at[step - 1],
                send_sem=norm_send.at[way, step - 1],
                recv_sem=norm_recv.at[way],
                device_id={axis: lax.rem(place + step, count)},
                device_id_type=MESH,
            )
            if action == "start":
                copy.start()
            else:
                copy.wait_send()

    def norm_end(way, parts, count):
        pltpu.make_async_copy(parts, parts, norm_recv.at[way]).wait()
        got = norm_own[way]
        for step in range(1, count):
            got = got + parts[step - 1]
        norm_own[way + 1] = got

    def norm_skip():
        lines = [jnp.zeros((1, width), jnp.float32) for _ in range(2)]
        all_mixed = jnp.sum(mixed_sums[...], axis=0, keepdims=True)
        for q in range(halves):
            lanes = slice(q * LANES, (q + 1) * LANES)
            part = skip[:, lanes].astype(jnp.float32)
            held = acc[pl.ds(2 * hidden_rows + q * width, width), :]
            for which, values in enumerate((held, all_mixed[:, lanes])):
                lines[which] += jnp.sum((part * values).T, axis=0, keepdims=True)
        for which in range(2):
            for half in range(halves):
                norm_own[0, pl.ds(which * halves + half, 1), :] = lines[which][
                    :, half * LANES : (half + 1) * LANES
                ]

    def norm_start():
        for half in range(halves):

            @pl.when(lax.rem(my_lon, halves) == half)
            def _(half=half):
                for which in range(2):
                    line = jnp.sum(norm_sums[which], axis=0, keepdims=True)
                    norm_own[0, pl.ds(which * halves + half, 1), :] += line

        norm_copies(0, "lon", lon, my_lon, norm_own.at[0], norm_lon, "start")

    def norm_middle():
        norm_end(0, norm_lon, lon)
        norm_copies(1, "lat", lat, my_lat, norm_own.at[1], norm_lat, "start")

    def norm_finish():
        norm_end(1, norm_lat, lat)
        where = pl.ds(lat * spec_rows, 8)
        copy = pltpu.make_async_copy(norm_own.at[2], small_hbm.at[where, :], own_sem.at[2])
        copy.start()
        norm_copies(0, "lon", lon, my_lon, norm_own.at[0], norm_lon, "end")
        norm_copies(1, "lat", lat, my_lat, norm_own.at[1], norm_lat, "end")
        copy.wait()

    def last_mixed_start():
        last_mixed_copy().start()

    def run(*steps):
        def go():
            for step, k in steps:
                step() if k is None else step(k)

        return go

    end = chunks - 1
    aside = {
        (0, "1"): build,
        (end + 6, "5b"): run((last_mixed_start, None), (norm_skip, None), (fold_start, 0)),
        (end + 7, "7b"): run((fold_end, 0), (fold_start, 1)),
        (end + 7, "9"): run((fold_end, 1), (fold_start, 2)),
        (end + 8, "6"): run((fold_end, 2), (fold_start, 3)),
        (end + 9, "7a"): run((fold_end, 3), (spread_start, 3)),
        (end + 10, "7b"): run((spread_end, 3), (spread_start, 2)),
        (end + 11, "7b"): run((spread_end, 2), (spread_start, 1), (spec_start, None)),
        (end + 12, "8"): run((spread_end, 1), (spread_start, 0), (norm_middle, None), (spec_back, None)),
        (end + 11, "9"): run((spec_middle, None)),
    }

    stages = {
        "1": stage_1,
        "2": stage_2,
        "3a": stage_3a,
        "3b": stage_3b,
        "4": stage_4,
        "5a": stage_5a,
        "5b": stage_5b,
        "6": stage_6,
        "7a": stage_7a,
        "7b": stage_7b,
        "8": stage_8,
        "9": stage_9,
    }

    for sample in range(group):
        x_load(sample).start()

    padded = lon_a.shape[2]
    if padded > rows:
        normed[:, :, rows:, :] = jnp.zeros_like(normed[:, :, rows:, :])
        for held in (send_4, send_8):
            held[:, :, rows:, :] = jnp.zeros_like(held[:, :, rows:, :])
    barrier = pltpu.get_barrier_semaphore()
    for step in range(1, lon):
        pl.semaphore_signal(
            barrier, inc=1, device_id={"lon": lax.rem(my_lon + step, lon)}, device_id_type=MESH
        )
    for step in range(1, lat):
        pl.semaphore_signal(
            barrier, inc=1, device_id={"lat": lax.rem(my_lat + step, lat)}, device_id_type=MESH
        )
    for k in range(group):
        normalize(k)
    for sample in range(group, batch):
        x_load(sample).start()
    for k in range(group):
        g_load(k, k).start()
    pl.semaphore_wait(barrier, lon - 1 + lat - 1)

    weight_copies(True)
    table_copies(True)

    def tick(now, carry):
        for stage in ORDER:
            chunk = now - OFFSET[stage]

            @pl.when(jnp.logical_and(chunk >= 0, chunk < (end if stage == "9" else chunks)))
            def _(stage=stage, chunk=chunk):
                stages[stage](chunk)

            for (when, after), action in aside.items():
                if after == stage:
                    pl.when(now == when)(action)

        return carry

    lax.fori_loop(0, chunks + max(OFFSET.values()), tick, 0)

    spread_end(0)
    norm_finish()
    spec_end()
    fold_sent()
    for step in range(group):
        member_landed(8, end, step)
    last_own().wait()
    last_mixed_copy().wait()
    weight_copies(False)
    table_copies(False)
    last = chunks - 1
    for chunk in range(chunks):
        sent(5, chunk, lon_a.at[chunk, pl.ds(0, lon - 1)])
    for chunk in range(max(chunks - 2, 0), chunks):
        for stage, buffer, count in (
            (2, send_2, slots - 2),
            (3, send_3, lat - 1),
            (4, send_4, lon - 1),
            (6, send_6, slots - 2),
            (7, send_7, lat - 1),
            (8, send_8, lon - 1),
            (9, send_3, near - 1),
            (10, send_7, near - 1),
        ):
            if count:
                sent(stage, chunk, buffer.at[chunk % 2, pl.ds(0, count)])
        for k in range(2):
            pack_copy(k, chunk).wait_send()
    for k in range(group):
        o_store(last * group + k, k).wait()
        if chunks > 1:
            i_store((last - 1) * group + k, k).wait()


def result_kernel(
    group,
    narrow,
    norm_at,
    out_from,
    gin_from,
    total,
    small,
    last_mixed,
    last_grid,
    x_hbm,
    skip,
    gain,
    bias,
    out_to,
    gin_to,
    grad_spec,
    grad_skip,
    grad_in,
    grad_out,
    in_bias,
    vectors,
    gin_held,
    out_held,
    x_held,
    mixed_held,
    grid_held,
    sems,
    last_sems,
):
    batch, rows, width = out_from.shape
    hidden = grad_in.shape[1]
    halves = width // LANES
    degrees = grad_spec.shape[2]
    first = batch - group

    def reads(sample):
        out = pltpu.make_async_copy(out_from.at[sample], out_held.at[sample], sems.at[1, sample])
        if sample >= first:
            return (out,)
        return (pltpu.make_async_copy(gin_from.at[sample], gin_held.at[sample], sems.at[0, sample]), out)

    def gin_write(sample):
        return pltpu.make_async_copy(gin_held.at[sample], gin_to.at[sample], sems.at[2, sample])

    def writes(sample):
        out = pltpu.make_async_copy(out_held.at[sample], out_to.at[sample], sems.at[3, sample])
        return (out,) if sample >= first else (gin_write(sample), out)

    last = [
        pltpu.make_async_copy(source, held, last_sems.at[at])
        for at, (source, held) in enumerate(
            ((x_hbm.at[pl.ds(first, group)], x_held), (last_mixed, mixed_held), (last_grid, grid_held))
        )
    ]
    for copy in last:
        copy.start()
    for sample in range(batch):
        for copy in reads(sample):
            copy.start()
    for copy in last:
        copy.wait()

    back_tile = row_tile(rows, 144)
    for k in range(group):

        @pl.loop(0, rows // back_tile)
        def _(i, k=k):
            where = pl.ds(pl.multiple_of(i * back_tile, 8), back_tile)
            gin_held[first + k, where, :] = norm_step(
                x_held[k, where, :],
                jnp.concatenate([mixed_held[k, h, where, :] for h in range(halves)], axis=1),
                jnp.concatenate([grid_held[k, h, where, :] for h in range(halves)], axis=1),
                skip[...],
                gain[...],
            )

        gin_write(first + k).start()

    for sample in range(batch):
        for read, write in zip(reads(sample), writes(sample)):
            read.wait()
            write.start()

    def tile(base, height, q):
        return total[pl.ds(base + q * height, height), :].astype(jnp.float32)

    hidden_rows = width * hidden // LANES
    vector_rows = 2 * hidden_rows + width * width // LANES

    for q in range(hidden // LANES):
        where = pl.ds(q * LANES, LANES)
        grad_in[:, where] = tile(0, width, q)
        grad_out[where, :] = tile(hidden_rows, width, q).T
        in_bias[:, where] = jnp.sum(tile(vector_rows, 8, q), axis=0, keepdims=True)
    for q in range(halves):
        where = pl.ds(q * LANES, LANES)
        grad_skip[:, where] = tile(2 * hidden_rows, width, q)
        for which in range(3):
            at = vector_rows + 8 * (hidden + which * width) // LANES
            vectors[which, :, where] = jnp.sum(tile(at, 8, q), axis=0, keepdims=True)
        all_normed, everything = (small[pl.ds(norm_at + which * halves + q, 1), :] for which in range(2))
        vectors[3, :, where] = (all_normed - bias[:, where] * everything) / gain[:, where]
        vectors[4, :, where] = everything
    place = lax.rem(lax.axis_index("lon"), group)
    for which in range(2):
        turned = small[pl.ds(which * degrees, degrees), :].T
        for q in range(group):

            @pl.when(place == q)
            def _(q=q, which=which, turned=turned):
                grad_spec[which] = turned[q * narrow : (q + 1) * narrow, :]

    for sample in range(batch):
        for write in writes(sample):
            write.wait()
    for k in range(group):
        gin_write(first + k).wait()


def per_device(
    lat,
    lon,
    inputs,
    legendre_forward,
    legendre_inverse,
    spectral_weight,
    skip_weight,
    gain_first,
    bias_first,
    gain_second,
    bias_second,
    mlp_in,
    mlp_in_bias,
    mlp_out,
    mlp_out_bias,
    cotangent,
):
    batch, band, columns, width = inputs.shape
    points = columns * lon
    slab, degrees, lats = legendre_forward.shape
    orders = slab * lat
    hidden = mlp_in.shape[1]
    rows = columns * band
    padded = -(-rows // 16) * 16
    halves = width // LANES
    group = lon // halves
    chunks = batch // group

    forward, inverse = fourier_tables(points, orders, lat)
    high, each = split_orders(orders, lat)
    near = lat // 2
    low_rows = degrees - high
    block = 2 * each * band
    waves = 2 * orders
    pack_rows = sum(low_rows - near * i // 8 * 8 for i in range(each))
    my_lon = lax.axis_index("lon")
    hidden = mlp_in.shape[1]
    flat_rows = (2 * hidden + width) * width // LANES + 8 * (hidden + 3 * width) // LANES
    share = -(-flat_rows // (16 * lat * lon)) * 16
    total_rows = share * lat * lon
    spec_rows = -(-2 * degrees // (8 * lat)) * 8

    def flat(values):
        return values.transpose(0, 2, 1, 3).reshape(batch, rows, width)

    def row(values):
        return values.reshape(1, -1)

    vmem = pl.BlockSpec(memory_space=pltpu.VMEM)
    hbm = pl.BlockSpec(memory_space=pl.ANY)
    fixed = pl.BlockSpec(memory_space=pltpu.HBM)
    low, full = jnp.bfloat16, jnp.float32
    results = pl.pallas_call(
        functools.partial(block_kernel, lat, lon),
        out_shape=(
            jax.ShapeDtypeStruct((batch, rows, width), low),
            jax.ShapeDtypeStruct((max(batch - group, 1), rows, width), full),
            jax.ShapeDtypeStruct((total_rows, LANES), low),
            jax.ShapeDtypeStruct((lat * spec_rows + 8, LANES), full),
            jax.ShapeDtypeStruct((group, halves, padded, LANES), low),
            jax.ShapeDtypeStruct((group, halves, padded, LANES), low),
        ),
        in_specs=[hbm, hbm] + [vmem] * 16,
        out_specs=(hbm,) * 6,
        scratch_shapes=[
            pltpu.VMEM((batch, rows, width), low),
            pltpu.VMEM((batch, halves, padded, LANES), low),
            pltpu.VMEM((chunks, lon, padded, LANES), low),
            pltpu.VMEM((chunks, lon, padded, LANES), low),
            pltpu.VMEM((batch, halves, padded, LANES), low),
            pltpu.VMEM((chunks, lat + near, block, LANES), low),
            pltpu.VMEM((chunks, lat + near, block, LANES), low),
            pltpu.VMEM((chunks, each, degrees, 2 * LANES), low),
            pltpu.VMEM((chunks, pack_rows, 2 * LANES), low),
            pltpu.VMEM((2, chunks, pack_rows, 2 * LANES), low),
            pltpu.VMEM((2, chunks, pack_rows, 2 * LANES), low),
            pltpu.VMEM((pack_rows, 2 * LANES), full),
            pltpu.VMEM((pack_rows, 2 * LANES), full),
            pltpu.VMEM((2, lat + near, block, LANES), low),
            pltpu.VMEM((2, lat + near, block, LANES), low),
            pltpu.VMEM((2, lon, padded, LANES), low),
            pltpu.VMEM((2, lat + near, block, LANES), low),
            pltpu.VMEM((2, lat + near, block, LANES), low),
            pltpu.VMEM((2, lon, padded, LANES), low),
            pltpu.VMEM((max(points, waves) * band, LANES), full),
            pltpu.VMEM((waves * band, LANES), full),
            pltpu.VMEM((group, rows, width), low),
            pltpu.VMEM((group, rows, width), low),
            pltpu.VMEM((group, rows, width), full),
            pltpu.SemaphoreType.DMA((10, chunks, group)),
            pltpu.SemaphoreType.DMA((12, 2)),
            pltpu.SemaphoreType.DMA((2, chunks)),
            pltpu.SemaphoreType.DMA((batch,)),
            pltpu.SemaphoreType.DMA((group,)),
            pltpu.SemaphoreType.DMA((group,)),
            pltpu.SemaphoreType.DMA((group,)),
            pltpu.VMEM((2, 2 * each, lats, degrees), low),
            pltpu.VMEM((each, degrees, lats), low),
            pltpu.VMEM((each, lats, degrees), low),
            pltpu.VMEM((each, lats, degrees), low),
            pltpu.VMEM((each, degrees, lats), low),
            pltpu.VMEM((each, low_rows, near * band), low),
            pltpu.VMEM((each, near * band, low_rows), low),
            pltpu.VMEM((each, near * band, low_rows), low),
            pltpu.VMEM((each, low_rows, near * band), low),
            pltpu.SemaphoreType.DMA((2,)),
            pltpu.SemaphoreType.DMA((2, slab, 2)),
            pltpu.VMEM((2, LANES, degrees), full),
            pltpu.VMEM((degrees, LANES), full),
            pltpu.VMEM((degrees, LANES), full),
            pltpu.VMEM((total_rows, LANES), full),
            pltpu.VMEM((1, total_rows // 2, LANES), full),
            pltpu.VMEM((1, total_rows // 4, LANES), full),
            pltpu.VMEM((max(lon // 2 - 1, 1), total_rows // (2 * lon), LANES), low),
            pltpu.VMEM((max(lat // 2 - 1, 1), share, LANES), low),
            pltpu.VMEM((total_rows // 4, LANES), low),
            pltpu.VMEM((total_rows // (2 * lon), LANES), low),
            pltpu.VMEM((share, LANES), low),
            pltpu.VMEM((lat * spec_rows, LANES), full),
            pltpu.VMEM((lat - 1, spec_rows, LANES), full),
            pltpu.VMEM((group, spec_rows, LANES), full),
            pltpu.VMEM((spec_rows, LANES), full),
            pltpu.VMEM((spec_rows, LANES), full),
            pltpu.VMEM((2, 8, LANES), full),
            pltpu.VMEM((8, width), full),
            pltpu.VMEM((3, 8, LANES), full),
            pltpu.VMEM((lon - 1, 8, LANES), full),
            pltpu.VMEM((lat - 1, 8, LANES), full),
            pltpu.SemaphoreType.DMA((2, group)),
            pltpu.SemaphoreType.DMA((2, 4)),
            pltpu.SemaphoreType.DMA((2, 4)),
            pltpu.SemaphoreType.DMA((2,)),
            pltpu.SemaphoreType.DMA((2,)),
            pltpu.SemaphoreType.DMA((2, group)),
            pltpu.SemaphoreType.DMA((2,)),
            pltpu.SemaphoreType.DMA((2, max(lat, lon) - 1)),
            pltpu.SemaphoreType.DMA((5,)),
        ],
        compiler_params=pltpu.CompilerParams(
            collective_id=0, has_side_effects=True, vmem_limit_bytes=63 * 2**20
        ),
    )(
        flat(inputs),
        flat(cotangent),
        jnp.asarray(forward),
        jnp.asarray(inverse),
        jnp.asarray(inverse.T),
        jnp.asarray(forward.T),
        legendre_forward.transpose(0, 2, 1),
        legendre_inverse,
        spectral_weight.transpose(0, 2, 1),
        skip_weight,
        mlp_in,
        mlp_out,
        row(gain_first),
        row(bias_first),
        row(gain_second),
        row(bias_second),
        row(mlp_in_bias),
        row(mlp_out_bias),
    )
    shapes = (
        ((batch, rows, width), low),
        ((batch, rows, width), full),
        ((2, width // lon, degrees), full),
        ((width, width), full),
        ((width, hidden), full),
        ((hidden, width), full),
        ((1, hidden), full),
        ((5, 1, width), full),
    )
    output, grad_inputs, grad_spec, grad_skip, grad_in, grad_out, in_bias, vectors = pl.pallas_call(
        functools.partial(result_kernel, group, width // lon, lat * spec_rows),
        out_shape=tuple(jax.ShapeDtypeStruct(*shape) for shape in shapes),
        in_specs=[fixed, fixed, vmem, vmem, fixed, fixed, fixed, vmem, vmem, vmem],
        out_specs=(fixed, fixed) + (vmem,) * 6,
        scratch_shapes=[
            pltpu.VMEM((batch, rows, width), full),
            pltpu.VMEM((batch, rows, width), low),
            pltpu.VMEM((group, rows, width), low),
            pltpu.VMEM((group, halves, padded, LANES), low),
            pltpu.VMEM((group, halves, padded, LANES), low),
            pltpu.SemaphoreType.DMA((4, batch)),
            pltpu.SemaphoreType.DMA((3,)),
        ],
        compiler_params=pltpu.CompilerParams(vmem_limit_bytes=48 * 2**20),
    )(*results, flat(inputs), skip_weight, row(gain_first), row(bias_first))

    def unflat(values):
        return values.reshape(batch, columns, band, width).transpose(0, 2, 1, 3)

    return (
        unflat(output),
        unflat(grad_inputs),
        grad_spec.transpose(0, 2, 1),
        grad_skip,
        vectors[3, 0],
        vectors[4, 0],
        vectors[1, 0],
        vectors[2, 0],
        grad_in,
        in_bias[0],
        grad_out,
        vectors[0, 0],
    )


def solution(mesh):
    lat, lon = mesh.shape["lat"], mesh.shape["lon"]
    grid = P(None, "lat", "lon", None)
    table = P("lat", None, None)
    channel = P(None, None, "lon")
    return jax.shard_map(
        functools.partial(per_device, lat, lon),
        mesh=mesh,
        in_specs=(grid, table, table, channel) + (P(),) * 9 + (grid,),
        out_specs=(grid, grid, channel) + (P(),) * 9,
        check_vma=False,
    )
```

```python
import functools
import math

import jax
import jax.numpy as jnp
import ml_dtypes
import numpy as np
from jax import lax
from jax.experimental import pallas as pl
from jax.experimental.pallas import tpu as pltpu
from jax.sharding import PartitionSpec as P

epsilon = 1e-05
LANES = 128
MESH = pl.DeviceIdType.MESH
root = math.sqrt(2.0 / math.pi)
cubic = 0.044715

OFFSET = {"1": 0, "2": 1, "3a": 3, "3b": 4, "4": 5, "5a": 7, "5b": 7, "6": 9, "7a": 12, "7b": 13, "8": 14, "9": 15}
ORDER = ("8", "1", "7b", "7a", "5a", "4", "5b", "3b", "3a", "6", "2", "9")


def split_orders(orders, lat):
    high = 2 * orders // 3
    each = high // lat
    assert each * lat == high and 3 * high == 2 * orders
    return high, each


def fourier_tables(points, orders, lat):
    waves = np.arange(orders)
    phase = (waves[:, None] * np.arange(points)[None, :] % points).astype(np.float32)
    phase = phase * np.float32(2.0 * math.pi / points)
    cosine, sine = np.cos(phase), np.sin(phase)
    factor = np.where(waves == 0, 1.0, 2.0).astype(np.float32)[:, None]
    high, each = split_orders(orders, lat)
    near = lat // 2
    owned = [[t * each + i for i in range(each)] for t in range(lat)]
    owned += [[high + near * i + d for i in range(each)] for d in range(near)]

    def arrange(*parts):
        stacked = [part[waves] for waves in owned for part in parts]
        return np.concatenate(stacked).astype(ml_dtypes.bfloat16)

    return arrange(cosine, -sine), arrange(factor * cosine, -factor * sine)


def row_tile(rows, most):
    fits = [t for t in range(16, most + 1, 16) if rows % t == 0]
    return fits[-1] if fits else rows


def norm_parts(values):
    center = values - jnp.mean(values, axis=-1, keepdims=True)
    spread = jnp.mean(center * center, axis=-1, keepdims=True)
    scaled = lax.rsqrt(spread + epsilon)
    return center * scaled, scaled


def norm_back(grad_out, normal, scaled, gain):
    grad_norm = grad_out * gain
    inner = jnp.mean(grad_norm, axis=-1, keepdims=True)
    cross = jnp.mean(grad_norm * normal, axis=-1, keepdims=True)
    return scaled * (grad_norm - inner - normal * cross)


def norm_step(values, mixed, sent, skip, gain):
    normal, scaled = norm_parts(values.astype(jnp.float32))
    grad_normed = dot_t(mixed, skip) + sent.astype(jnp.float32)
    return mixed.astype(jnp.float32) + norm_back(grad_normed, normal, scaled, gain)


def fold(values):
    rows, width = values.shape
    return jnp.sum(values.reshape(rows // 8, 8, width), axis=0)


def dot(a, b):
    return jnp.dot(a, b, preferred_element_type=jnp.float32)


def dot_t(a, b):
    return lax.dot_general(a, b, (((1,), (1,)), ((), ())), preferred_element_type=jnp.float32)


def t_dot(a, b):
    return lax.dot_general(a, b, (((0,), (0,)), ((), ())), preferred_element_type=jnp.float32)


def block_kernel(
    lat,
    lon,
    x_hbm,
    g_hbm,
    fwd_t,
    inv_t,
    inv,
    fwd,
    raw_ana,
    raw_syn,
    weight,
    skip,
    mlp_in,
    mlp_out,
    gain_one,
    bias_one,
    gain_two,
    bias_two,
    bias_in,
    bias_out,
    out_hbm,
    gin_hbm,
    total_hbm,
    small_hbm,
    last_mixed,
    last_grid,
    x_all,
    normed,
    lon_a,
    lon_c,
    lon_b,
    lat_a,
    lat_b,
    coeffs,
    coeffs_high,
    pack_own,
    pack_far,
    stack,
    stack_held,
    send_2,
    send_3,
    send_4,
    send_6,
    send_7,
    send_8,
    wide,
    slim,
    g_buf,
    o_buf,
    i_buf,
    recv_sem,
    send_sem,
    rows_sem,
    x_sem,
    g_sem,
    o_sem,
    i_sem,
    tabs,
    ana,
    ana_t,
    syn,
    syn_t,
    ana_high,
    ana_high_t,
    syn_high,
    syn_high_t,
    tab_recv,
    tab_send,
    w_parts,
    w_real,
    w_imag,
    acc,
    part_core,
    part_near,
    part_chip,
    part_far,
    wire_chip,
    wire_far,
    share,
    spec,
    spec_lat,
    spec_lon,
    spec_sum,
    spec_own,
    norm_sums,
    mixed_sums,
    norm_own,
    norm_lon,
    norm_lat,
    w_sem,
    fold_recv,
    fold_send,
    spec_recv,
    spec_send,
    spec_pair,
    norm_recv,
    norm_send,
    own_sem,
):
    batch, rows, width = x_hbm.shape
    halves = width // LANES
    group = lon // halves
    chunks = batch // group
    points = fwd_t.shape[1]
    slab, lats, degrees = raw_ana.shape
    narrow = width // lon
    hidden = mlp_in.shape[1]
    band = lats // lat
    waves = 2 * slab * lat
    high, each = split_orders(slab * lat, lat)
    near = lat // 2
    block = 2 * each * band
    slots = lat + near
    low_rows = degrees - high
    starts = [near * i // 8 * 8 for i in range(each)]
    packs = [sum(low_rows - start for start in starts[:i]) for i in range(each)]
    my_lat, my_lon = lax.axis_index("lat"), lax.axis_index("lon")
    mixed = normed
    my_side, my_near = my_lat // near, lax.rem(my_lat, near)
    half_tile = row_tile(rows, 144)
    full_tile = row_tile(rows, 240)

    def slot_of(chunk):
        return lax.rem(chunk, 2)

    def lon_copy(stage, chunk, src, dst, peer, member=0):
        return pltpu.make_async_remote_copy(
            src_ref=src,
            dst_ref=dst,
            send_sem=rows_sem.at[stage // 4, chunk] if stage in (1, 5) else send_sem.at[stage - 1, slot_of(chunk)],
            recv_sem=recv_sem.at[stage - 1, chunk, member],
            device_id={"lon": peer},
            device_id_type=MESH,
        )

    def lat_copy(send_at, recv_at, chunk, src, dst, peer):
        return pltpu.make_async_remote_copy(
            src_ref=src,
            dst_ref=dst,
            send_sem=send_sem.at[send_at, slot_of(chunk)],
            recv_sem=recv_sem.at[recv_at, chunk, 0],
            device_id={"lat": peer},
            device_id_type=MESH,
        )

    def own_copy(stage, chunk, src, dst):
        return pltpu.make_async_copy(src, dst, recv_sem.at[stage - 1, chunk, 0])

    def landed(stage, chunk, whole, member=0):
        pltpu.make_async_copy(whole, whole, recv_sem.at[stage - 1, chunk, member]).wait()

    def member_at(step):
        return lax.rem(my_lon // halves + step, group)

    def member_landed(stage, chunk, step):
        count = halves if step else halves - 1
        landed(stage, chunk, lon_a.at[chunk, pl.ds(0, count)], member_at(step))

    def sent(stage, chunk, part):
        lon_copy(stage, chunk, part, part, my_lon).wait_send()

    def x_load(sample):
        return pltpu.make_async_copy(x_hbm.at[sample], x_all.at[sample], x_sem.at[sample])

    def g_load(sample, slot):
        return pltpu.make_async_copy(g_hbm.at[sample], g_buf.at[slot], g_sem.at[slot])

    def o_store(sample, slot):
        return pltpu.make_async_copy(o_buf.at[slot], out_hbm.at[sample], o_sem.at[slot])

    def i_store(sample, slot):
        return pltpu.make_async_copy(i_buf.at[slot], gin_hbm.at[sample], i_sem.at[slot])

    def spread_rows(stage, chunk, held, sample, landing):
        src = chunk * group + sample
        for half in range(halves):
            peer = sample * halves + half

            @pl.when(peer != my_lon)
            def _(peer=peer, half=half):
                lon_copy(stage, chunk, held.at[src, half], landing.at[chunk, my_lon], peer).start()

            @pl.when(peer == my_lon)
            def _(half=half):
                own_copy(stage, chunk, held.at[src, half], landing.at[chunk, my_lon]).start()

    def spread_low(send_at, recv_at, chunk, buffer, target):
        for step in range(1, lat):
            peer = lax.rem(my_lat + step, lat)
            lat_copy(send_at, recv_at, chunk, buffer.at[peer], target.at[chunk, my_lat], peer).start()

    def spread_high(send_at, recv_at, chunk, buffer, target):
        for step in range(1, near):
            peer = lax.rem(my_near + step, near)
            src, dst = buffer.at[lat + peer], target.at[chunk, lat + my_near]
            lat_copy(send_at, recv_at, chunk, src, dst, my_side * near + peer).start()

    def own_rows(at):
        return pl.ds(pl.multiple_of(at * block, 16), block)

    def to_waves(stage, chunk, table, scale, buffer, landing):
        slot = slot_of(chunk)
        landed(stage - 1, chunk, landing.at[chunk])
        for source in range(lon):
            wide[pl.ds(source * rows, rows), :] = landing[chunk, source, pl.ds(0, rows), :].astype(jnp.float32)
        for first in range(0, band, 2):
            rhs = jnp.concatenate(
                [wide[pl.ds(first + k, points, stride=band), :] for k in range(2)], axis=1
            ).astype(jnp.bfloat16)
            got = dot(table[...], rhs)
            if scale is not None:
                got = got * scale
            for k in range(2):
                slim[pl.ds(first + k, waves, stride=band), :] = got[:, k * LANES : (k + 1) * LANES]

        @pl.when(chunk > 1)
        def _():
            sent(stage, chunk, buffer.at[slot, pl.ds(0, slots - 2)])

        for target in range(slots):
            buffer[slot, target] = slim[pl.ds(target * block, block), :].astype(jnp.bfloat16)
        spread_low(stage - 1, stage - 1, chunk, buffer.at[slot], lat_a)
        spread_high(stage - 1, stage - 1, chunk, buffer.at[slot], lat_a)
        lat_a[chunk, my_lat] = slim[own_rows(my_lat), :].astype(jnp.bfloat16)
        lat_a[chunk, lat + my_near] = slim[own_rows(lat + my_near), :].astype(jnp.bfloat16)

    def to_points(stage, chunk, table, scale, buffer):
        slot = slot_of(chunk)
        landed(stage - 1, chunk, lat_b.at[chunk, pl.ds(0, slots - 2)])
        for source in range(slots):
            slim[pl.ds(source * block, block), :] = lat_b[chunk, source].astype(jnp.float32)
        for first in range(0, band, 2):
            rhs = jnp.concatenate(
                [slim[pl.ds(first + k, waves, stride=band), :] for k in range(2)], axis=1
            ).astype(jnp.bfloat16)
            got = dot(table[...], rhs)
            if scale is not None:
                got = got * scale
            for k in range(2):
                wide[pl.ds(first + k, points, stride=band), :] = got[:, k * LANES : (k + 1) * LANES]

        @pl.when(chunk > 1)
        def _():
            sent(stage, chunk, buffer.at[slot, pl.ds(0, lon - 1)])

        for target in range(lon):
            grid = wide[pl.ds(target * rows, rows), :]
            buffer[slot, target, pl.ds(0, rows), :] = grid.astype(jnp.bfloat16)
            if stage == 8:
                before = lon_a[chunk, target, pl.ds(0, rows), :].astype(jnp.float32)
                norm_sums[0] += fold(grid * before)
                norm_sums[1] += fold(grid)
        member, half = my_lon // halves, lax.rem(my_lon, halves)

        def send(landing):
            for step in range(1, lon):
                peer = lax.rem(my_lon + step, lon)
                lon_copy(stage, chunk, buffer.at[slot, peer], landing, peer, member).start()

        def send_here():
            send(lon_b.at[chunk * group + member, half])
            own = pl.ds(pl.multiple_of(my_lon * rows, 8), rows)
            lon_b[chunk * group + member, half, pl.ds(0, rows), :] = wide[own, :].astype(jnp.bfloat16)

        if stage == 4:
            send_here()
        else:
            pl.when(chunk < chunks - 1)(send_here)

            @pl.when(chunk == chunks - 1)
            def _():
                norm_start()
                send(last_grid.at[member, half])
                last_own().start()

    def last_own():
        held = last_grid.at[my_lon // halves, lax.rem(my_lon, halves)]
        return pltpu.make_async_copy(send_8.at[(chunks - 1) % 2, my_lon], held, own_sem.at[3])

    def last_mixed_copy():
        part = mixed.at[pl.ds((chunks - 1) * group, group)]
        return pltpu.make_async_copy(part, last_mixed, own_sem.at[4])

    def wave_rows(first, count, i):
        parts = []
        for r in range(2):
            at = (r * each + i) * band
            held = [slim[pl.ds(s * block + at, band), :] for s in range(first, first + count)]
            parts.append(jnp.concatenate(held, axis=0))
        return jnp.concatenate(parts, axis=1).astype(jnp.bfloat16)

    def put_rows(got, count, i):
        for r in range(2):
            at = (r * each + i) * band
            for t in range(count):
                wide[pl.ds(t * block + at, band), :] = got[
                    t * band : (t + 1) * band, r * LANES : (r + 1) * LANES
                ]

    def pack_copy(k, chunk):
        peer = lax.rem(my_lat + near, lat)
        return lat_copy(10 + k, 8 + k, chunk, pack_own.at[k, chunk], pack_far.at[k, chunk], peer)

    def slab_first(stage, k, chunk, tables, between, buffer):
        first_table, second_table, high_table = tables
        slot = slot_of(chunk)
        landed(stage - 1, chunk, lat_a.at[chunk, pl.ds(0, slots - 2)])
        for source in range(slots):
            slim[pl.ds(source * block, block), :] = lat_a[chunk, source].astype(jnp.float32)
        for i in range(each):
            got = dot(high_table[i], wave_rows(lat, near, i))
            stack[pl.ds(packs[i], low_rows - starts[i]), :] = got[starts[i] :, :]

        @pl.when(chunk > 1)
        def _():
            pack_copy(k, chunk).wait_send()

        pack_own[k, chunk] = stack[...].astype(jnp.bfloat16)
        pack_copy(k, chunk).start()
        for m in range(each):
            real, imag = between(m, dot(first_table[m], wave_rows(0, lat, m)))
            low = jnp.concatenate([real, imag], axis=1).astype(jnp.bfloat16)
            put_rows(dot(second_table[m], low), lat, m)

        @pl.when(chunk > 1)
        def _():
            sent(stage, chunk, buffer.at[slot, pl.ds(0, lat - 1)])

        for target in range(lat):
            buffer[slot, target] = wide[pl.ds(target * block, block), :].astype(jnp.bfloat16)
        spread_low(stage - 1, stage - 1, chunk, buffer.at[slot], lat_b)
        lat_b[chunk, my_lat] = wide[own_rows(my_lat), :].astype(jnp.bfloat16)

    def slab_second(stage, k, chunk, table, before, between, buffer):
        slot = slot_of(chunk)
        landed(9 + k, chunk, pack_far.at[k, chunk])
        stack[...] = pack_own[k, chunk].astype(jnp.float32) + pack_far[k, chunk].astype(jnp.float32)
        before()
        for i in range(each):
            count = low_rows - starts[i]
            real, imag = between(pl.ds(packs[i], count), high + starts[i], count)
            low = jnp.concatenate([real, imag], axis=1)
            if starts[i]:
                low = jnp.concatenate([jnp.zeros((starts[i], 2 * LANES), jnp.float32), low], axis=0)
            put_rows(dot(table[i], low.astype(jnp.bfloat16)), near, i)

        if near > 1:

            @pl.when(chunk > 1)
            def _():
                sent(9 + k, chunk, buffer.at[slot, pl.ds(lat, near - 1)])

        for target in range(near):
            buffer[slot, lat + target] = wide[pl.ds(target * block, block), :].astype(jnp.bfloat16)
        spread_high(8 + k, stage - 1, chunk, buffer.at[slot], lat_b)
        lat_b[chunk, lat + my_near] = wide[own_rows(my_near), :].astype(jnp.bfloat16)

    hidden_rows = width * hidden // LANES
    vector_rows = 2 * hidden_rows + width * width // LANES

    def gather_rows(base, values):
        count = values.shape[0]
        for q in range(values.shape[1] // LANES):
            acc[pl.ds(base + q * count, count), :] += values[:, q * LANES : (q + 1) * LANES]

    def both(held, sample, where):
        return jnp.concatenate([held[sample, h, where, :] for h in range(halves)], axis=1)

    def normalize(sample):
        x_load(sample).wait()

        @pl.loop(0, rows // half_tile)
        def _(i):
            where = pl.ds(pl.multiple_of(i * half_tile, 8), half_tile)
            normal, _ = norm_parts(x_all[sample, where, :].astype(jnp.float32))
            low = (normal * gain_one[...] + bias_one[...]).astype(jnp.bfloat16)
            for h in range(halves):
                normed[sample, h, where, :] = low[:, h * LANES : (h + 1) * LANES]

    def stage_1(chunk):
        for step in reversed(range(group)):
            k = member_at(step)

            @pl.when(jnp.logical_or(chunk > 0, step == 0))
            def _(k=k):
                normalize(chunk * group + k)

            spread_rows(1, chunk, normed, k, lon_a)

    def stage_2(chunk):
        to_waves(2, chunk, fwd_t, 1.0 / points, send_2, lon_a)

    def filtered(real, imag, rows):
        wr, wi = w_real[rows, :], w_imag[rows, :]
        return wr * real - wi * imag, wr * imag + wi * real

    def stage_3a(chunk):
        def between(m, got):
            coeffs[chunk, m] = got.astype(jnp.bfloat16)
            return filtered(got[:, :LANES], got[:, LANES:], pl.ds(0, degrees))

        slab_first(3, 0, chunk, (ana, syn, ana_high), between, send_3)

    def stage_3b(chunk):
        def before():
            coeffs_high[chunk] = stack[...].astype(jnp.bfloat16)

        def between(where, degree, count):
            got = stack[where, :]
            return filtered(got[:, :LANES], got[:, LANES:], pl.ds(degree, count))

        slab_second(3, 0, chunk, syn_high, before, between, send_3)

    def stage_4(chunk):
        to_points(4, chunk, inv, None, send_4)

    def stage_5a(chunk):
        sent(1, chunk, lon_a.at[chunk, pl.ds(0, lon - 1)])
        feed_forward(chunk, range(group // 2))

    def stage_5b(chunk):
        feed_forward(chunk, range(group // 2, group))

    def feed_forward(chunk, steps):
        for step in steps:
            member_landed(4, chunk, step)
            k = member_at(step)
            sample = chunk * group + k
            g_load(sample, k).wait()

            @pl.when(chunk > 0)
            def _(sample=sample, k=k):
                o_store(sample, k).wait()

            @pl.loop(0, rows // full_tile)
            def _(i):
                where = pl.ds(pl.multiple_of(i * full_tile, 8), full_tile)
                low_one = both(normed, sample, where)
                spatial = both(lon_b, sample, where).astype(jnp.float32)
                resid = x_all[sample, where, :].astype(jnp.float32) + (spatial + dot(low_one, skip[...]))
                normal, scaled = norm_parts(resid)
                low_two = (normal * gain_two[...] + bias_two[...]).astype(jnp.bfloat16)
                pre = dot(low_two, mlp_in[...]) + bias_in[...]
                square = pre * pre
                curve = jnp.tanh(root * pre * (1.0 + cubic * square))
                lifted = 0.5 + 0.5 * curve
                act = (pre * lifted).astype(jnp.bfloat16)
                slope = lifted + (0.5 * root) * pre * (1.0 - curve * curve) * (1.0 + (3.0 * cubic) * square)
                o_buf[k, where, :] = (resid + dot(act, mlp_out[...]) + bias_out[...]).astype(jnp.bfloat16)
                g_low = g_buf[k, where, :]
                gather_rows(hidden_rows, t_dot(g_low, act))
                grad_pre = (dot_t(g_low, mlp_out[...]) * slope).astype(jnp.bfloat16)
                gather_rows(0, t_dot(low_two, grad_pre))
                gather_rows(vector_rows, fold(grad_pre.astype(jnp.float32)))
                grad_second = dot_t(grad_pre, mlp_in[...])
                g_full = g_low.astype(jnp.float32)
                for at, values in enumerate((g_full, grad_second * normal, grad_second)):
                    gather_rows(vector_rows + 8 * (hidden + at * width) // LANES, fold(values))
                grad_mixed = (g_full + norm_back(grad_second, normal, scaled, gain_two[...])).astype(jnp.bfloat16)
                gather_rows(2 * hidden_rows, t_dot(low_one, grad_mixed))
                mixed_sums[...] += fold(grad_mixed.astype(jnp.float32))
                for h in range(halves):
                    mixed[sample, h, where, :] = grad_mixed[:, h * LANES : (h + 1) * LANES]

            o_store(sample, k).start()

            @pl.when(chunk < chunks - 1)
            def _(sample=sample, k=k):
                g_load(sample + group, k).start()

            spread_rows(5, chunk, mixed, k, lon_c)

    def stage_6(chunk):
        to_waves(6, chunk, inv_t, None, send_6, lon_c)

    def unfiltered(got, held, degree, count, share_of):
        dr, di = got[:, :LANES], got[:, LANES:]
        ar, ai = held[:, :LANES], held[:, LANES:]
        spec[pl.ds(degree, count), :] += share_of * (dr * ar + di * ai)
        spec[pl.ds(degrees + degree, count), :] += share_of * (di * ar - dr * ai)
        wr, wi = w_real[pl.ds(degree, count), :], w_imag[pl.ds(degree, count), :]
        return wr * dr + wi * di, wr * di - wi * dr

    def stage_7a(chunk):
        def between(m, got):
            return unfiltered(got, coeffs[chunk, m].astype(jnp.float32), 0, degrees, 1.0)

        slab_first(7, 1, chunk, (syn_t, ana_t, syn_high_t), between, send_7)

    def stage_7b(chunk):
        def before():
            stack_held[...] = coeffs_high[chunk].astype(jnp.float32)

        def between(where, degree, count):
            return unfiltered(stack[where, :], stack_held[where, :], degree, count, 0.5)

        slab_second(7, 1, chunk, ana_high_t, before, between, send_7)

    def stage_8(chunk):
        to_points(8, chunk, fwd, 1.0 / points, send_8)

    def stage_9(chunk):
        for step in range(group):
            member_landed(8, chunk, step)
            k = member_at(step)
            sample = chunk * group + k

            @pl.when(chunk > 0)
            def _(sample=sample, k=k):
                i_store(sample, k).wait()

            @pl.loop(0, rows // half_tile)
            def _(i):
                where = pl.ds(pl.multiple_of(i * half_tile, 8), half_tile)
                i_buf[k, where, :] = norm_step(
                    x_all[sample, where, :],
                    both(mixed, sample, where),
                    both(lon_b, sample, where),
                    skip[...],
                    gain_one[...],
                )

            i_store(sample, k).start()

    def weight_copies(start):
        place = lax.rem(my_lon, group)
        held = w_parts.at[:, pl.ds(pl.multiple_of(place * narrow, 8), narrow), :]
        for q in range(group):
            peer = my_lon // group + halves * q

            @pl.when(peer != my_lon)
            def _(peer=peer, q=q):
                copy = pltpu.make_async_remote_copy(
                    src_ref=weight,
                    dst_ref=held,
                    send_sem=w_sem.at[1, q],
                    recv_sem=w_sem.at[0, place],
                    device_id={"lon": peer},
                    device_id_type=MESH,
                )
                if start:
                    copy.start()
                else:
                    copy.wait_send()

            if start:

                @pl.when(peer == my_lon)
                def _():
                    pltpu.make_async_copy(weight, held, w_sem.at[0, place]).start()

    def table_copies(start):
        def one(i, carry):
            wave = my_lat * slab + i

            def give(peer, slot, way):
                for which, raw in enumerate((raw_ana, raw_syn)):

                    @pl.when(peer != my_lat)
                    def _(which=which, raw=raw):
                        copy = pltpu.make_async_remote_copy(
                            src_ref=raw.at[i],
                            dst_ref=tabs.at[which, slot],
                            send_sem=tab_send.at[which, i, way],
                            recv_sem=tab_recv.at[which],
                            device_id={"lat": peer},
                            device_id_type=MESH,
                        )
                        if start:
                            copy.start()
                        else:
                            copy.wait_send()

                    if start:

                        @pl.when(peer == my_lat)
                        def _(which=which, raw=raw):
                            pltpu.make_async_copy(raw.at[i], tabs.at[which, slot], tab_recv.at[which]).start()

            @pl.when(wave < high)
            def _():
                give(lax.div(wave, each), lax.rem(wave, each), 0)

            @pl.when(wave >= high)
            def _():
                above = wave - high
                for side in range(2):
                    give(side * near + lax.rem(above, near), each + lax.div(above, near), side)

            return carry

        lax.fori_loop(0, slab, one, 0)

    def build():
        acc[...] = jnp.zeros_like(acc)
        spec[...] = jnp.zeros_like(spec)
        norm_sums[...] = jnp.zeros_like(norm_sums)
        mixed_sums[...] = jnp.zeros_like(mixed_sums)
        norm_own[...] = jnp.zeros_like(norm_own)
        degree = lax.broadcasted_iota(jnp.int32, (lats, degrees), 1)
        for which in range(2):
            pltpu.make_async_copy(tabs.at[which], tabs.at[which], tab_recv.at[which]).wait()
        kinds = ((ana_t, ana, ana_high_t, ana_high), (syn, syn_t, syn_high, syn_high_t))

        @pl.loop(0, each)
        def _(i):
            half = pl.ds(pl.multiple_of(my_side * near * band, 16), near * band)
            for which, (plain, turned, part, part_turned) in enumerate(kinds):
                values = tabs[which, i].astype(jnp.float32)
                values = jnp.where(degree >= my_lat * each + i, values, 0.0)
                plain[i] = values.astype(jnp.bfloat16)
                turned[i] = values.T.astype(jnp.bfloat16)
                values = tabs[which, each + i, half, :].astype(jnp.float32)
                values = jnp.where(degree[: near * band] >= high + near * i + my_near, values, 0.0)
                values = values.T[high:, :]
                part_turned[i] = values.astype(jnp.bfloat16)
                part[i] = values.T.astype(jnp.bfloat16)

        for q in range(group):
            part = w_parts.at[:, pl.ds(q * narrow, narrow), :]
            pltpu.make_async_copy(part, part, w_sem.at[0, q]).wait()
        w_real[...] = w_parts[0].T
        w_imag[...] = w_parts[1].T

    total_rows = acc.shape[0]
    place_core, place_chip = lax.rem(my_lon, 2), my_lon // 2
    place_near, place_far = lax.rem(my_lat, 2), my_lat // 2
    levels = (
        (2, place_core, part_core, None, lambda p: {"lon": 2 * place_chip + p}),
        (2, place_near, part_near, None, lambda p: {"lat": 2 * place_far + p}),
        (lon // 2, place_chip, part_chip, wire_chip, lambda p: {"lon": 2 * p + place_core}),
        (lat // 2, place_far, part_far, wire_far, lambda p: {"lat": 2 * p + place_near}),
    )
    bases, sizes = [0], [total_rows]
    for count, place, _, _, _ in levels:
        sizes.append(sizes[-1] // count)
        bases.append(bases[-1] + place * sizes[-1])

    def row_part(at, count):
        return pl.ds(pl.multiple_of(at, 16), count)

    def fold_start(k):
        count, place, parts, wire, device = levels[k]
        if wire is not None:
            wire[...] = acc[row_part(bases[k], sizes[k]), :].astype(jnp.bfloat16)
        for step in range(1, count):
            peer = lax.rem(place + step, count)
            if wire is None:
                src = acc.at[row_part(bases[k] + peer * sizes[k + 1], sizes[k + 1]), :]
            else:
                src = wire.at[row_part(peer * sizes[k + 1], sizes[k + 1]), :]
            pltpu.make_async_remote_copy(
                src_ref=src,
                dst_ref=parts.at[step - 1],
                send_sem=fold_send.at[0, k],
                recv_sem=fold_recv.at[0, k],
                device_id=device(peer),
                device_id_type=MESH,
            ).start()

    def fold_end(k):
        count, _, parts, _, _ = levels[k]
        if count == 1:
            return
        pltpu.make_async_copy(parts, parts, fold_recv.at[0, k]).wait()
        got = parts[0].astype(jnp.float32)
        for step in range(2, count):
            got = got + parts[step - 1].astype(jnp.float32)
        acc[row_part(bases[k + 1], sizes[k + 1]), :] += got

    def spread_start(k):
        count, place, _, _, device = levels[k]
        own = row_part(bases[k + 1], sizes[k + 1])
        src = total_hbm.at[own, :]
        if k == len(levels) - 1:
            share[...] = acc[own, :].astype(jnp.bfloat16)
            src = share
            pltpu.make_async_copy(share, total_hbm.at[own, :], own_sem.at[0]).start()
        for step in range(1, count):
            pltpu.make_async_remote_copy(
                src_ref=src,
                dst_ref=total_hbm.at[own, :],
                send_sem=fold_send.at[1, k],
                recv_sem=fold_recv.at[1, k],
                device_id=device(lax.rem(place + step, count)),
                device_id_type=MESH,
            ).start()

    def spread_end(k):
        count = levels[k][0]
        if count > 1:
            all_parts = total_hbm.at[pl.ds(0, (count - 1) * sizes[k + 1]), :]
            pltpu.make_async_copy(all_parts, all_parts, fold_recv.at[1, k]).wait()
        if k == len(levels) - 1:
            own = row_part(bases[k + 1], sizes[k + 1])
            pltpu.make_async_copy(share, total_hbm.at[own, :], own_sem.at[0]).wait()

    def fold_sent():
        for k, (count, _, _, wire, _) in enumerate(levels):
            for way, held in ((0, acc if wire is None else wire), (1, total_hbm)):
                if count == 1:
                    continue
                part = held.at[pl.ds(0, (count - 1) * sizes[k + 1]), :]
                pltpu.make_async_remote_copy(
                    src_ref=part,
                    dst_ref=part,
                    send_sem=fold_send.at[way, k],
                    recv_sem=fold_recv.at[way, k],
                    device_id={"lon": my_lon},
                    device_id_type=MESH,
                ).wait_send()

    spec_rows = spec_sum.shape[0]

    def spec_part(at):
        return pl.ds(pl.multiple_of(at * spec_rows, 8), spec_rows)

    def spec_lat_copies(way, src, dst):
        for step in range(1, lat):
            peer = lax.rem(my_lat + step, lat)
            pltpu.make_async_remote_copy(
                src_ref=src(peer),
                dst_ref=dst(step),
                send_sem=spec_send.at[way],
                recv_sem=spec_recv.at[way],
                device_id={"lat": peer},
                device_id_type=MESH,
            ).start()

    def spec_start():
        spec_lat_copies(
            0, lambda p: spec.at[spec_part(p), :], lambda s: spec_lat.at[s - 1]
        )

    def spec_pairs(action):
        half = lax.rem(my_lon, halves)
        for q in range(group):
            target = half * group + q

            @pl.when(target != my_lon)
            def _(target=target, q=q):
                copy = pltpu.make_async_remote_copy(
                    src_ref=spec_sum,
                    dst_ref=spec_lon.at[my_lon // halves],
                    send_sem=spec_pair.at[1, q],
                    recv_sem=spec_pair.at[0, my_lon // halves],
                    device_id={"lon": target},
                    device_id_type=MESH,
                )
                if action == "start":
                    copy.start()
                else:
                    copy.wait_send()

            if action == "start":

                @pl.when(target == my_lon)
                def _():
                    pltpu.make_async_copy(
                        spec_sum, spec_lon.at[my_lon // halves], spec_pair.at[0, my_lon // halves]
                    ).start()

    def spec_middle():
        pltpu.make_async_copy(spec_lat, spec_lat, spec_recv.at[0]).wait()
        got = spec[spec_part(my_lat), :]
        for step in range(1, lat):
            got = got + spec_lat[step - 1]
        spec_sum[...] = got
        spec_pairs("start")

    def spec_back():
        for q in range(group):
            pltpu.make_async_copy(spec_lon.at[q], spec_lon.at[q], spec_pair.at[0, q]).wait()
        got = spec_lon[0]
        for q in range(1, group):
            got = got + spec_lon[q]
        spec_own[...] = got
        own = spec_part(my_lat)
        spec_lat_copies(1, lambda p: spec_own, lambda s: small_hbm.at[own, :])
        pltpu.make_async_copy(spec_own, small_hbm.at[own, :], own_sem.at[1]).start()

    def spec_end():
        pltpu.make_async_copy(spec_own, small_hbm.at[spec_part(my_lat), :], own_sem.at[1]).wait()
        part = spec.at[pl.ds(0, (lat - 1) * spec_rows), :]
        pltpu.make_async_copy(part, part, spec_recv.at[1]).wait()
        for way in range(2):
            pltpu.make_async_remote_copy(
                src_ref=part,
                dst_ref=part,
                send_sem=spec_send.at[way],
                recv_sem=spec_recv.at[way],
                device_id={"lat": my_lat},
                device_id_type=MESH,
            ).wait_send()
        spec_pairs("end")

    def norm_copies(way, axis, count, place, src, parts, action):
        for step in range(1, count):
            copy = pltpu.make_async_remote_copy(
                src_ref=src,
                dst_ref=parts.at[step - 1],
                send_sem=norm_send.at[way, step - 1],
                recv_sem=norm_recv.at[way],
                device_id={axis: lax.rem(place + step, count)},
                device_id_type=MESH,
            )
            if action == "start":
                copy.start()
            else:
                copy.wait_send()

    def norm_end(way, parts, count):
        pltpu.make_async_copy(parts, parts, norm_recv.at[way]).wait()
        got = norm_own[way]
        for step in range(1, count):
            got = got + parts[step - 1]
        norm_own[way + 1] = got

    def norm_skip():
        lines = [jnp.zeros((1, width), jnp.float32) for _ in range(2)]
        all_mixed = jnp.sum(mixed_sums[...], axis=0, keepdims=True)
        for q in range(halves):
            lanes = slice(q * LANES, (q + 1) * LANES)
            part = skip[:, lanes].astype(jnp.float32)
            held = acc[pl.ds(2 * hidden_rows + q * width, width), :]
            for which, values in enumerate((held, all_mixed[:, lanes])):
                lines[which] += jnp.sum((part * values).T, axis=0, keepdims=True)
        for which in range(2):
            for half in range(halves):
                norm_own[0, pl.ds(which * halves + half, 1), :] = lines[which][
                    :, half * LANES : (half + 1) * LANES
                ]

    def norm_start():
        for half in range(halves):

            @pl.when(lax.rem(my_lon, halves) == half)
            def _(half=half):
                for which in range(2):
                    line = jnp.sum(norm_sums[which], axis=0, keepdims=True)
                    norm_own[0, pl.ds(which * halves + half, 1), :] += line

        norm_copies(0, "lon", lon, my_lon, norm_own.at[0], norm_lon, "start")

    def norm_middle():
        norm_end(0, norm_lon, lon)
        norm_copies(1, "lat", lat, my_lat, norm_own.at[1], norm_lat, "start")

    def norm_finish():
        norm_end(1, norm_lat, lat)
        where = pl.ds(lat * spec_rows, 8)
        copy = pltpu.make_async_copy(norm_own.at[2], small_hbm.at[where, :], own_sem.at[2])
        copy.start()
        norm_copies(0, "lon", lon, my_lon, norm_own.at[0], norm_lon, "end")
        norm_copies(1, "lat", lat, my_lat, norm_own.at[1], norm_lat, "end")
        copy.wait()

    def last_mixed_start():
        last_mixed_copy().start()

    def run(*steps):
        def go():
            for step, k in steps:
                step() if k is None else step(k)

        return go

    end = chunks - 1
    aside = {
        (0, "1"): build,
        (end + 7, "5b"): run((last_mixed_start, None), (norm_skip, None), (fold_start, 0)),
        (end + 8, "7a"): run((fold_end, 0), (fold_start, 1)),
        (end + 9, "7b"): run((fold_end, 1), (fold_start, 2)),
        (end + 10, "8"): run((fold_end, 2), (fold_start, 3)),
        (end + 11, "8"): run((fold_end, 3), (spread_start, 3)),
        (end + 11, "9"): run((spread_end, 3), (spread_start, 2)),
        (end + 12, "9"): run((spread_end, 2), (spread_start, 1)),
        (end + 14, "8"): run((spread_end, 1), (spread_start, 0), (norm_middle, None), (spec_back, None)),
        (end + 13, "7b"): run((spec_start, None)),
        (end + 13, "9"): run((spec_middle, None)),
    }

    stages = {
        "1": stage_1,
        "2": stage_2,
        "3a": stage_3a,
        "3b": stage_3b,
        "4": stage_4,
        "5a": stage_5a,
        "5b": stage_5b,
        "6": stage_6,
        "7a": stage_7a,
        "7b": stage_7b,
        "8": stage_8,
        "9": stage_9,
    }

    for sample in range(group):
        x_load(sample).start()

    padded = lon_a.shape[2]
    if padded > rows:
        normed[:, :, rows:, :] = jnp.zeros_like(normed[:, :, rows:, :])
        for held in (send_4, send_8):
            held[:, :, rows:, :] = jnp.zeros_like(held[:, :, rows:, :])
    barrier = pltpu.get_barrier_semaphore()
    for step in range(1, lon):
        pl.semaphore_signal(
            barrier, inc=1, device_id={"lon": lax.rem(my_lon + step, lon)}, device_id_type=MESH
        )
    for step in range(1, lat):
        pl.semaphore_signal(
            barrier, inc=1, device_id={"lat": lax.rem(my_lat + step, lat)}, device_id_type=MESH
        )
    for step in range(1, group):
        normalize(member_at(step))
    for sample in range(group, batch):
        x_load(sample).start()
    for k in range(group):
        g_load(k, k).start()
    pl.semaphore_wait(barrier, lon - 1 + lat - 1)

    weight_copies(True)
    table_copies(True)

    def tick(now, carry):
        for stage in ORDER:
            chunk = now - OFFSET[stage]

            @pl.when(jnp.logical_and(chunk >= 0, chunk < (end if stage == "9" else chunks)))
            def _(stage=stage, chunk=chunk):
                stages[stage](chunk)

            for (when, after), action in aside.items():
                if after == stage:
                    pl.when(now == when)(action)

        return carry

    lax.fori_loop(0, chunks + max(OFFSET.values()), tick, 0)

    spread_end(0)
    norm_finish()
    spec_end()
    fold_sent()
    for step in range(group):
        member_landed(8, end, step)
    last_own().wait()
    last_mixed_copy().wait()
    weight_copies(False)
    table_copies(False)
    last = chunks - 1
    for chunk in range(chunks):
        sent(5, chunk, lon_a.at[chunk, pl.ds(0, lon - 1)])
    for chunk in range(max(chunks - 2, 0), chunks):
        for stage, buffer, count in (
            (2, send_2, slots - 2),
            (3, send_3, lat - 1),
            (4, send_4, lon - 1),
            (6, send_6, slots - 2),
            (7, send_7, lat - 1),
            (8, send_8, lon - 1),
            (9, send_3, near - 1),
            (10, send_7, near - 1),
        ):
            if count:
                sent(stage, chunk, buffer.at[chunk % 2, pl.ds(0, count)])
        for k in range(2):
            pack_copy(k, chunk).wait_send()
    for k in range(group):
        o_store(last * group + k, k).wait()
        if chunks > 1:
            i_store((last - 1) * group + k, k).wait()


def result_kernel(
    group,
    narrow,
    norm_at,
    out_from,
    gin_from,
    total_hbm,
    small_hbm,
    last_mixed,
    last_grid,
    x_hbm,
    skip,
    gain,
    bias,
    out_to,
    gin_to,
    grad_spec,
    grad_skip,
    grad_in,
    grad_out,
    in_bias,
    vectors,
    gin_held,
    out_held,
    x_held,
    mixed_held,
    grid_held,
    total,
    small,
    sems,
    last_sems,
):
    batch, rows, width = out_from.shape
    hidden = grad_in.shape[1]
    halves = width // LANES
    degrees = grad_spec.shape[2]
    first = batch - group

    def reads(sample):
        out = pltpu.make_async_copy(out_from.at[sample], out_held.at[sample], sems.at[1, sample])
        if sample >= first:
            return (out,)
        return (pltpu.make_async_copy(gin_from.at[sample], gin_held.at[sample], sems.at[0, sample]), out)

    def gin_write(sample):
        return pltpu.make_async_copy(gin_held.at[sample], gin_to.at[sample], sems.at[2, sample])

    def writes(sample):
        out = pltpu.make_async_copy(out_held.at[sample], out_to.at[sample], sems.at[3, sample])
        return (out,) if sample >= first else (gin_write(sample), out)

    last = [
        pltpu.make_async_copy(source, held, last_sems.at[at])
        for at, (source, held) in enumerate(
            (
                (x_hbm.at[pl.ds(first, group)], x_held),
                (last_mixed, mixed_held),
                (last_grid, grid_held),
                (total_hbm, total),
                (small_hbm, small),
            )
        )
    ]
    for copy in last[:3]:
        copy.start()
    for sample in range(batch):
        for copy in reads(sample):
            copy.start()
    for copy in last[3:]:
        copy.start()
    for copy in last[:3]:
        copy.wait()

    def pass_on(samples):
        for sample in samples:
            for read, write in zip(reads(sample), writes(sample)):
                read.wait()
                write.start()

    pass_on(range(batch // 2))
    back_tile = row_tile(rows, 144)
    for k in range(group):

        @pl.loop(0, rows // back_tile)
        def _(i, k=k):
            where = pl.ds(pl.multiple_of(i * back_tile, 8), back_tile)
            gin_held[first + k, where, :] = norm_step(
                x_held[k, where, :],
                jnp.concatenate([mixed_held[k, h, where, :] for h in range(halves)], axis=1),
                jnp.concatenate([grid_held[k, h, where, :] for h in range(halves)], axis=1),
                skip[...],
                gain[...],
            )

        gin_write(first + k).start()

    pass_on(range(batch // 2, batch))
    for copy in last[3:]:
        copy.wait()

    def tile(base, height, q):
        return total[pl.ds(base + q * height, height), :].astype(jnp.float32)

    hidden_rows = width * hidden // LANES
    vector_rows = 2 * hidden_rows + width * width // LANES

    for q in range(hidden // LANES):
        where = pl.ds(q * LANES, LANES)
        grad_in[:, where] = tile(0, width, q)
        grad_out[where, :] = tile(hidden_rows, width, q).T
        in_bias[:, where] = jnp.sum(tile(vector_rows, 8, q), axis=0, keepdims=True)
    for q in range(halves):
        where = pl.ds(q * LANES, LANES)
        grad_skip[:, where] = tile(2 * hidden_rows, width, q)
        for which in range(3):
            at = vector_rows + 8 * (hidden + which * width) // LANES
            vectors[which, :, where] = jnp.sum(tile(at, 8, q), axis=0, keepdims=True)
        all_normed, everything = (small[pl.ds(norm_at + which * halves + q, 1), :] for which in range(2))
        vectors[3, :, where] = (all_normed - bias[:, where] * everything) / gain[:, where]
        vectors[4, :, where] = everything
    place = lax.rem(lax.axis_index("lon"), group)
    for which in range(2):
        turned = small[pl.ds(which * degrees, degrees), :].T
        for q in range(group):

            @pl.when(place == q)
            def _(q=q, which=which, turned=turned):
                grad_spec[which] = turned[q * narrow : (q + 1) * narrow, :]

    for sample in range(batch):
        for write in writes(sample):
            write.wait()
    for k in range(group):
        gin_write(first + k).wait()


def per_device(
    lat,
    lon,
    inputs,
    legendre_forward,
    legendre_inverse,
    spectral_weight,
    skip_weight,
    gain_first,
    bias_first,
    gain_second,
    bias_second,
    mlp_in,
    mlp_in_bias,
    mlp_out,
    mlp_out_bias,
    cotangent,
):
    batch, band, columns, width = inputs.shape
    points = columns * lon
    slab, degrees, lats = legendre_forward.shape
    orders = slab * lat
    hidden = mlp_in.shape[1]
    rows = columns * band
    padded = -(-rows // 16) * 16
    halves = width // LANES
    group = lon // halves
    chunks = batch // group

    forward, inverse = fourier_tables(points, orders, lat)
    high, each = split_orders(orders, lat)
    near = lat // 2
    low_rows = degrees - high
    block = 2 * each * band
    waves = 2 * orders
    pack_rows = sum(low_rows - near * i // 8 * 8 for i in range(each))
    my_lon = lax.axis_index("lon")
    hidden = mlp_in.shape[1]
    flat_rows = (2 * hidden + width) * width // LANES + 8 * (hidden + 3 * width) // LANES
    share = -(-flat_rows // (16 * lat * lon)) * 16
    total_rows = share * lat * lon
    spec_rows = -(-2 * degrees // (8 * lat)) * 8

    def flat(values):
        return values.transpose(0, 2, 1, 3).reshape(batch, rows, width)

    def row(values):
        return values.reshape(1, -1)

    vmem = pl.BlockSpec(memory_space=pltpu.VMEM)
    hbm = pl.BlockSpec(memory_space=pl.ANY)
    fixed = pl.BlockSpec(memory_space=pltpu.HBM)
    low, full = jnp.bfloat16, jnp.float32
    results = pl.pallas_call(
        functools.partial(block_kernel, lat, lon),
        out_shape=(
            jax.ShapeDtypeStruct((batch, rows, width), low),
            jax.ShapeDtypeStruct((max(batch - group, 1), rows, width), full),
            jax.ShapeDtypeStruct((total_rows, LANES), low),
            jax.ShapeDtypeStruct((lat * spec_rows + 8, LANES), full),
            jax.ShapeDtypeStruct((group, halves, padded, LANES), low),
            jax.ShapeDtypeStruct((group, halves, padded, LANES), low),
        ),
        in_specs=[hbm, hbm] + [vmem] * 16,
        out_specs=(hbm,) * 6,
        scratch_shapes=[
            pltpu.VMEM((batch, rows, width), low),
            pltpu.VMEM((batch, halves, padded, LANES), low),
            pltpu.VMEM((chunks, lon, padded, LANES), low),
            pltpu.VMEM((chunks, lon, padded, LANES), low),
            pltpu.VMEM((batch, halves, padded, LANES), low),
            pltpu.VMEM((chunks, lat + near, block, LANES), low),
            pltpu.VMEM((chunks, lat + near, block, LANES), low),
            pltpu.VMEM((chunks, each, degrees, 2 * LANES), low),
            pltpu.VMEM((chunks, pack_rows, 2 * LANES), low),
            pltpu.VMEM((2, chunks, pack_rows, 2 * LANES), low),
            pltpu.VMEM((2, chunks, pack_rows, 2 * LANES), low),
            pltpu.VMEM((pack_rows, 2 * LANES), full),
            pltpu.VMEM((pack_rows, 2 * LANES), full),
            pltpu.VMEM((2, lat + near, block, LANES), low),
            pltpu.VMEM((2, lat + near, block, LANES), low),
            pltpu.VMEM((2, lon, padded, LANES), low),
            pltpu.VMEM((2, lat + near, block, LANES), low),
            pltpu.VMEM((2, lat + near, block, LANES), low),
            pltpu.VMEM((2, lon, padded, LANES), low),
            pltpu.VMEM((max(points, waves) * band, LANES), full),
            pltpu.VMEM((waves * band, LANES), full),
            pltpu.VMEM((group, rows, width), low),
            pltpu.VMEM((group, rows, width), low),
            pltpu.VMEM((group, rows, width), full),
            pltpu.SemaphoreType.DMA((10, chunks, group)),
            pltpu.SemaphoreType.DMA((12, 2)),
            pltpu.SemaphoreType.DMA((2, chunks)),
            pltpu.SemaphoreType.DMA((batch,)),
            pltpu.SemaphoreType.DMA((group,)),
            pltpu.SemaphoreType.DMA((group,)),
            pltpu.SemaphoreType.DMA((group,)),
            pltpu.VMEM((2, 2 * each, lats, degrees), low),
            pltpu.VMEM((each, degrees, lats), low),
            pltpu.VMEM((each, lats, degrees), low),
            pltpu.VMEM((each, lats, degrees), low),
            pltpu.VMEM((each, degrees, lats), low),
            pltpu.VMEM((each, low_rows, near * band), low),
            pltpu.VMEM((each, near * band, low_rows), low),
            pltpu.VMEM((each, near * band, low_rows), low),
            pltpu.VMEM((each, low_rows, near * band), low),
            pltpu.SemaphoreType.DMA((2,)),
            pltpu.SemaphoreType.DMA((2, slab, 2)),
            pltpu.VMEM((2, LANES, degrees), full),
            pltpu.VMEM((degrees, LANES), full),
            pltpu.VMEM((degrees, LANES), full),
            pltpu.VMEM((total_rows, LANES), full),
            pltpu.VMEM((1, total_rows // 2, LANES), full),
            pltpu.VMEM((1, total_rows // 4, LANES), full),
            pltpu.VMEM((max(lon // 2 - 1, 1), total_rows // (2 * lon), LANES), low),
            pltpu.VMEM((max(lat // 2 - 1, 1), share, LANES), low),
            pltpu.VMEM((total_rows // 4, LANES), low),
            pltpu.VMEM((total_rows // (2 * lon), LANES), low),
            pltpu.VMEM((share, LANES), low),
            pltpu.VMEM((lat * spec_rows, LANES), full),
            pltpu.VMEM((lat - 1, spec_rows, LANES), full),
            pltpu.VMEM((group, spec_rows, LANES), full),
            pltpu.VMEM((spec_rows, LANES), full),
            pltpu.VMEM((spec_rows, LANES), full),
            pltpu.VMEM((2, 8, LANES), full),
            pltpu.VMEM((8, width), full),
            pltpu.VMEM((3, 8, LANES), full),
            pltpu.VMEM((lon - 1, 8, LANES), full),
            pltpu.VMEM((lat - 1, 8, LANES), full),
            pltpu.SemaphoreType.DMA((2, group)),
            pltpu.SemaphoreType.DMA((2, 4)),
            pltpu.SemaphoreType.DMA((2, 4)),
            pltpu.SemaphoreType.DMA((2,)),
            pltpu.SemaphoreType.DMA((2,)),
            pltpu.SemaphoreType.DMA((2, group)),
            pltpu.SemaphoreType.DMA((2,)),
            pltpu.SemaphoreType.DMA((2, max(lat, lon) - 1)),
            pltpu.SemaphoreType.DMA((5,)),
        ],
        compiler_params=pltpu.CompilerParams(
            collective_id=0, has_side_effects=True, vmem_limit_bytes=63 * 2**20
        ),
    )(
        flat(inputs),
        flat(cotangent),
        jnp.asarray(forward),
        jnp.asarray(inverse),
        jnp.asarray(inverse.T),
        jnp.asarray(forward.T),
        legendre_forward.transpose(0, 2, 1),
        legendre_inverse,
        spectral_weight.transpose(0, 2, 1),
        skip_weight,
        mlp_in,
        mlp_out,
        row(gain_first),
        row(bias_first),
        row(gain_second),
        row(bias_second),
        row(mlp_in_bias),
        row(mlp_out_bias),
    )
    shapes = (
        ((batch, rows, width), low),
        ((batch, rows, width), full),
        ((2, width // lon, degrees), full),
        ((width, width), full),
        ((width, hidden), full),
        ((hidden, width), full),
        ((1, hidden), full),
        ((5, 1, width), full),
    )
    output, grad_inputs, grad_spec, grad_skip, grad_in, grad_out, in_bias, vectors = pl.pallas_call(
        functools.partial(result_kernel, group, width // lon, lat * spec_rows),
        out_shape=tuple(jax.ShapeDtypeStruct(*shape) for shape in shapes),
        in_specs=[fixed] * 7 + [vmem] * 3,
        out_specs=(fixed, fixed) + (vmem,) * 6,
        scratch_shapes=[
            pltpu.VMEM((batch, rows, width), full),
            pltpu.VMEM((batch, rows, width), low),
            pltpu.VMEM((group, rows, width), low),
            pltpu.VMEM((group, halves, padded, LANES), low),
            pltpu.VMEM((group, halves, padded, LANES), low),
            pltpu.VMEM((total_rows, LANES), low),
            pltpu.VMEM((lat * spec_rows + 8, LANES), full),
            pltpu.SemaphoreType.DMA((4, batch)),
            pltpu.SemaphoreType.DMA((5,)),
        ],
        compiler_params=pltpu.CompilerParams(vmem_limit_bytes=63 * 2**20),
    )(*results, flat(inputs), skip_weight, row(gain_first), row(bias_first))

    def unflat(values):
        return values.reshape(batch, columns, band, width).transpose(0, 2, 1, 3)

    return (
        unflat(output),
        unflat(grad_inputs),
        grad_spec.transpose(0, 2, 1),
        grad_skip,
        vectors[3, 0],
        vectors[4, 0],
        vectors[1, 0],
        vectors[2, 0],
        grad_in,
        in_bias[0],
        grad_out,
        vectors[0, 0],
    )


def solution(mesh):
    lat, lon = mesh.shape["lat"], mesh.shape["lon"]
    grid = P(None, "lat", "lon", None)
    table = P("lat", None, None)
    channel = P(None, None, "lon")
    return jax.shard_map(
        functools.partial(per_device, lat, lon),
        mesh=mesh,
        in_specs=(grid, table, table, channel) + (P(),) * 9 + (grid,),
        out_specs=(grid, grid, channel) + (P(),) * 9,
        check_vma=False,
    )
```

```python
import functools
import math

import jax
import jax.numpy as jnp
import ml_dtypes
import numpy as np
from jax import lax
from jax.experimental import pallas as pl
from jax.experimental.pallas import tpu as pltpu
from jax.sharding import PartitionSpec as P

epsilon = 1e-05
LANES = 128
MESH = pl.DeviceIdType.MESH
root = math.sqrt(2.0 / math.pi)
cubic = 0.044715

OFFSET = {"1": 0, "2": 1, "3a": 3, "3b": 4, "4": 5, "5a": 7, "5b": 7, "6": 9, "7a": 12, "7b": 13, "8": 14, "9": 15}
ORDER = ("8", "1", "7b", "7a", "5a", "4", "5b", "3b", "3a", "6", "2", "9")


def split_orders(orders, lat):
    high = 2 * orders // 3
    each = high // lat
    assert each * lat == high and 3 * high == 2 * orders
    return high, each


def fourier_tables(points, orders, lat):
    waves = np.arange(orders)
    phase = (waves[:, None] * np.arange(points)[None, :] % points).astype(np.float32)
    phase = phase * np.float32(2.0 * math.pi / points)
    cosine, sine = np.cos(phase), np.sin(phase)
    factor = np.where(waves == 0, 1.0, 2.0).astype(np.float32)[:, None]
    high, each = split_orders(orders, lat)
    near = lat // 2
    owned = [[t * each + i for i in range(each)] for t in range(lat)]
    owned += [[high + near * i + d for i in range(each)] for d in range(near)]

    def arrange(*parts):
        stacked = [part[waves] for waves in owned for part in parts]
        return np.concatenate(stacked).astype(ml_dtypes.bfloat16)

    return arrange(cosine, -sine), arrange(factor * cosine, -factor * sine)


def row_tile(rows, most):
    fits = [t for t in range(16, most + 1, 16) if rows % t == 0]
    return fits[-1] if fits else rows


def norm_parts(values):
    center = values - jnp.mean(values, axis=-1, keepdims=True)
    spread = jnp.mean(center * center, axis=-1, keepdims=True)
    scaled = lax.rsqrt(spread + epsilon)
    return center * scaled, scaled


def norm_back(grad_out, normal, scaled, gain):
    grad_norm = grad_out * gain
    inner = jnp.mean(grad_norm, axis=-1, keepdims=True)
    cross = jnp.mean(grad_norm * normal, axis=-1, keepdims=True)
    return scaled * (grad_norm - inner - normal * cross)


def norm_step(values, mixed, sent, skip, gain):
    normal, scaled = norm_parts(values.astype(jnp.float32))
    grad_normed = dot_t(mixed, skip) + sent.astype(jnp.float32)
    return mixed.astype(jnp.float32) + norm_back(grad_normed, normal, scaled, gain)


def fold(values):
    rows, width = values.shape
    return jnp.sum(values.reshape(rows // 8, 8, width), axis=0)


def dot(a, b):
    return jnp.dot(a, b, preferred_element_type=jnp.float32)


def dot_t(a, b):
    return lax.dot_general(a, b, (((1,), (1,)), ((), ())), preferred_element_type=jnp.float32)


def t_dot(a, b):
    return lax.dot_general(a, b, (((0,), (0,)), ((), ())), preferred_element_type=jnp.float32)


def block_kernel(
    lat,
    lon,
    x_hbm,
    g_hbm,
    fwd_t,
    inv_t,
    inv,
    fwd,
    raw_ana,
    raw_syn,
    weight,
    skip,
    mlp_in,
    mlp_out,
    gain_one,
    bias_one,
    gain_two,
    bias_two,
    bias_in,
    bias_out,
    out_hbm,
    gin_hbm,
    total_hbm,
    small_hbm,
    last_mixed,
    last_grid,
    x_all,
    normed,
    lon_a,
    lon_c,
    lon_b,
    lat_a,
    lat_b,
    coeffs,
    coeffs_high,
    pack_own,
    pack_far,
    stack,
    stack_held,
    send_2,
    send_3,
    send_4,
    send_6,
    send_7,
    send_8,
    wide,
    slim,
    g_buf,
    o_buf,
    i_buf,
    recv_sem,
    send_sem,
    rows_sem,
    x_sem,
    g_sem,
    o_sem,
    i_sem,
    tabs,
    ana,
    ana_t,
    syn,
    syn_t,
    ana_high,
    ana_high_t,
    syn_high,
    syn_high_t,
    tab_recv,
    tab_send,
    w_parts,
    w_real,
    w_imag,
    acc,
    part_core,
    part_near,
    part_chip,
    part_far,
    wire_chip,
    wire_far,
    share,
    spec,
    spec_lat,
    spec_lon,
    spec_sum,
    spec_own,
    norm_sums,
    mixed_sums,
    norm_own,
    norm_lon,
    norm_lat,
    w_sem,
    fold_recv,
    fold_send,
    spec_recv,
    spec_send,
    spec_pair,
    norm_recv,
    norm_send,
    own_sem,
):
    batch, rows, width = x_hbm.shape
    halves = width // LANES
    group = lon // halves
    chunks = batch // group
    points = fwd_t.shape[1]
    slab, lats, degrees = raw_ana.shape
    narrow = width // lon
    hidden = mlp_in.shape[1]
    band = lats // lat
    waves = 2 * slab * lat
    high, each = split_orders(slab * lat, lat)
    near = lat // 2
    block = 2 * each * band
    slots = lat + near
    low_rows = degrees - high
    starts = [near * i // 8 * 8 for i in range(each)]
    packs = [sum(low_rows - start for start in starts[:i]) for i in range(each)]
    my_lat, my_lon = lax.axis_index("lat"), lax.axis_index("lon")
    mixed = normed
    my_side, my_near = my_lat // near, lax.rem(my_lat, near)
    half_tile = row_tile(rows, 144)
    full_tile = row_tile(rows, 240)

    def slot_of(chunk):
        return lax.rem(chunk, 2)

    def lon_copy(stage, chunk, src, dst, peer, member=0):
        return pltpu.make_async_remote_copy(
            src_ref=src,
            dst_ref=dst,
            send_sem=rows_sem.at[stage // 4, chunk] if stage in (1, 5) else send_sem.at[stage - 1, slot_of(chunk)],
            recv_sem=recv_sem.at[stage - 1, chunk, member],
            device_id={"lon": peer},
            device_id_type=MESH,
        )

    def lat_copy(send_at, recv_at, chunk, src, dst, peer):
        return pltpu.make_async_remote_copy(
            src_ref=src,
            dst_ref=dst,
            send_sem=send_sem.at[send_at, slot_of(chunk)],
            recv_sem=recv_sem.at[recv_at, chunk, 0],
            device_id={"lat": peer},
            device_id_type=MESH,
        )

    def own_copy(stage, chunk, src, dst):
        return pltpu.make_async_copy(src, dst, recv_sem.at[stage - 1, chunk, 0])

    def landed(stage, chunk, whole, member=0):
        pltpu.make_async_copy(whole, whole, recv_sem.at[stage - 1, chunk, member]).wait()

    def member_at(step):
        return lax.rem(my_lon // halves + step, group)

    def member_landed(stage, chunk, step):
        count = halves if step else halves - 1
        landed(stage, chunk, lon_a.at[chunk, pl.ds(0, count)], member_at(step))

    def sent(stage, chunk, part):
        lon_copy(stage, chunk, part, part, my_lon).wait_send()

    def x_load(sample):
        return pltpu.make_async_copy(x_hbm.at[sample], x_all.at[sample], x_sem.at[sample])

    def g_load(sample, slot):
        return pltpu.make_async_copy(g_hbm.at[sample], g_buf.at[slot], g_sem.at[slot])

    def o_store(sample, slot):
        return pltpu.make_async_copy(o_buf.at[slot], out_hbm.at[sample], o_sem.at[slot])

    def i_store(sample, slot):
        return pltpu.make_async_copy(i_buf.at[slot], gin_hbm.at[sample], i_sem.at[slot])

    def spread_rows(stage, chunk, held, sample, landing):
        src = chunk * group + sample
        for half in range(halves):
            peer = sample * halves + half

            @pl.when(peer != my_lon)
            def _(peer=peer, half=half):
                lon_copy(stage, chunk, held.at[src, half], landing.at[chunk, my_lon], peer).start()

            @pl.when(peer == my_lon)
            def _(half=half):
                own_copy(stage, chunk, held.at[src, half], landing.at[chunk, my_lon]).start()

    def spread_low(send_at, recv_at, chunk, buffer, target):
        for step in range(1, lat):
            peer = lax.rem(my_lat + step, lat)
            lat_copy(send_at, recv_at, chunk, buffer.at[peer], target.at[chunk, my_lat], peer).start()

    def spread_high(send_at, recv_at, chunk, buffer, target):
        for step in range(1, near):
            peer = lax.rem(my_near + step, near)
            src, dst = buffer.at[lat + peer], target.at[chunk, lat + my_near]
            lat_copy(send_at, recv_at, chunk, src, dst, my_side * near + peer).start()

    def own_rows(at):
        return pl.ds(pl.multiple_of(at * block, 16), block)

    def to_waves(stage, chunk, table, scale, buffer, landing):
        slot = slot_of(chunk)
        landed(stage - 1, chunk, landing.at[chunk])
        for source in range(lon):
            wide[pl.ds(source * rows, rows), :] = landing[chunk, source, pl.ds(0, rows), :].astype(jnp.float32)
        for first in range(0, band, 2):
            rhs = jnp.concatenate(
                [wide[pl.ds(first + k, points, stride=band), :] for k in range(2)], axis=1
            ).astype(jnp.bfloat16)
            got = dot(table[...], rhs)
            if scale is not None:
                got = got * scale
            for k in range(2):
                slim[pl.ds(first + k, waves, stride=band), :] = got[:, k * LANES : (k + 1) * LANES]

        @pl.when(chunk > 1)
        def _():
            sent(stage, chunk, buffer.at[slot, pl.ds(0, slots - 2)])

        for target in range(slots):
            buffer[slot, target] = slim[pl.ds(target * block, block), :].astype(jnp.bfloat16)
        spread_low(stage - 1, stage - 1, chunk, buffer.at[slot], lat_a)
        spread_high(stage - 1, stage - 1, chunk, buffer.at[slot], lat_a)
        lat_a[chunk, my_lat] = slim[own_rows(my_lat), :].astype(jnp.bfloat16)
        lat_a[chunk, lat + my_near] = slim[own_rows(lat + my_near), :].astype(jnp.bfloat16)

    def to_points(stage, chunk, table, scale, buffer):
        slot = slot_of(chunk)
        landed(stage - 1, chunk, lat_b.at[chunk, pl.ds(0, slots - 2)])
        for source in range(slots):
            slim[pl.ds(source * block, block), :] = lat_b[chunk, source].astype(jnp.float32)
        for first in range(0, band, 2):
            rhs = jnp.concatenate(
                [slim[pl.ds(first + k, waves, stride=band), :] for k in range(2)], axis=1
            ).astype(jnp.bfloat16)
            got = dot(table[...], rhs)
            if scale is not None:
                got = got * scale
            for k in range(2):
                wide[pl.ds(first + k, points, stride=band), :] = got[:, k * LANES : (k + 1) * LANES]

        @pl.when(chunk > 1)
        def _():
            sent(stage, chunk, buffer.at[slot, pl.ds(0, lon - 1)])

        for target in range(lon):
            grid = wide[pl.ds(target * rows, rows), :]
            buffer[slot, target, pl.ds(0, rows), :] = grid.astype(jnp.bfloat16)
            if stage == 8:
                before = lon_a[chunk, target, pl.ds(0, rows), :].astype(jnp.float32)
                norm_sums[0] += fold(grid * before)
                norm_sums[1] += fold(grid)
        member, half = my_lon // halves, lax.rem(my_lon, halves)

        def send(landing):
            for step in range(1, lon):
                peer = lax.rem(my_lon + step, lon)
                lon_copy(stage, chunk, buffer.at[slot, peer], landing, peer, member).start()

        def send_here():
            send(lon_b.at[chunk * group + member, half])
            own = pl.ds(pl.multiple_of(my_lon * rows, 8), rows)
            lon_b[chunk * group + member, half, pl.ds(0, rows), :] = wide[own, :].astype(jnp.bfloat16)

        if stage == 4:
            send_here()
        else:
            pl.when(chunk < chunks - 1)(send_here)

            @pl.when(chunk == chunks - 1)
            def _():
                norm_start()
                send(last_grid.at[member, half])
                last_own().start()

    def last_own():
        held = last_grid.at[my_lon // halves, lax.rem(my_lon, halves)]
        return pltpu.make_async_copy(send_8.at[(chunks - 1) % 2, my_lon], held, own_sem.at[3])

    def last_mixed_copy():
        part = mixed.at[pl.ds((chunks - 1) * group, group)]
        return pltpu.make_async_copy(part, last_mixed, own_sem.at[4])

    def wave_rows(first, count, i):
        parts = []
        for r in range(2):
            at = (r * each + i) * band
            held = [slim[pl.ds(s * block + at, band), :] for s in range(first, first + count)]
            parts.append(jnp.concatenate(held, axis=0))
        return jnp.concatenate(parts, axis=1).astype(jnp.bfloat16)

    def put_rows(got, count, i):
        for r in range(2):
            at = (r * each + i) * band
            for t in range(count):
                wide[pl.ds(t * block + at, band), :] = got[
                    t * band : (t + 1) * band, r * LANES : (r + 1) * LANES
                ]

    def pack_copy(k, chunk):
        peer = lax.rem(my_lat + near, lat)
        return lat_copy(10 + k, 8 + k, chunk, pack_own.at[k, chunk], pack_far.at[k, chunk], peer)

    def slab_first(stage, k, chunk, tables, between, buffer):
        first_table, second_table, high_table = tables
        slot = slot_of(chunk)
        landed(stage - 1, chunk, lat_a.at[chunk, pl.ds(0, slots - 2)])
        for source in range(slots):
            slim[pl.ds(source * block, block), :] = lat_a[chunk, source].astype(jnp.float32)
        for i in range(each):
            got = dot(high_table[i], wave_rows(lat, near, i))
            stack[pl.ds(packs[i], low_rows - starts[i]), :] = got[starts[i] :, :]

        @pl.when(chunk > 1)
        def _():
            pack_copy(k, chunk).wait_send()

        pack_own[k, chunk] = stack[...].astype(jnp.bfloat16)
        pack_copy(k, chunk).start()
        for m in range(each):
            real, imag = between(m, dot(first_table[m], wave_rows(0, lat, m)))
            low = jnp.concatenate([real, imag], axis=1).astype(jnp.bfloat16)
            put_rows(dot(second_table[m], low), lat, m)

        @pl.when(chunk > 1)
        def _():
            sent(stage, chunk, buffer.at[slot, pl.ds(0, lat - 1)])

        for target in range(lat):
            buffer[slot, target] = wide[pl.ds(target * block, block), :].astype(jnp.bfloat16)
        spread_low(stage - 1, stage - 1, chunk, buffer.at[slot], lat_b)
        lat_b[chunk, my_lat] = wide[own_rows(my_lat), :].astype(jnp.bfloat16)

    def slab_second(stage, k, chunk, table, before, between, buffer):
        slot = slot_of(chunk)
        landed(9 + k, chunk, pack_far.at[k, chunk])
        stack[...] = pack_own[k, chunk].astype(jnp.float32) + pack_far[k, chunk].astype(jnp.float32)
        before()
        for i in range(each):
            count = low_rows - starts[i]
            real, imag = between(pl.ds(packs[i], count), high + starts[i], count)
            low = jnp.concatenate([real, imag], axis=1)
            if starts[i]:
                low = jnp.concatenate([jnp.zeros((starts[i], 2 * LANES), jnp.float32), low], axis=0)
            put_rows(dot(table[i], low.astype(jnp.bfloat16)), near, i)

        if near > 1:

            @pl.when(chunk > 1)
            def _():
                sent(9 + k, chunk, buffer.at[slot, pl.ds(lat, near - 1)])

        for target in range(near):
            buffer[slot, lat + target] = wide[pl.ds(target * block, block), :].astype(jnp.bfloat16)
        spread_high(8 + k, stage - 1, chunk, buffer.at[slot], lat_b)
        lat_b[chunk, lat + my_near] = wide[own_rows(my_near), :].astype(jnp.bfloat16)

    hidden_rows = width * hidden // LANES
    vector_rows = 2 * hidden_rows + width * width // LANES

    def gather_rows(base, values):
        count = values.shape[0]
        for q in range(values.shape[1] // LANES):
            acc[pl.ds(base + q * count, count), :] += values[:, q * LANES : (q + 1) * LANES]

    def both(held, sample, where):
        return jnp.concatenate([held[sample, h, where, :] for h in range(halves)], axis=1)

    def normalize(sample):
        x_load(sample).wait()

        @pl.loop(0, rows // half_tile)
        def _(i):
            where = pl.ds(pl.multiple_of(i * half_tile, 8), half_tile)
            normal, _ = norm_parts(x_all[sample, where, :].astype(jnp.float32))
            low = (normal * gain_one[...] + bias_one[...]).astype(jnp.bfloat16)
            for h in range(halves):
                normed[sample, h, where, :] = low[:, h * LANES : (h + 1) * LANES]

    def stage_1(chunk):
        for step in reversed(range(group)):
            k = member_at(step)

            @pl.when(jnp.logical_or(chunk > 0, step == 0))
            def _(k=k):
                normalize(chunk * group + k)

            spread_rows(1, chunk, normed, k, lon_a)

    def stage_2(chunk):
        to_waves(2, chunk, fwd_t, 1.0 / points, send_2, lon_a)

    def filtered(real, imag, rows):
        wr, wi = w_real[rows, :], w_imag[rows, :]
        return wr * real - wi * imag, wr * imag + wi * real

    def stage_3a(chunk):
        def between(m, got):
            coeffs[chunk, m] = got.astype(jnp.bfloat16)
            return filtered(got[:, :LANES], got[:, LANES:], pl.ds(0, degrees))

        slab_first(3, 0, chunk, (ana, syn, ana_high), between, send_3)

    def stage_3b(chunk):
        def before():
            coeffs_high[chunk] = stack[...].astype(jnp.bfloat16)

        def between(where, degree, count):
            got = stack[where, :]
            return filtered(got[:, :LANES], got[:, LANES:], pl.ds(degree, count))

        slab_second(3, 0, chunk, syn_high, before, between, send_3)

    def stage_4(chunk):
        to_points(4, chunk, inv, None, send_4)

    def stage_5a(chunk):
        sent(1, chunk, lon_a.at[chunk, pl.ds(0, lon - 1)])
        feed_forward(chunk, range(group // 2))

    def stage_5b(chunk):
        feed_forward(chunk, range(group // 2, group))

    def feed_forward(chunk, steps):
        for step in steps:
            member_landed(4, chunk, step)
            k = member_at(step)
            sample = chunk * group + k
            g_load(sample, k).wait()

            @pl.when(chunk > 0)
            def _(sample=sample, k=k):
                o_store(sample, k).wait()

            @pl.loop(0, rows // full_tile)
            def _(i):
                where = pl.ds(pl.multiple_of(i * full_tile, 8), full_tile)
                low_one = both(normed, sample, where)
                spatial = both(lon_b, sample, where).astype(jnp.float32)
                resid = x_all[sample, where, :].astype(jnp.float32) + (spatial + dot(low_one, skip[...]))
                normal, scaled = norm_parts(resid)
                low_two = (normal * gain_two[...] + bias_two[...]).astype(jnp.bfloat16)
                pre = dot(low_two, mlp_in[...]) + bias_in[...]
                square = pre * pre
                curve = jnp.tanh(root * pre * (1.0 + cubic * square))
                lifted = 0.5 + 0.5 * curve
                act = (pre * lifted).astype(jnp.bfloat16)
                slope = lifted + (0.5 * root) * pre * (1.0 - curve * curve) * (1.0 + (3.0 * cubic) * square)
                o_buf[k, where, :] = (resid + dot(act, mlp_out[...]) + bias_out[...]).astype(jnp.bfloat16)
                g_low = g_buf[k, where, :]
                gather_rows(hidden_rows, t_dot(g_low, act))
                grad_pre = (dot_t(g_low, mlp_out[...]) * slope).astype(jnp.bfloat16)
                gather_rows(0, t_dot(low_two, grad_pre))
                gather_rows(vector_rows, fold(grad_pre.astype(jnp.float32)))
                grad_second = dot_t(grad_pre, mlp_in[...])
                g_full = g_low.astype(jnp.float32)
                for at, values in enumerate((g_full, grad_second * normal, grad_second)):
                    gather_rows(vector_rows + 8 * (hidden + at * width) // LANES, fold(values))
                grad_mixed = (g_full + norm_back(grad_second, normal, scaled, gain_two[...])).astype(jnp.bfloat16)
                gather_rows(2 * hidden_rows, t_dot(low_one, grad_mixed))
                mixed_sums[...] += fold(grad_mixed.astype(jnp.float32))
                for h in range(halves):
                    mixed[sample, h, where, :] = grad_mixed[:, h * LANES : (h + 1) * LANES]

            o_store(sample, k).start()

            @pl.when(chunk < chunks - 1)
            def _(sample=sample, k=k):
                g_load(sample + group, k).start()

            spread_rows(5, chunk, mixed, k, lon_c)

    def stage_6(chunk):
        to_waves(6, chunk, inv_t, None, send_6, lon_c)

    def unfiltered(got, held, degree, count, share_of):
        dr, di = got[:, :LANES], got[:, LANES:]
        ar, ai = held[:, :LANES], held[:, LANES:]
        spec[pl.ds(degree, count), :] += share_of * (dr * ar + di * ai)
        spec[pl.ds(degrees + degree, count), :] += share_of * (di * ar - dr * ai)
        wr, wi = w_real[pl.ds(degree, count), :], w_imag[pl.ds(degree, count), :]
        return wr * dr + wi * di, wr * di - wi * dr

    def stage_7a(chunk):
        def between(m, got):
            return unfiltered(got, coeffs[chunk, m].astype(jnp.float32), 0, degrees, 1.0)

        slab_first(7, 1, chunk, (syn_t, ana_t, syn_high_t), between, send_7)

    def stage_7b(chunk):
        def before():
            stack_held[...] = coeffs_high[chunk].astype(jnp.float32)

        def between(where, degree, count):
            return unfiltered(stack[where, :], stack_held[where, :], degree, count, 0.5)

        slab_second(7, 1, chunk, ana_high_t, before, between, send_7)

    def stage_8(chunk):
        to_points(8, chunk, fwd, 1.0 / points, send_8)

    def stage_9(chunk):
        for step in range(group):
            member_landed(8, chunk, step)
            k = member_at(step)
            sample = chunk * group + k

            @pl.when(chunk > 0)
            def _(sample=sample, k=k):
                i_store(sample, k).wait()

            @pl.loop(0, rows // half_tile)
            def _(i):
                where = pl.ds(pl.multiple_of(i * half_tile, 8), half_tile)
                i_buf[k, where, :] = norm_step(
                    x_all[sample, where, :],
                    both(mixed, sample, where),
                    both(lon_b, sample, where),
                    skip[...],
                    gain_one[...],
                )

            i_store(sample, k).start()

    def weight_copies(start):
        place = lax.rem(my_lon, group)
        held = w_parts.at[:, pl.ds(pl.multiple_of(place * narrow, 8), narrow), :]
        for q in range(group):
            peer = my_lon // group + halves * q

            @pl.when(peer != my_lon)
            def _(peer=peer, q=q):
                copy = pltpu.make_async_remote_copy(
                    src_ref=weight,
                    dst_ref=held,
                    send_sem=w_sem.at[1, q],
                    recv_sem=w_sem.at[0, place],
                    device_id={"lon": peer},
                    device_id_type=MESH,
                )
                if start:
                    copy.start()
                else:
                    copy.wait_send()

            if start:

                @pl.when(peer == my_lon)
                def _():
                    pltpu.make_async_copy(weight, held, w_sem.at[0, place]).start()

    def table_copies(start):
        def one(i, carry):
            wave = my_lat * slab + i

            def give(peer, slot, way):
                for which, raw in enumerate((raw_ana, raw_syn)):

                    @pl.when(peer != my_lat)
                    def _(which=which, raw=raw):
                        copy = pltpu.make_async_remote_copy(
                            src_ref=raw.at[i],
                            dst_ref=tabs.at[which, slot],
                            send_sem=tab_send.at[which, i, way],
                            recv_sem=tab_recv.at[which],
                            device_id={"lat": peer},
                            device_id_type=MESH,
                        )
                        if start:
                            copy.start()
                        else:
                            copy.wait_send()

                    if start:

                        @pl.when(peer == my_lat)
                        def _(which=which, raw=raw):
                            pltpu.make_async_copy(raw.at[i], tabs.at[which, slot], tab_recv.at[which]).start()

            @pl.when(wave < high)
            def _():
                give(lax.div(wave, each), lax.rem(wave, each), 0)

            @pl.when(wave >= high)
            def _():
                above = wave - high
                for side in range(2):
                    give(side * near + lax.rem(above, near), each + lax.div(above, near), side)

            return carry

        lax.fori_loop(0, slab, one, 0)

    def build():
        acc[...] = jnp.zeros_like(acc)
        spec[...] = jnp.zeros_like(spec)
        norm_sums[...] = jnp.zeros_like(norm_sums)
        mixed_sums[...] = jnp.zeros_like(mixed_sums)
        norm_own[...] = jnp.zeros_like(norm_own)
        degree = lax.broadcasted_iota(jnp.int32, (lats, degrees), 1)
        for which in range(2):
            pltpu.make_async_copy(tabs.at[which], tabs.at[which], tab_recv.at[which]).wait()
        kinds = ((ana_t, ana, ana_high_t, ana_high), (syn, syn_t, syn_high, syn_high_t))

        @pl.loop(0, each)
        def _(i):
            half = pl.ds(pl.multiple_of(my_side * near * band, 16), near * band)
            for which, (plain, turned, part, part_turned) in enumerate(kinds):
                values = tabs[which, i].astype(jnp.float32)
                values = jnp.where(degree >= my_lat * each + i, values, 0.0)
                plain[i] = values.astype(jnp.bfloat16)
                turned[i] = values.T.astype(jnp.bfloat16)
                values = tabs[which, each + i, half, :].astype(jnp.float32)
                values = jnp.where(degree[: near * band] >= high + near * i + my_near, values, 0.0)
                values = values.T[high:, :]
                part_turned[i] = values.astype(jnp.bfloat16)
                part[i] = values.T.astype(jnp.bfloat16)

        for q in range(group):
            part = w_parts.at[:, pl.ds(q * narrow, narrow), :]
            pltpu.make_async_copy(part, part, w_sem.at[0, q]).wait()
        w_real[...] = w_parts[0].T
        w_imag[...] = w_parts[1].T

    total_rows = acc.shape[0]
    place_core, place_chip = lax.rem(my_lon, 2), my_lon // 2
    place_near, place_far = lax.rem(my_lat, 2), my_lat // 2
    levels = (
        (2, place_core, part_core, None, lambda p: {"lon": 2 * place_chip + p}),
        (2, place_near, part_near, None, lambda p: {"lat": 2 * place_far + p}),
        (lon // 2, place_chip, part_chip, wire_chip, lambda p: {"lon": 2 * p + place_core}),
        (lat // 2, place_far, part_far, wire_far, lambda p: {"lat": 2 * p + place_near}),
    )
    bases, sizes = [0], [total_rows]
    for count, place, _, _, _ in levels:
        sizes.append(sizes[-1] // count)
        bases.append(bases[-1] + place * sizes[-1])

    def row_part(at, count):
        return pl.ds(pl.multiple_of(at, 16), count)

    def fold_start(k):
        count, place, parts, wire, device = levels[k]
        if wire is not None:
            wire[...] = acc[row_part(bases[k], sizes[k]), :].astype(jnp.bfloat16)
        for step in range(1, count):
            peer = lax.rem(place + step, count)
            if wire is None:
                src = acc.at[row_part(bases[k] + peer * sizes[k + 1], sizes[k + 1]), :]
            else:
                src = wire.at[row_part(peer * sizes[k + 1], sizes[k + 1]), :]
            pltpu.make_async_remote_copy(
                src_ref=src,
                dst_ref=parts.at[step - 1],
                send_sem=fold_send.at[0, k],
                recv_sem=fold_recv.at[0, k],
                device_id=device(peer),
                device_id_type=MESH,
            ).start()

    def fold_end(k):
        count, _, parts, _, _ = levels[k]
        if count == 1:
            return
        pltpu.make_async_copy(parts, parts, fold_recv.at[0, k]).wait()
        got = parts[0].astype(jnp.float32)
        for step in range(2, count):
            got = got + parts[step - 1].astype(jnp.float32)
        acc[row_part(bases[k + 1], sizes[k + 1]), :] += got

    def spread_start(k):
        count, place, _, _, device = levels[k]
        own = row_part(bases[k + 1], sizes[k + 1])
        src = total_hbm.at[own, :]
        if k == len(levels) - 1:
            share[...] = acc[own, :].astype(jnp.bfloat16)
            src = share
            pltpu.make_async_copy(share, total_hbm.at[own, :], own_sem.at[0]).start()
        for step in range(1, count):
            pltpu.make_async_remote_copy(
                src_ref=src,
                dst_ref=total_hbm.at[own, :],
                send_sem=fold_send.at[1, k],
                recv_sem=fold_recv.at[1, k],
                device_id=device(lax.rem(place + step, count)),
                device_id_type=MESH,
            ).start()

    def spread_end(k):
        count = levels[k][0]
        if count > 1:
            all_parts = total_hbm.at[pl.ds(0, (count - 1) * sizes[k + 1]), :]
            pltpu.make_async_copy(all_parts, all_parts, fold_recv.at[1, k]).wait()
        if k == len(levels) - 1:
            own = row_part(bases[k + 1], sizes[k + 1])
            pltpu.make_async_copy(share, total_hbm.at[own, :], own_sem.at[0]).wait()

    def fold_sent():
        for k, (count, _, _, wire, _) in enumerate(levels):
            for way, held in ((0, acc if wire is None else wire), (1, total_hbm)):
                if count == 1:
                    continue
                part = held.at[pl.ds(0, (count - 1) * sizes[k + 1]), :]
                pltpu.make_async_remote_copy(
                    src_ref=part,
                    dst_ref=part,
                    send_sem=fold_send.at[way, k],
                    recv_sem=fold_recv.at[way, k],
                    device_id={"lon": my_lon},
                    device_id_type=MESH,
                ).wait_send()

    spec_rows = spec_sum.shape[0]

    def spec_part(at):
        return pl.ds(pl.multiple_of(at * spec_rows, 8), spec_rows)

    def spec_lat_copies(way, src, dst):
        for step in range(1, lat):
            peer = lax.rem(my_lat + step, lat)
            pltpu.make_async_remote_copy(
                src_ref=src(peer),
                dst_ref=dst(step),
                send_sem=spec_send.at[way],
                recv_sem=spec_recv.at[way],
                device_id={"lat": peer},
                device_id_type=MESH,
            ).start()

    def spec_start():
        spec_lat_copies(
            0, lambda p: spec.at[spec_part(p), :], lambda s: spec_lat.at[s - 1]
        )

    def spec_pairs(action):
        half = lax.rem(my_lon, halves)
        for q in range(group):
            target = half * group + q

            @pl.when(target != my_lon)
            def _(target=target, q=q):
                copy = pltpu.make_async_remote_copy(
                    src_ref=spec_sum,
                    dst_ref=spec_lon.at[my_lon // halves],
                    send_sem=spec_pair.at[1, q],
                    recv_sem=spec_pair.at[0, my_lon // halves],
                    device_id={"lon": target},
                    device_id_type=MESH,
                )
                if action == "start":
                    copy.start()
                else:
                    copy.wait_send()

            if action == "start":

                @pl.when(target == my_lon)
                def _():
                    pltpu.make_async_copy(
                        spec_sum, spec_lon.at[my_lon // halves], spec_pair.at[0, my_lon // halves]
                    ).start()

    def spec_middle():
        pltpu.make_async_copy(spec_lat, spec_lat, spec_recv.at[0]).wait()
        got = spec[spec_part(my_lat), :]
        for step in range(1, lat):
            got = got + spec_lat[step - 1]
        spec_sum[...] = got
        spec_pairs("start")

    def spec_back():
        for q in range(group):
            pltpu.make_async_copy(spec_lon.at[q], spec_lon.at[q], spec_pair.at[0, q]).wait()
        got = spec_lon[0]
        for q in range(1, group):
            got = got + spec_lon[q]
        spec_own[...] = got
        own = spec_part(my_lat)
        spec_lat_copies(1, lambda p: spec_own, lambda s: small_hbm.at[own, :])
        pltpu.make_async_copy(spec_own, small_hbm.at[own, :], own_sem.at[1]).start()

    def spec_end():
        pltpu.make_async_copy(spec_own, small_hbm.at[spec_part(my_lat), :], own_sem.at[1]).wait()
        part = spec.at[pl.ds(0, (lat - 1) * spec_rows), :]
        pltpu.make_async_copy(part, part, spec_recv.at[1]).wait()
        for way in range(2):
            pltpu.make_async_remote_copy(
                src_ref=part,
                dst_ref=part,
                send_sem=spec_send.at[way],
                recv_sem=spec_recv.at[way],
                device_id={"lat": my_lat},
                device_id_type=MESH,
            ).wait_send()
        spec_pairs("end")

    def norm_copies(way, axis, count, place, src, parts, action):
        for step in range(1, count):
            copy = pltpu.make_async_remote_copy(
                src_ref=src,
                dst_ref=parts.at[step - 1],
                send_sem=norm_send.at[way, step - 1],
                recv_sem=norm_recv.at[way],
                device_id={axis: lax.rem(place + step, count)},
                device_id_type=MESH,
            )
            if action == "start":
                copy.start()
            else:
                copy.wait_send()

    def norm_end(way, parts, count):
        pltpu.make_async_copy(parts, parts, norm_recv.at[way]).wait()
        got = norm_own[way]
        for step in range(1, count):
            got = got + parts[step - 1]
        norm_own[way + 1] = got

    def norm_skip():
        lines = [jnp.zeros((1, width), jnp.float32) for _ in range(2)]
        all_mixed = jnp.sum(mixed_sums[...], axis=0, keepdims=True)
        for q in range(halves):
            lanes = slice(q * LANES, (q + 1) * LANES)
            part = skip[:, lanes].astype(jnp.float32)
            held = acc[pl.ds(2 * hidden_rows + q * width, width), :]
            for which, values in enumerate((held, all_mixed[:, lanes])):
                lines[which] += jnp.sum((part * values).T, axis=0, keepdims=True)
        for which in range(2):
            for half in range(halves):
                norm_own[0, pl.ds(which * halves + half, 1), :] = lines[which][
                    :, half * LANES : (half + 1) * LANES
                ]

    def norm_start():
        for half in range(halves):

            @pl.when(lax.rem(my_lon, halves) == half)
            def _(half=half):
                for which in range(2):
                    line = jnp.sum(norm_sums[which], axis=0, keepdims=True)
                    norm_own[0, pl.ds(which * halves + half, 1), :] += line

        norm_copies(0, "lon", lon, my_lon, norm_own.at[0], norm_lon, "start")

    def norm_middle():
        norm_end(0, norm_lon, lon)
        norm_copies(1, "lat", lat, my_lat, norm_own.at[1], norm_lat, "start")

    def norm_finish():
        norm_end(1, norm_lat, lat)
        where = pl.ds(lat * spec_rows, 8)
        copy = pltpu.make_async_copy(norm_own.at[2], small_hbm.at[where, :], own_sem.at[2])
        copy.start()
        norm_copies(0, "lon", lon, my_lon, norm_own.at[0], norm_lon, "end")
        norm_copies(1, "lat", lat, my_lat, norm_own.at[1], norm_lat, "end")
        copy.wait()

    def last_mixed_start():
        last_mixed_copy().start()

    def run(*steps):
        def go():
            for step, k in steps:
                step() if k is None else step(k)

        return go

    end = chunks - 1
    aside = {
        (0, "1"): build,
        (end + 7, "5b"): run((last_mixed_start, None), (norm_skip, None), (fold_start, 0)),
        (end + 8, "7a"): run((fold_end, 0), (fold_start, 1)),
        (end + 9, "7b"): run((fold_end, 1), (fold_start, 2)),
        (end + 10, "8"): run((fold_end, 2), (fold_start, 3)),
        (end + 11, "8"): run((fold_end, 3), (spread_start, 3)),
        (end + 11, "9"): run((spread_end, 3), (spread_start, 2)),
        (end + 12, "9"): run((spread_end, 2), (spread_start, 1)),
        (end + 14, "8"): run((spread_end, 1), (spread_start, 0), (norm_middle, None), (spec_back, None)),
        (end + 13, "7b"): run((spec_start, None)),
        (end + 13, "9"): run((spec_middle, None)),
    }

    stages = {
        "1": stage_1,
        "2": stage_2,
        "3a": stage_3a,
        "3b": stage_3b,
        "4": stage_4,
        "5a": stage_5a,
        "5b": stage_5b,
        "6": stage_6,
        "7a": stage_7a,
        "7b": stage_7b,
        "8": stage_8,
        "9": stage_9,
    }

    for sample in range(group):
        x_load(sample).start()

    padded = lon_a.shape[2]
    if padded > rows:
        normed[:, :, rows:, :] = jnp.zeros_like(normed[:, :, rows:, :])
        for held in (send_4, send_8):
            held[:, :, rows:, :] = jnp.zeros_like(held[:, :, rows:, :])
    barrier = pltpu.get_barrier_semaphore()
    for step in range(1, lon):
        pl.semaphore_signal(
            barrier, inc=1, device_id={"lon": lax.rem(my_lon + step, lon)}, device_id_type=MESH
        )
    for step in range(1, lat):
        pl.semaphore_signal(
            barrier, inc=1, device_id={"lat": lax.rem(my_lat + step, lat)}, device_id_type=MESH
        )
    for step in range(1, group):
        normalize(member_at(step))
    for sample in range(group, batch):
        x_load(sample).start()
    for k in range(group):
        g_load(k, k).start()
    pl.semaphore_wait(barrier, lon - 1 + lat - 1)

    weight_copies(True)
    table_copies(True)

    def tick(now, carry):
        for stage in ORDER:
            chunk = now - OFFSET[stage]

            @pl.when(jnp.logical_and(chunk >= 0, chunk < (end if stage == "9" else chunks)))
            def _(stage=stage, chunk=chunk):
                stages[stage](chunk)

            for (when, after), action in aside.items():
                if after == stage:
                    pl.when(now == when)(action)

        return carry

    lax.fori_loop(0, chunks + max(OFFSET.values()), tick, 0)

    spread_end(0)
    norm_finish()
    spec_end()
    fold_sent()
    for step in range(group):
        member_landed(8, end, step)
    last_own().wait()
    last_mixed_copy().wait()
    weight_copies(False)
    table_copies(False)
    last = chunks - 1
    for chunk in range(chunks):
        sent(5, chunk, lon_a.at[chunk, pl.ds(0, lon - 1)])
    for chunk in range(max(chunks - 2, 0), chunks):
        for stage, buffer, count in (
            (2, send_2, slots - 2),
            (3, send_3, lat - 1),
            (4, send_4, lon - 1),
            (6, send_6, slots - 2),
            (7, send_7, lat - 1),
            (8, send_8, lon - 1),
            (9, send_3, near - 1),
            (10, send_7, near - 1),
        ):
            if count:
                sent(stage, chunk, buffer.at[chunk % 2, pl.ds(0, count)])
        for k in range(2):
            pack_copy(k, chunk).wait_send()
    for k in range(group):
        o_store(last * group + k, k).wait()
        if chunks > 1:
            i_store((last - 1) * group + k, k).wait()


def result_kernel(
    group,
    narrow,
    norm_at,
    out_from,
    gin_from,
    total_hbm,
    small_hbm,
    last_mixed,
    last_grid,
    x_hbm,
    skip,
    gain,
    bias,
    out_to,
    gin_to,
    grad_spec,
    grad_skip,
    grad_in,
    grad_out,
    in_bias,
    vectors,
    gin_held,
    out_held,
    x_held,
    mixed_held,
    grid_held,
    total,
    small,
    sems,
    last_sems,
):
    batch, rows, width = out_from.shape
    hidden = grad_in.shape[1]
    halves = width // LANES
    degrees = grad_spec.shape[2]
    first = batch - group

    def reads(sample):
        out = pltpu.make_async_copy(out_from.at[sample], out_held.at[sample], sems.at[1, sample])
        if sample >= first:
            return (out,)
        return (pltpu.make_async_copy(gin_from.at[sample], gin_held.at[sample], sems.at[0, sample]), out)

    def gin_write(sample):
        return pltpu.make_async_copy(gin_held.at[sample], gin_to.at[sample], sems.at[2, sample])

    def writes(sample):
        out = pltpu.make_async_copy(out_held.at[sample], out_to.at[sample], sems.at[3, sample])
        return (out,) if sample >= first else (gin_write(sample), out)

    last = [
        pltpu.make_async_copy(source, held, last_sems.at[at])
        for at, (source, held) in enumerate(
            (
                (x_hbm.at[pl.ds(first, group)], x_held),
                (last_mixed, mixed_held),
                (last_grid, grid_held),
                (total_hbm, total),
                (small_hbm, small),
            )
        )
    ]
    for copy in last[:3]:
        copy.start()
    for sample in range(batch):
        for copy in reads(sample):
            copy.start()
    for copy in last[3:]:
        copy.start()
    for copy in last[:3]:
        copy.wait()

    def pass_on(samples):
        for sample in samples:
            for read, write in zip(reads(sample), writes(sample)):
                read.wait()
                write.start()

    pass_on(range(batch // 2))
    back_tile = row_tile(rows, 144)
    for k in range(group):

        @pl.loop(0, rows // back_tile)
        def _(i, k=k):
            where = pl.ds(pl.multiple_of(i * back_tile, 8), back_tile)
            gin_held[first + k, where, :] = norm_step(
                x_held[k, where, :],
                jnp.concatenate([mixed_held[k, h, where, :] for h in range(halves)], axis=1),
                jnp.concatenate([grid_held[k, h, where, :] for h in range(halves)], axis=1),
                skip[...],
                gain[...],
            )

        gin_write(first + k).start()

    pass_on(range(batch // 2, batch))
    for copy in last[3:]:
        copy.wait()

    def tile(base, height, q):
        return total[pl.ds(base + q * height, height), :].astype(jnp.float32)

    hidden_rows = width * hidden // LANES
    vector_rows = 2 * hidden_rows + width * width // LANES

    for q in range(hidden // LANES):
        where = pl.ds(q * LANES, LANES)
        grad_in[:, where] = tile(0, width, q)
        grad_out[where, :] = tile(hidden_rows, width, q).T
        in_bias[:, where] = jnp.sum(tile(vector_rows, 8, q), axis=0, keepdims=True)
    for q in range(halves):
        where = pl.ds(q * LANES, LANES)
        grad_skip[:, where] = tile(2 * hidden_rows, width, q)
        for which in range(3):
            at = vector_rows + 8 * (hidden + which * width) // LANES
            vectors[which, :, where] = jnp.sum(tile(at, 8, q), axis=0, keepdims=True)
        all_normed, everything = (small[pl.ds(norm_at + which * halves + q, 1), :] for which in range(2))
        vectors[3, :, where] = (all_normed - bias[:, where] * everything) / gain[:, where]
        vectors[4, :, where] = everything
    place = lax.rem(lax.axis_index("lon"), group)
    for which in range(2):
        turned = small[pl.ds(which * degrees, degrees), :].T
        for q in range(group):

            @pl.when(place == q)
            def _(q=q, which=which, turned=turned):
                grad_spec[which] = turned[q * narrow : (q + 1) * narrow, :]

    for sample in range(batch):
        for write in writes(sample):
            write.wait()
    for k in range(group):
        gin_write(first + k).wait()


def per_device(
    lat,
    lon,
    inputs,
    legendre_forward,
    legendre_inverse,
    spectral_weight,
    skip_weight,
    gain_first,
    bias_first,
    gain_second,
    bias_second,
    mlp_in,
    mlp_in_bias,
    mlp_out,
    mlp_out_bias,
    cotangent,
):
    batch, band, columns, width = inputs.shape
    points = columns * lon
    slab, degrees, lats = legendre_forward.shape
    orders = slab * lat
    hidden = mlp_in.shape[1]
    rows = columns * band
    padded = -(-rows // 16) * 16
    halves = width // LANES
    group = lon // halves
    chunks = batch // group

    forward, inverse = fourier_tables(points, orders, lat)
    high, each = split_orders(orders, lat)
    near = lat // 2
    low_rows = degrees - high
    block = 2 * each * band
    waves = 2 * orders
    pack_rows = sum(low_rows - near * i // 8 * 8 for i in range(each))
    my_lon = lax.axis_index("lon")
    hidden = mlp_in.shape[1]
    flat_rows = (2 * hidden + width) * width // LANES + 8 * (hidden + 3 * width) // LANES
    share = -(-flat_rows // (16 * lat * lon)) * 16
    total_rows = share * lat * lon
    spec_rows = -(-2 * degrees // (8 * lat)) * 8

    def flat(values):
        return values.transpose(0, 2, 1, 3).reshape(batch, rows, width)

    def row(values):
        return values.reshape(1, -1)

    vmem = pl.BlockSpec(memory_space=pltpu.VMEM)
    hbm = pl.BlockSpec(memory_space=pl.ANY)
    fixed = pl.BlockSpec(memory_space=pltpu.HBM)
    low, full = jnp.bfloat16, jnp.float32
    results = pl.pallas_call(
        functools.partial(block_kernel, lat, lon),
        out_shape=(
            jax.ShapeDtypeStruct((batch, rows, width), low),
            jax.ShapeDtypeStruct((max(batch - group, 1), rows, width), full),
            jax.ShapeDtypeStruct((total_rows, LANES), low),
            jax.ShapeDtypeStruct((lat * spec_rows + 8, LANES), full),
            jax.ShapeDtypeStruct((group, halves, padded, LANES), low),
            jax.ShapeDtypeStruct((group, halves, padded, LANES), low),
        ),
        in_specs=[hbm, hbm] + [vmem] * 16,
        out_specs=(hbm,) * 6,
        scratch_shapes=[
            pltpu.VMEM((batch, rows, width), low),
            pltpu.VMEM((batch, halves, padded, LANES), low),
            pltpu.VMEM((chunks, lon, padded, LANES), low),
            pltpu.VMEM((chunks, lon, padded, LANES), low),
            pltpu.VMEM((batch, halves, padded, LANES), low),
            pltpu.VMEM((chunks, lat + near, block, LANES), low),
            pltpu.VMEM((chunks, lat + near, block, LANES), low),
            pltpu.VMEM((chunks, each, degrees, 2 * LANES), low),
            pltpu.VMEM((chunks, pack_rows, 2 * LANES), low),
            pltpu.VMEM((2, chunks, pack_rows, 2 * LANES), low),
            pltpu.VMEM((2, chunks, pack_rows, 2 * LANES), low),
            pltpu.VMEM((pack_rows, 2 * LANES), full),
            pltpu.VMEM((pack_rows, 2 * LANES), full),
            pltpu.VMEM((2, lat + near, block, LANES), low),
            pltpu.VMEM((2, lat + near, block, LANES), low),
            pltpu.VMEM((2, lon, padded, LANES), low),
            pltpu.VMEM((2, lat + near, block, LANES), low),
            pltpu.VMEM((2, lat + near, block, LANES), low),
            pltpu.VMEM((2, lon, padded, LANES), low),
            pltpu.VMEM((max(points, waves) * band + 8, LANES), full),
            pltpu.VMEM((waves * band + 8, LANES), full),
            pltpu.VMEM((group, rows, width), low),
            pltpu.VMEM((group, rows, width), low),
            pltpu.VMEM((group, rows, width), full),
            pltpu.SemaphoreType.DMA((10, chunks, group)),
            pltpu.SemaphoreType.DMA((12, 2)),
            pltpu.SemaphoreType.DMA((2, chunks)),
            pltpu.SemaphoreType.DMA((batch,)),
            pltpu.SemaphoreType.DMA((group,)),
            pltpu.SemaphoreType.DMA((group,)),
            pltpu.SemaphoreType.DMA((group,)),
            pltpu.VMEM((2, 2 * each, lats, degrees), low),
            pltpu.VMEM((each, degrees, lats), low),
            pltpu.VMEM((each, lats, degrees), low),
            pltpu.VMEM((each, lats, degrees), low),
            pltpu.VMEM((each, degrees, lats), low),
            pltpu.VMEM((each, low_rows, near * band), low),
            pltpu.VMEM((each, near * band, low_rows), low),
            pltpu.VMEM((each, near * band, low_rows), low),
            pltpu.VMEM((each, low_rows, near * band), low),
            pltpu.SemaphoreType.DMA((2,)),
            pltpu.SemaphoreType.DMA((2, slab, 2)),
            pltpu.VMEM((2, LANES, degrees), full),
            pltpu.VMEM((degrees, LANES), full),
            pltpu.VMEM((degrees, LANES), full),
            pltpu.VMEM((total_rows, LANES), full),
            pltpu.VMEM((1, total_rows // 2, LANES), full),
            pltpu.VMEM((1, total_rows // 4, LANES), full),
            pltpu.VMEM((max(lon // 2 - 1, 1), total_rows // (2 * lon), LANES), low),
            pltpu.VMEM((max(lat // 2 - 1, 1), share, LANES), low),
            pltpu.VMEM((total_rows // 4, LANES), low),
            pltpu.VMEM((total_rows // (2 * lon), LANES), low),
            pltpu.VMEM((share, LANES), low),
            pltpu.VMEM((lat * spec_rows, LANES), full),
            pltpu.VMEM((lat - 1, spec_rows, LANES), full),
            pltpu.VMEM((group, spec_rows, LANES), full),
            pltpu.VMEM((spec_rows, LANES), full),
            pltpu.VMEM((spec_rows, LANES), full),
            pltpu.VMEM((2, 8, LANES), full),
            pltpu.VMEM((8, width), full),
            pltpu.VMEM((3, 8, LANES), full),
            pltpu.VMEM((lon - 1, 8, LANES), full),
            pltpu.VMEM((lat - 1, 8, LANES), full),
            pltpu.SemaphoreType.DMA((2, group)),
            pltpu.SemaphoreType.DMA((2, 4)),
            pltpu.SemaphoreType.DMA((2, 4)),
            pltpu.SemaphoreType.DMA((2,)),
            pltpu.SemaphoreType.DMA((2,)),
            pltpu.SemaphoreType.DMA((2, group)),
            pltpu.SemaphoreType.DMA((2,)),
            pltpu.SemaphoreType.DMA((2, max(lat, lon) - 1)),
            pltpu.SemaphoreType.DMA((5,)),
        ],
        compiler_params=pltpu.CompilerParams(
            collective_id=0, has_side_effects=True, vmem_limit_bytes=63 * 2**20
        ),
    )(
        flat(inputs),
        flat(cotangent),
        jnp.asarray(forward),
        jnp.asarray(inverse),
        jnp.asarray(inverse.T),
        jnp.asarray(forward.T),
        legendre_forward.transpose(0, 2, 1),
        legendre_inverse,
        spectral_weight.transpose(0, 2, 1),
        skip_weight,
        mlp_in,
        mlp_out,
        row(gain_first),
        row(bias_first),
        row(gain_second),
        row(bias_second),
        row(mlp_in_bias),
        row(mlp_out_bias),
    )
    shapes = (
        ((batch, rows, width), low),
        ((batch, rows, width), full),
        ((2, width // lon, degrees), full),
        ((width, width), full),
        ((width, hidden), full),
        ((hidden, width), full),
        ((1, hidden), full),
        ((5, 1, width), full),
    )
    output, grad_inputs, grad_spec, grad_skip, grad_in, grad_out, in_bias, vectors = pl.pallas_call(
        functools.partial(result_kernel, group, width // lon, lat * spec_rows),
        out_shape=tuple(jax.ShapeDtypeStruct(*shape) for shape in shapes),
        in_specs=[fixed] * 7 + [vmem] * 3,
        out_specs=(fixed, fixed) + (vmem,) * 6,
        scratch_shapes=[
            pltpu.VMEM((batch, rows, width), full),
            pltpu.VMEM((batch, rows, width), low),
            pltpu.VMEM((group, rows, width), low),
            pltpu.VMEM((group, halves, padded, LANES), low),
            pltpu.VMEM((group, halves, padded, LANES), low),
            pltpu.VMEM((total_rows, LANES), low),
            pltpu.VMEM((lat * spec_rows + 8, LANES), full),
            pltpu.SemaphoreType.DMA((4, batch)),
            pltpu.SemaphoreType.DMA((5,)),
        ],
        compiler_params=pltpu.CompilerParams(vmem_limit_bytes=63 * 2**20),
    )(*results, flat(inputs), skip_weight, row(gain_first), row(bias_first))

    def unflat(values):
        return values.reshape(batch, columns, band, width).transpose(0, 2, 1, 3)

    return (
        unflat(output),
        unflat(grad_inputs),
        grad_spec.transpose(0, 2, 1),
        grad_skip,
        vectors[3, 0],
        vectors[4, 0],
        vectors[1, 0],
        vectors[2, 0],
        grad_in,
        in_bias[0],
        grad_out,
        vectors[0, 0],
    )


def solution(mesh):
    lat, lon = mesh.shape["lat"], mesh.shape["lon"]
    grid = P(None, "lat", "lon", None)
    table = P("lat", None, None)
    channel = P(None, None, "lon")
    return jax.shard_map(
        functools.partial(per_device, lat, lon),
        mesh=mesh,
        in_specs=(grid, table, table, channel) + (P(),) * 9 + (grid,),
        out_specs=(grid, grid, channel) + (P(),) * 9,
        check_vma=False,
    )
```
